32 devices in a mesh: groups: 1, layer: 32 (over z, y, x, core).
Axes of the slice: x: 2, y: 2, z: 4, core: 2. Of those that a mesh axis runs over, the one named last changes fastest.
Arguments:
- resid: bfloat16 [32, 8, 8192], P('layer', 'groups'), may hold values from -6 to 6
- enc_weight: bfloat16 [32, 8192, 256], P('layer'), may hold values from -0.0625 to 0.0625
- enc_bias: bfloat16 [32, 256], P('layer'), may hold values from -0.5 to 0.5
- active: int32 [32, 2, 2], P('layer', 'groups'), may hold values from 0 to 1, as said below
- dec_weight: bfloat16 [32, 2, 256, 8192], P('layer'), may hold values from -0.125 to 0.125
- target: bfloat16 [32, 8, 8192], P('layer', 'groups'), may hold values from -5 to 5
Outputs:
- error: bfloat16 [32, 8, 8192], P('layer', 'groups')
- grad_codes: float32 [32, 64, 256], P('layer', 'groups')
The draws below stay inside these ranges and needn't reach their ends.
Inputs may be any that keep to these rules, and one draw needn't show every extreme that they name: `active`: in every slab exactly 3 of the 2 x 2 (token tile, feature block) pairs are 1.
All inputs are finite; a program needn't handle non-finite values.
Results may differ from the reference program's by a relative error of at most 0.0041.
Values may be sent and summed in bfloat16 or wider, within the bound.
No kernel may reach another device: no remote copies, remote signals or barrier semaphores. Data moves between devices by JAX's collectives and lax.ppermute only.
A program may use at most 128 MiB of HBM per device.

```python
import jax
import jax.numpy as jnp
from jax import lax

D = 8192
BLOCK = 128
FEAT_DEV = 256
BLK_DEV = 2
LAYERS = 4
GROUP = 8
FEAT = 2048
TOK_DEV = 8
TOKENS_L = 64
TILE = 32
TILES_L = 2
LIVE = 3
REACH = 2
SLABS = 32


def draw_active(key, part):
    key = jax.random.fold_in(key, 7)
    pairs = TILES_L * BLK_DEV
    scores = jax.random.randint(key, (SLABS, pairs), 0, 1 << 20) * pairs + jnp.arange(pairs, dtype=jnp.int32)[None, :]
    ranks = jnp.argsort(jnp.argsort(scores, axis=1), axis=1)
    return (ranks < LIVE).astype(jnp.int32).reshape(SLABS, TILES_L, BLK_DEV)


def steps_of(own_key, extent, shards, smallest, high):
    factor_of = 1.0
    for position, parts in shards:
        steps = jax.random.uniform(jax.random.fold_in(jax.random.fold_in(own_key, 6), position), (parts,), jnp.float32, smallest / len(shards), high / len(shards))
        factor_of = factor_of * jnp.repeat(jnp.exp(steps), extent[position] // parts).reshape((-1,) + (1,) * (len(extent) - 1 - position))
    return factor_of


def centred(rng, shape, scale, most, cuts=(), held_as=jnp.bfloat16):
    entries = jax.random.normal(rng, shape, jnp.float32) * scale
    if len(cuts) > 0:
        entries = steps_of(rng, shape, cuts, -0.22, 0.18) * entries
    return jnp.clip(entries, min=-most, max=most).astype(held_as)


def setup_inputs(seed: int = 0, part: int = 0) -> dict:
    keys = jax.random.split(jax.random.key(seed), 7)
    part_keys = jax.random.split(jax.random.fold_in(keys[6], part), 7)
    return {
        "resid": centred(part_keys[0], (SLABS, TOK_DEV, D), 1.0, 6.0, ((0, 32),)),
        "enc_weight": centred(keys[1], (SLABS, D, FEAT_DEV), D ** -0.5, 0.0625, ((0, 32),)),
        "enc_bias": jnp.clip(jax.random.uniform(keys[2], (SLABS, FEAT_DEV), jnp.float32, -0.5, 0.5) * steps_of(keys[2], (SLABS, FEAT_DEV), ((0, 32),), -0.4, 0.0), -0.5, 0.5).astype(jnp.bfloat16),
        "active": draw_active(jax.random.fold_in(jax.random.fold_in(keys[6], part), 71), part),
        "dec_weight": centred(keys[4], (SLABS, REACH, FEAT_DEV, D), FEAT ** -0.5, 0.125, ((0, 32),)),
        "target": centred(part_keys[5], (SLABS, TOK_DEV, D), 0.7, 5.0, ((0, 32),)),
    }


def reference(resid, enc_weight, enc_bias, active, dec_weight, target):
    enc = enc_weight.reshape(LAYERS, GROUP, D, FEAT_DEV)
    bias = enc_bias.reshape(LAYERS, GROUP * FEAT_DEV)
    dec = dec_weight.reshape(LAYERS, GROUP, REACH, FEAT_DEV, D)
    inputs = resid.reshape(LAYERS, TOKENS_L, D)
    wanted = target.reshape(LAYERS, TOKENS_L, D)
    masks = active.reshape(LAYERS, GROUP, TILES_L, BLK_DEV)

    def decoder(layer, reach):
        return dec[layer, :, reach].reshape(GROUP * FEAT_DEV, D)

    def encode(layer):
        weight = jnp.transpose(enc[layer], (1, 0, 2)).reshape(D, GROUP * FEAT_DEV)
        pre = jnp.dot(inputs[layer], weight, preferred_element_type=jnp.float32) + bias[layer].astype(jnp.float32)[None, :]
        gate = jnp.repeat(jnp.repeat(masks[layer], TILE, axis=1), BLOCK, axis=2)
        gate = jnp.transpose(gate, (1, 0, 2)).reshape(TOKENS_L, GROUP * FEAT_DEV).astype(jnp.float32)
        return (jax.nn.relu(pre) * gate).astype(jnp.bfloat16)

    layer_ids = jnp.arange(LAYERS, dtype=jnp.int32)
    codes = lax.map(encode, layer_ids)

    def rebuild(layer):
        before = jnp.maximum(layer - 1, 0)
        own = jnp.dot(codes[layer], decoder(layer, 0), preferred_element_type=jnp.float32)
        prior = jnp.dot(codes[before], decoder(before, 1), preferred_element_type=jnp.float32)
        recon = own + jnp.where(layer >= 1, prior, 0.0)
        return (recon - wanted[layer].astype(jnp.float32)).astype(jnp.bfloat16)

    errors = lax.map(rebuild, layer_ids)

    def backward(layer):
        after = jnp.minimum(layer + 1, LAYERS - 1)
        dims = (((1,), (1,)), ((), ()))
        own = lax.dot_general(errors[layer], decoder(layer, 0), dims, preferred_element_type=jnp.float32)
        later = lax.dot_general(errors[after], decoder(layer, 1), dims, preferred_element_type=jnp.float32)
        grad = own + jnp.where(layer + 1 < LAYERS, later, 0.0)
        return jnp.transpose(grad.reshape(TOKENS_L, GROUP, FEAT_DEV), (1, 0, 2))

    grads = lax.map(backward, layer_ids)
    error = errors.reshape(SLABS, TOK_DEV, D)
    grad_codes = grads.reshape(SLABS, TOKENS_L, FEAT_DEV)
    return error, grad_codes
```

```python
import jax
import jax.numpy as jnp
from jax import lax
from jax.sharding import PartitionSpec as P

BLOCK = 128
LAYERS = 4
TILE = 32
CORES = 2
AXIS = "layer"


def swap(value, mask):
    pairs = [(source, source ^ mask) for source in range(lax.axis_size(AXIS))]
    return lax.ppermute(value, AXIS, pairs)


def shifted(block, distance):
    devices = range(lax.axis_size(AXIS))
    route = [(i - distance, i) for i in devices if i - distance in devices]
    return lax.ppermute(block, AXIS, route)


def transposed(left, weight):
    return lax.dot_general(
        left, weight, (((1,), (1,)), ((), ())), preferred_element_type=jnp.float32
    )


def gathered(slab, chips):
    near = [slab] + [swap(slab, CORES * chip) for chip in range(1, chips)]
    far = [swap(piece, 1) for piece in near]
    return jnp.concatenate(near + far, axis=0)


def scattered(part, chips):
    half = part.shape[0] // CORES
    rows = half // chips
    got = swap(part[half:].astype(jnp.bfloat16), 1)
    total = part[:half] + got.astype(jnp.float32)
    sends = [total[chip * rows : (chip + 1) * rows].astype(jnp.bfloat16) for chip in range(1, chips)]
    came = [swap(sends[chip - 1], CORES * chip) for chip in range(1, chips)]
    out = total[:rows]
    for block in came:
        out = out + block.astype(jnp.float32)
    return out


def on_device(resid, enc_weight, enc_bias, active, dec_weight, target):
    group = lax.axis_size(AXIS) // LAYERS
    chips = group // CORES
    bits = chips.bit_length() - 1
    place = lax.axis_index(AXIS) % group
    tokens = resid.shape[1]
    x = gathered(resid[0], chips)
    pre = (
        jnp.dot(x, enc_weight[0], preferred_element_type=jnp.float32)
        + enc_bias[0].astype(jnp.float32)[None, :]
    )
    order = jnp.array(
        [CORES * chip + core for core in range(CORES) for chip in range(chips)], dtype=jnp.int32
    )
    slab = jnp.bitwise_xor(order, place)
    tile = (slab * tokens) // TILE
    pick = (tile[:, None] == jnp.arange(active.shape[1], dtype=jnp.int32)[None, :]).astype(jnp.int32)
    live = jnp.sum(pick[:, :, None] * active[0][None, :, :], axis=1)
    gate = jnp.repeat(jnp.repeat(live, tokens, axis=0), BLOCK, axis=1).astype(jnp.float32)
    codes = (jax.nn.relu(pre) * gate).astype(jnp.bfloat16)
    own_dec = dec_weight[0, 0]
    next_dec = dec_weight[0, 1]
    wanted = target[0].astype(jnp.float32)
    next_part = jnp.dot(codes, next_dec, preferred_element_type=jnp.float32)
    own_part = jnp.dot(codes, own_dec, preferred_element_type=jnp.float32)
    next_sum = scattered(next_part, chips).astype(jnp.bfloat16)
    from_before = shifted(next_sum, group).astype(jnp.float32)
    own_sum = scattered(own_part, chips)
    error = (own_sum + from_before - wanted).astype(jnp.bfloat16)
    later = shifted(error, -group)
    here_rows = gathered(error, chips)
    after_rows = gathered(later, chips)
    grad = transposed(here_rows, own_dec) + transposed(after_rows, next_dec)
    features = grad.shape[1]
    grad = grad.reshape((2,) * (bits + 1) + (tokens, features))
    for axis in range(bits + 1):
        bit = 0 if axis == 0 else bits + 1 - axis
        grad = jnp.where((place >> bit) & 1 == 1, jnp.flip(grad, axis), grad)
    grad = jnp.moveaxis(grad, 0, bits).reshape(group * tokens, features)
    return (error[None], grad[None])


def solution(mesh):
    return jax.shard_map(
        on_device,
        mesh=mesh,
        in_specs=(
            P("layer", "groups", None),
            P("layer", None, None),
            P("layer", None),
            P("layer", "groups", None),
            P("layer", None, None, None),
            P("layer", "groups", None),
        ),
        out_specs=(P("layer", "groups", None), P("layer", "groups", None)),
        check_vma=False,
    )
```

```python
import jax
import jax.numpy as jnp
from jax import lax
from jax.sharding import PartitionSpec as P

BLOCK = 128
LAYERS = 4
TILE = 32
CORES = 2
AXIS = "layer"


def swap(value, mask):
    pairs = [(source, source ^ mask) for source in range(lax.axis_size(AXIS))]
    return lax.ppermute(value, AXIS, pairs)


def shifted(block, distance):
    devices = range(lax.axis_size(AXIS))
    route = [(i - distance, i) for i in devices if i - distance in devices]
    return lax.ppermute(block, AXIS, route)


def transposed(left, weight):
    return lax.dot_general(
        left, weight, (((1,), (1,)), ((), ())), preferred_element_type=jnp.float32
    )


def chip_sets(group):
    size = lax.axis_size(AXIS)
    return [
        [start + CORES * chip + core for chip in range(group // CORES)]
        for start in range(0, size, group)
        for core in range(CORES)
    ]


def gathered(slab, group):
    near = lax.all_gather(slab, AXIS, axis_index_groups=chip_sets(group), tiled=True)
    return jnp.concatenate([near, swap(near, 1)], axis=0)


def scattered(part, group):
    half = part.shape[0] // CORES
    got = swap(part[half:].astype(jnp.bfloat16), 1)
    total = (part[:half] + got.astype(jnp.float32)).astype(jnp.bfloat16)
    blocks = total.reshape(group // CORES, -1, part.shape[1])
    came = lax.all_to_all(blocks, AXIS, 0, 0, axis_index_groups=chip_sets(group))
    return jnp.sum(came.astype(jnp.float32), axis=0)


def on_device(resid, enc_weight, enc_bias, active, dec_weight, target):
    group = lax.axis_size(AXIS) // LAYERS
    chips = group // CORES
    place = lax.axis_index(AXIS) % group
    tokens = resid.shape[1]
    x = gathered(resid[0], group)
    pre = (
        jnp.dot(x, enc_weight[0], preferred_element_type=jnp.float32)
        + enc_bias[0].astype(jnp.float32)[None, :]
    )
    slab = jnp.arange(group, dtype=jnp.int32) % chips * CORES + (
        (place % CORES) ^ (jnp.arange(group, dtype=jnp.int32) // chips)
    )
    tile = (slab * tokens) // TILE
    pick = (tile[:, None] == jnp.arange(active.shape[1], dtype=jnp.int32)[None, :]).astype(jnp.int32)
    live = jnp.sum(pick[:, :, None] * active[0][None, :, :], axis=1)
    gate = jnp.repeat(jnp.repeat(live, tokens, axis=0), BLOCK, axis=1).astype(jnp.float32)
    codes = (jax.nn.relu(pre) * gate).astype(jnp.bfloat16)
    own_dec = dec_weight[0, 0]
    next_dec = dec_weight[0, 1]
    wanted = target[0].astype(jnp.float32)
    next_part = jnp.dot(codes, next_dec, preferred_element_type=jnp.float32)
    own_part = jnp.dot(codes, own_dec, preferred_element_type=jnp.float32)
    next_sum = scattered(next_part, group).astype(jnp.bfloat16)
    from_before = shifted(next_sum, group).astype(jnp.float32)
    own_sum = scattered(own_part, group)
    error = (own_sum + from_before - wanted).astype(jnp.bfloat16)
    later = shifted(error, -group)
    here_rows = gathered(error, group)
    after_rows = gathered(later, group)
    grad = transposed(here_rows, own_dec) + transposed(after_rows, next_dec)
    features = grad.shape[1]
    grad = grad.reshape(CORES, chips, tokens, features)
    grad = jnp.where(place % CORES == 1, jnp.flip(grad, 0), grad)
    grad = jnp.swapaxes(grad, 0, 1).reshape(group * tokens, features)
    return (error[None], grad[None])


def solution(mesh):
    return jax.shard_map(
        on_device,
        mesh=mesh,
        in_specs=(
            P("layer", "groups", None),
            P("layer", None, None),
            P("layer", None),
            P("layer", "groups", None),
            P("layer", None, None, None),
            P("layer", "groups", None),
        ),
        out_specs=(P("layer", "groups", None), P("layer", "groups", None)),
        check_vma=False,
    )
```

```python
import jax
import jax.numpy as jnp
from jax import lax
from jax.experimental import pallas as pl
from jax.experimental.pallas import tpu as pltpu
from jax.sharding import PartitionSpec as P

BLOCK = 128
LAYERS = 4
TILE = 32
CORES = 2
AXIS = "layer"


def swap(value, mask):
    pairs = [(source, source ^ mask) for source in range(lax.axis_size(AXIS))]
    return lax.ppermute(value, AXIS, pairs)


def shifted(block, distance):
    devices = range(lax.axis_size(AXIS))
    route = [(i - distance, i) for i in devices if i - distance in devices]
    return lax.ppermute(block, AXIS, route)


def transposed(left, weight):
    return lax.dot_general(
        left, weight, (((1,), (1,)), ((), ())), preferred_element_type=jnp.float32
    )


def gathered(slab, chips):
    near = [slab] + [swap(slab, CORES * chip) for chip in range(1, chips)]
    far = [swap(piece, 1) for piece in near]
    return jnp.concatenate(near + far, axis=0)


def scattered(part, chips):
    half = part.shape[0] // CORES
    rows = half // chips
    got = swap(part[half:].astype(jnp.bfloat16), 1)
    total = part[:half] + got.astype(jnp.float32)
    sends = [total[chip * rows : (chip + 1) * rows].astype(jnp.bfloat16) for chip in range(1, chips)]
    came = [swap(sends[chip - 1], CORES * chip) for chip in range(1, chips)]
    out = total[:rows]
    for block in came:
        out = out + block.astype(jnp.float32)
    return out


def load_kernel(*refs):
    count = len(refs) // 2
    sources, held, sems = refs[:count], refs[count : 2 * count], refs[-1]
    copies = [
        pltpu.make_async_copy(source, target, sems.at[i])
        for i, (source, target) in enumerate(zip(sources, held))
    ]
    for copy in copies:
        copy.start()
    for copy in copies:
        copy.wait()


def loaded(*weights):
    size = sum(w.size * w.dtype.itemsize for w in weights)
    return pl.pallas_call(
        load_kernel,
        out_shape=[pltpu.VMEM(w.shape, w.dtype) for w in weights],
        in_specs=[pl.BlockSpec(memory_space=pl.ANY)] * len(weights),
        out_specs=[pl.BlockSpec(memory_space=pltpu.VMEM)] * len(weights),
        scratch_shapes=[pltpu.SemaphoreType.DMA((len(weights),))],
        compiler_params=pltpu.CompilerParams(vmem_limit_bytes=1 << 20),
        cost_estimate=pl.CostEstimate(flops=0, bytes_accessed=2 * size, transcendentals=0),
        name="load_weights",
    )(*[pltpu.with_memory_space_constraint(w, pltpu.HBM) for w in weights])


def on_device(resid, enc_weight, enc_bias, active, dec_weight, target):
    group = lax.axis_size(AXIS) // LAYERS
    chips = group // CORES
    bits = chips.bit_length() - 1
    place = lax.axis_index(AXIS) % group
    tokens = resid.shape[1]
    enc, dec = loaded(enc_weight, dec_weight)
    x = gathered(resid[0], chips)
    pre = (
        jnp.dot(x, enc[0], preferred_element_type=jnp.float32)
        + enc_bias[0].astype(jnp.float32)[None, :]
    )
    order = jnp.array(
        [CORES * chip + core for core in range(CORES) for chip in range(chips)], dtype=jnp.int32
    )
    slab = jnp.bitwise_xor(order, place)
    tile = (slab * tokens) // TILE
    pick = (tile[:, None] == jnp.arange(active.shape[1], dtype=jnp.int32)[None, :]).astype(jnp.int32)
    live = jnp.sum(pick[:, :, None] * active[0][None, :, :], axis=1)
    gate = jnp.repeat(jnp.repeat(live, tokens, axis=0), BLOCK, axis=1).astype(jnp.float32)
    codes = (jax.nn.relu(pre) * gate).astype(jnp.bfloat16)
    own_dec = dec[0, 0]
    next_dec = dec[0, 1]
    wanted = target[0].astype(jnp.float32)
    next_part = jnp.dot(codes, next_dec, preferred_element_type=jnp.float32)
    own_part = jnp.dot(codes, own_dec, preferred_element_type=jnp.float32)
    next_sum = scattered(next_part, chips).astype(jnp.bfloat16)
    from_before = shifted(next_sum, group).astype(jnp.float32)
    own_sum = scattered(own_part, chips)
    error = (own_sum + from_before - wanted).astype(jnp.bfloat16)
    later = shifted(error, -group)
    here_rows = gathered(error, chips)
    after_rows = gathered(later, chips)
    grad = transposed(here_rows, own_dec) + transposed(after_rows, next_dec)
    features = grad.shape[1]
    grad = grad.reshape((2,) * (bits + 1) + (tokens, features))
    for axis in range(bits + 1):
        bit = 0 if axis == 0 else bits + 1 - axis
        grad = jnp.where((place >> bit) & 1 == 1, jnp.flip(grad, axis), grad)
    grad = jnp.moveaxis(grad, 0, bits).reshape(group * tokens, features)
    return (error[None], grad[None])


def solution(mesh):
    return jax.shard_map(
        on_device,
        mesh=mesh,
        in_specs=(
            P("layer", "groups", None),
            P("layer", None, None),
            P("layer", None),
            P("layer", "groups", None),
            P("layer", None, None, None),
            P("layer", "groups", None),
        ),
        out_specs=(P("layer", "groups", None), P("layer", "groups", None)),
        check_vma=False,
    )
```

```python
import functools

import jax
import jax.numpy as jnp
from jax import lax
from jax.experimental import pallas as pl
from jax.experimental.pallas import tpu as pltpu
from jax.sharding import PartitionSpec as P

BLOCK = 128
LAYERS = 4
TILE = 32
CORES = 2
AXIS = "layer"
CHUNK = 1024
LIMIT = 4 << 20


def swap(value, mask):
    pairs = [(source, source ^ mask) for source in range(lax.axis_size(AXIS))]
    return lax.ppermute(value, AXIS, pairs)


def shifted(block, distance):
    devices = range(lax.axis_size(AXIS))
    route = [(i - distance, i) for i in devices if i - distance in devices]
    return lax.ppermute(block, AXIS, route)


def in_vmem(*arrays):
    return [pltpu.with_memory_space_constraint(a, pltpu.VMEM) for a in arrays]


VMEM_SPEC = pl.BlockSpec(memory_space=pltpu.VMEM)
SMEM_SPEC = pl.BlockSpec(memory_space=pltpu.SMEM)


def gathered(slab, chips):
    near = [slab] + [swap(slab, CORES * chip) for chip in range(1, chips)]
    far = [swap(piece, 1) for piece in near]
    return jnp.concatenate(near + far, axis=0)


def scattered(near, far, chips):
    rows = near.shape[0] // chips
    total = near + swap(far, 1).astype(jnp.float32)
    sends = [total[chip * rows : (chip + 1) * rows].astype(jnp.bfloat16) for chip in range(1, chips)]
    came = [swap(sends[chip - 1], CORES * chip) for chip in range(1, chips)]
    out = total[:rows]
    for block in came:
        out = out + block.astype(jnp.float32)
    return out


def load_kernel(*refs):
    count = len(refs) // 2
    sources, held, sems = refs[:count], refs[count : 2 * count], refs[-1]
    copies = [
        pltpu.make_async_copy(source, target, sems.at[i])
        for i, (source, target) in enumerate(zip(sources, held))
    ]
    for copy in copies:
        copy.start()
    for copy in copies:
        copy.wait()


def loaded(*weights):
    size = sum(w.size * w.dtype.itemsize for w in weights)
    return pl.pallas_call(
        load_kernel,
        out_shape=[pltpu.VMEM(w.shape, w.dtype) for w in weights],
        in_specs=[pl.BlockSpec(memory_space=pl.ANY)] * len(weights),
        out_specs=[pl.BlockSpec(memory_space=pltpu.VMEM)] * len(weights),
        scratch_shapes=[pltpu.SemaphoreType.DMA((len(weights),))],
        compiler_params=pltpu.CompilerParams(vmem_limit_bytes=1 << 20),
        cost_estimate=pl.CostEstimate(flops=0, bytes_accessed=2 * size, transcendentals=0),
        name="load_weights",
    )(*[pltpu.with_memory_space_constraint(w, pltpu.HBM) for w in weights])


def decode(codes, dec_ref, reach, near_ref, far_ref):
    half, width = near_ref.shape

    @pl.loop(0, width // CHUNK)
    def _(step):
        columns = pl.ds(pl.multiple_of(step * CHUNK, CHUNK), CHUNK)
        part = jnp.dot(codes, dec_ref[0, reach, :, columns], preferred_element_type=jnp.float32)
        near_ref[:, columns] = part[:half]
        far_ref[:, columns] = part[half:].astype(jnp.bfloat16)


def encode_kernel(tokens, place_ref, active_ref, x_ref, enc_ref, bias_ref, dec_ref, codes_ref, near_ref, far_ref, held):
    rows, depth = x_ref.shape
    group = rows // tokens
    chips = group // CORES

    def step(i, total):
        part = pl.ds(pl.multiple_of(i * CHUNK, CHUNK), CHUNK)
        return total + jnp.dot(x_ref[:, part], enc_ref[0, part, :], preferred_element_type=jnp.float32)

    pre = lax.fori_loop(0, depth // CHUNK, step, jnp.zeros((rows, enc_ref.shape[2]), jnp.float32))
    held[...] = jnp.maximum(pre + bias_ref[...].astype(jnp.float32), 0.0)
    for block in range(group):
        core, chip = block // chips, block % chips
        tile = ((place_ref[0] ^ (CORES * chip + core)) * tokens) // TILE
        for part in range(active_ref.shape[1]):
            where = (pl.ds(block * tokens, tokens), pl.ds(part * BLOCK, BLOCK))
            held[where] = held[where] * active_ref[tile, part].astype(jnp.float32)
    codes_ref[...] = held[...].astype(jnp.bfloat16)
    decode(codes_ref[...], dec_ref, 1, near_ref, far_ref)


def decode_kernel(codes_ref, dec_ref, near_ref, far_ref):
    decode(codes_ref[...], dec_ref, 0, near_ref, far_ref)


def halves_of(rows, width):
    return [pltpu.VMEM((rows // CORES, width), jnp.float32), pltpu.VMEM((rows // CORES, width), jnp.bfloat16)]


def encoded(place, active, x, enc, bias, dec, tokens):
    rows, depth = x.shape
    features = enc.shape[2]
    return pl.pallas_call(
        functools.partial(encode_kernel, tokens),
        out_shape=[pltpu.VMEM((rows, features), jnp.bfloat16)] + halves_of(rows, depth),
        in_specs=[SMEM_SPEC, SMEM_SPEC] + [VMEM_SPEC] * 4,
        out_specs=[VMEM_SPEC] * 3,
        scratch_shapes=[pltpu.VMEM((rows, features), jnp.float32)],
        compiler_params=pltpu.CompilerParams(vmem_limit_bytes=LIMIT),
        cost_estimate=pl.CostEstimate(flops=4 * rows * depth * features, bytes_accessed=4 * depth * features, transcendentals=0),
        name="encode",
    )(place, active, *in_vmem(x, enc, bias, dec))


def decoded(codes, dec):
    rows, features = codes.shape
    width = dec.shape[3]
    return pl.pallas_call(
        decode_kernel,
        out_shape=halves_of(rows, width),
        in_specs=[VMEM_SPEC] * 2,
        out_specs=[VMEM_SPEC] * 2,
        compiler_params=pltpu.CompilerParams(vmem_limit_bytes=LIMIT),
        cost_estimate=pl.CostEstimate(flops=2 * rows * width * features, bytes_accessed=2 * width * features, transcendentals=0),
        name="decode_own",
    )(*in_vmem(codes, dec))


def back(rows_ref, dec_ref, reach, total):
    def step(i, total):
        part = pl.ds(pl.multiple_of(i * CHUNK, CHUNK), CHUNK)
        return total + lax.dot_general(
            rows_ref[:, part], dec_ref[0, reach, :, part], (((1,), (1,)), ((), ())), preferred_element_type=jnp.float32
        )

    return lax.fori_loop(0, rows_ref.shape[1] // CHUNK, step, total)


def grad_own_kernel(rows_ref, dec_ref, out_ref):
    out_ref[...] = back(rows_ref, dec_ref, 0, jnp.zeros(out_ref.shape, jnp.float32))


def grad_kernel(tokens, place_ref, rows_ref, dec_ref, own_ref, out_ref):
    total = back(rows_ref, dec_ref, 1, own_ref[...])
    group = rows_ref.shape[0] // tokens
    chips = group // CORES
    for block in range(group):
        slab = place_ref[0] ^ (CORES * (block % chips) + block // chips)
        out_ref[0, pl.ds(pl.multiple_of(slab * tokens, tokens), tokens), :] = total[block * tokens : (block + 1) * tokens]


def grad_own(rows, dec):
    shape = (rows.shape[0], dec.shape[2])
    return pl.pallas_call(
        grad_own_kernel,
        out_shape=pltpu.VMEM(shape, jnp.float32),
        in_specs=[VMEM_SPEC] * 2,
        out_specs=VMEM_SPEC,
        compiler_params=pltpu.CompilerParams(vmem_limit_bytes=LIMIT),
        cost_estimate=pl.CostEstimate(flops=2 * rows.size * shape[1], bytes_accessed=dec.size, transcendentals=0),
        name="grad_own",
    )(*in_vmem(rows, dec))


def grad_all(place, rows, dec, own, tokens):
    return pl.pallas_call(
        functools.partial(grad_kernel, tokens),
        out_shape=jax.ShapeDtypeStruct((1,) + own.shape, jnp.float32),
        in_specs=[SMEM_SPEC] + [VMEM_SPEC] * 3,
        out_specs=VMEM_SPEC,
        compiler_params=pltpu.CompilerParams(vmem_limit_bytes=LIMIT),
        cost_estimate=pl.CostEstimate(flops=2 * rows.size * own.shape[1], bytes_accessed=dec.size, transcendentals=0),
        name="grad_all",
    )(place, *in_vmem(rows, dec, own))


def on_device(resid, enc_weight, enc_bias, active, dec_weight, target):
    group = lax.axis_size(AXIS) // LAYERS
    chips = group // CORES
    place = (lax.axis_index(AXIS) % group).astype(jnp.int32).reshape(1)
    tokens = resid.shape[1]
    enc, dec = loaded(enc_weight, dec_weight)
    x = gathered(resid[0], chips)
    codes, next_near, next_far = encoded(place, active[0], x, enc, enc_bias, dec, tokens)
    own_near, own_far = decoded(codes, dec)
    next_sum = scattered(next_near, next_far, chips).astype(jnp.bfloat16)
    from_before = shifted(next_sum, group).astype(jnp.float32)
    own_sum = scattered(own_near, own_far, chips)
    error = (own_sum + from_before - target[0].astype(jnp.float32)).astype(jnp.bfloat16)

    later = shifted(error, -group)
    here = [error] + [swap(error, CORES * chip) for chip in range(1, chips)]
    after = [later] + [swap(later, CORES * chip) for chip in range(1, chips - 1)]
    last = shifted(here[-1], -group)
    here_near = jnp.concatenate(here, axis=0)
    here_rows = jnp.concatenate([here_near, swap(here_near, 1)], axis=0)
    after_most = jnp.concatenate(after, axis=0)
    after_rows = jnp.concatenate([after_most, last, swap(after_most, 1), swap(last, 1)], axis=0)
    grad = grad_all(place, after_rows, dec, grad_own(here_rows, dec), tokens)
    return (error[None], grad)


def solution(mesh):
    return jax.shard_map(
        on_device,
        mesh=mesh,
        in_specs=(
            P("layer", "groups", None),
            P("layer", None, None),
            P("layer", None),
            P("layer", "groups", None),
            P("layer", None, None, None),
            P("layer", "groups", None),
        ),
        out_specs=(P("layer", "groups", None), P("layer", "groups", None)),
        check_vma=False,
    )
```

```python
import functools

import jax
import jax.numpy as jnp
from jax import lax
from jax.experimental import pallas as pl
from jax.experimental.pallas import tpu as pltpu
from jax.sharding import PartitionSpec as P

BLOCK = 128
LAYERS = 4
TILE = 32
CORES = 2
AXIS = "layer"
CHUNK = 1024
LIMIT = 4 << 20


def swap(value, mask):
    pairs = [(source, source ^ mask) for source in range(lax.axis_size(AXIS))]
    return lax.ppermute(value, AXIS, pairs)


def shifted(block, distance):
    devices = range(lax.axis_size(AXIS))
    route = [(i - distance, i) for i in devices if i - distance in devices]
    return lax.ppermute(block, AXIS, route)


def in_vmem(*arrays):
    return [pltpu.with_memory_space_constraint(a, pltpu.VMEM) for a in arrays]


VMEM_SPEC = pl.BlockSpec(memory_space=pltpu.VMEM)
SMEM_SPEC = pl.BlockSpec(memory_space=pltpu.SMEM)


def gathered(slab, chips):
    near = [slab] + [swap(slab, CORES * chip) for chip in range(1, chips)]
    far = [swap(piece, 1) for piece in near]
    return jnp.concatenate(near + far, axis=0)


def blocks_of(near, far, chips):
    rows = near.shape[0] // chips
    total = near + swap(far, 1).astype(jnp.float32)
    return [total[chip * rows : (chip + 1) * rows] for chip in range(chips)]


def summed(blocks, sent):
    total = blocks[0]
    for came in [swap(blocks[chip].astype(jnp.bfloat16), CORES * chip) for chip in sent]:
        total = total + came.astype(jnp.float32)
    return total


def load_kernel(*refs):
    count = len(refs) // 2
    sources, held, sems = refs[:count], refs[count : 2 * count], refs[-1]
    copies = [
        pltpu.make_async_copy(source, target, sems.at[i])
        for i, (source, target) in enumerate(zip(sources, held))
    ]
    for copy in copies:
        copy.start()
    for copy in copies:
        copy.wait()


def loaded(*weights):
    size = sum(w.size * w.dtype.itemsize for w in weights)
    return pl.pallas_call(
        load_kernel,
        out_shape=[pltpu.VMEM(w.shape, w.dtype) for w in weights],
        in_specs=[pl.BlockSpec(memory_space=pl.ANY)] * len(weights),
        out_specs=[pl.BlockSpec(memory_space=pltpu.VMEM)] * len(weights),
        scratch_shapes=[pltpu.SemaphoreType.DMA((len(weights),))],
        compiler_params=pltpu.CompilerParams(vmem_limit_bytes=1 << 20),
        cost_estimate=pl.CostEstimate(flops=0, bytes_accessed=2 * size, transcendentals=0),
        name="load_weights",
    )(*[pltpu.with_memory_space_constraint(w, pltpu.HBM) for w in weights])


def decode(codes, dec_ref, reach, near_ref, far_ref):
    half, width = near_ref.shape

    for step in range(width // CHUNK):
        columns = pl.ds(step * CHUNK, CHUNK)
        part = jnp.dot(codes, dec_ref[0, reach, :, columns], preferred_element_type=jnp.float32)
        near_ref[:, columns] = part[:half]
        far_ref[:, columns] = part[half:].astype(jnp.bfloat16)


def encode_kernel(tokens, place_ref, active_ref, x_ref, enc_ref, bias_ref, dec_ref, codes_ref, near_ref, far_ref, held):
    rows, depth = x_ref.shape
    group = rows // tokens
    chips = group // CORES

    pre = jnp.dot(x_ref[...], enc_ref[0], preferred_element_type=jnp.float32)
    held[...] = jnp.maximum(pre + bias_ref[...].astype(jnp.float32), 0.0)
    for block in range(group):
        core, chip = block // chips, block % chips
        tile = ((place_ref[0] ^ (CORES * chip + core)) * tokens) // TILE
        for part in range(active_ref.shape[1]):
            where = (pl.ds(block * tokens, tokens), pl.ds(part * BLOCK, BLOCK))
            held[where] = held[where] * active_ref[tile, part].astype(jnp.float32)
    codes_ref[...] = held[...].astype(jnp.bfloat16)
    decode(codes_ref[...], dec_ref, 1, near_ref, far_ref)


def decode_kernel(codes_ref, dec_ref, near_ref, far_ref):
    decode(codes_ref[...], dec_ref, 0, near_ref, far_ref)


def halves_of(rows, width):
    return [pltpu.VMEM((rows // CORES, width), jnp.float32), pltpu.VMEM((rows // CORES, width), jnp.bfloat16)]


def encoded(place, active, x, enc, bias, dec, tokens):
    rows, depth = x.shape
    features = enc.shape[2]
    return pl.pallas_call(
        functools.partial(encode_kernel, tokens),
        out_shape=[pltpu.VMEM((rows, features), jnp.bfloat16)] + halves_of(rows, depth),
        in_specs=[SMEM_SPEC, SMEM_SPEC] + [VMEM_SPEC] * 4,
        out_specs=[VMEM_SPEC] * 3,
        scratch_shapes=[pltpu.VMEM((rows, features), jnp.float32)],
        compiler_params=pltpu.CompilerParams(vmem_limit_bytes=LIMIT),
        cost_estimate=pl.CostEstimate(flops=4 * rows * depth * features, bytes_accessed=4 * depth * features, transcendentals=0),
        name="encode",
    )(place, active, *in_vmem(x, enc, bias, dec))


def decoded(codes, dec):
    rows, features = codes.shape
    width = dec.shape[3]
    return pl.pallas_call(
        decode_kernel,
        out_shape=halves_of(rows, width),
        in_specs=[VMEM_SPEC] * 2,
        out_specs=[VMEM_SPEC] * 2,
        compiler_params=pltpu.CompilerParams(vmem_limit_bytes=LIMIT),
        cost_estimate=pl.CostEstimate(flops=2 * rows * width * features, bytes_accessed=2 * width * features, transcendentals=0),
        name="decode_own",
    )(*in_vmem(codes, dec))


def back(rows_ref, dec_ref, reach, total):
    return total + lax.dot_general(
        rows_ref[...], dec_ref[0, reach], (((1,), (1,)), ((), ())), preferred_element_type=jnp.float32
    )


def grad_own_kernel(rows_ref, dec_ref, out_ref):
    out_ref[...] = back(rows_ref, dec_ref, 0, jnp.zeros(out_ref.shape, jnp.float32))


def grad_kernel(tokens, place_ref, rows_ref, dec_ref, own_ref, out_ref):
    total = back(rows_ref, dec_ref, 1, own_ref[...])
    group = rows_ref.shape[0] // tokens
    chips = group // CORES
    for block in range(group):
        slab = place_ref[0] ^ (CORES * (block % chips) + block // chips)
        out_ref[0, pl.ds(pl.multiple_of(slab * tokens, tokens), tokens), :] = total[block * tokens : (block + 1) * tokens]


def grad_own(rows, dec):
    shape = (rows.shape[0], dec.shape[2])
    return pl.pallas_call(
        grad_own_kernel,
        out_shape=pltpu.VMEM(shape, jnp.float32),
        in_specs=[VMEM_SPEC] * 2,
        out_specs=VMEM_SPEC,
        compiler_params=pltpu.CompilerParams(vmem_limit_bytes=LIMIT),
        cost_estimate=pl.CostEstimate(flops=2 * rows.size * shape[1], bytes_accessed=dec.size, transcendentals=0),
        name="grad_own",
    )(*in_vmem(rows, dec))


def grad_all(place, rows, dec, own, tokens):
    return pl.pallas_call(
        functools.partial(grad_kernel, tokens),
        out_shape=jax.ShapeDtypeStruct((1,) + own.shape, jnp.float32),
        in_specs=[SMEM_SPEC] + [VMEM_SPEC] * 3,
        out_specs=VMEM_SPEC,
        compiler_params=pltpu.CompilerParams(vmem_limit_bytes=LIMIT),
        cost_estimate=pl.CostEstimate(flops=2 * rows.size * own.shape[1], bytes_accessed=dec.size, transcendentals=0),
        name="grad_all",
    )(place, *in_vmem(rows, dec, own))


def on_device(resid, enc_weight, enc_bias, active, dec_weight, target):
    group = lax.axis_size(AXIS) // LAYERS
    chips = group // CORES
    place = (lax.axis_index(AXIS) % group).astype(jnp.int32).reshape(1)
    tokens = resid.shape[1]
    (enc,), (dec,) = loaded(enc_weight), loaded(dec_weight)
    x = gathered(resid[0], chips)
    codes, next_near, next_far = encoded(place, active[0], x, enc, enc_bias, dec, tokens)
    own_near, own_far = decoded(codes, dec)
    nexts = blocks_of(next_near, next_far, chips)
    owns = blocks_of(own_near, own_far, chips)
    risen = shifted(nexts[-1].astype(jnp.bfloat16), group)
    next_sum = summed(nexts, range(1, chips - 1)).astype(jnp.bfloat16)
    owns[-1] = owns[-1] + risen.astype(jnp.float32)
    from_before = shifted(next_sum, group).astype(jnp.float32)
    own_sum = summed(owns, range(1, chips))
    error = (own_sum + from_before - target[0].astype(jnp.float32)).astype(jnp.bfloat16)

    later = shifted(error, -group)
    here = [error] + [swap(error, CORES * chip) for chip in range(1, chips)]
    after = [later] + [swap(later, CORES * chip) for chip in range(1, chips - 1)]
    here[-1], _ = lax.optimization_barrier((here[-1], later))
    last = shifted(here[-1], -group)
    here_near = jnp.concatenate(here, axis=0)
    here_far = swap(here_near, 1)
    here_rows = jnp.concatenate([here_near, here_far], axis=0)
    after_most, _ = lax.optimization_barrier((jnp.concatenate(after, axis=0), here_far))
    after_rows = jnp.concatenate([after_most, last, swap(after_most, 1), swap(last, 1)], axis=0)
    grad = grad_all(place, after_rows, dec, grad_own(here_rows, dec), tokens)
    return (error[None], grad)


def solution(mesh):
    return jax.shard_map(
        on_device,
        mesh=mesh,
        in_specs=(
            P("layer", "groups", None),
            P("layer", None, None),
            P("layer", None),
            P("layer", "groups", None),
            P("layer", None, None, None),
            P("layer", "groups", None),
        ),
        out_specs=(P("layer", "groups", None), P("layer", "groups", None)),
        check_vma=False,
    )
```

```python
import functools

import jax
import jax.numpy as jnp
from jax import lax
from jax.experimental import pallas as pl
from jax.experimental.pallas import tpu as pltpu
from jax.sharding import PartitionSpec as P

BLOCK = 128
LAYERS = 4
TILE = 32
CORES = 2
PARTS = 2
CHUNK = 1024
LIMIT = 20 << 20
AXIS = "layer"

ANY_SPEC = pl.BlockSpec(memory_space=pl.ANY)
VMEM_SPEC = pl.BlockSpec(memory_space=pltpu.VMEM)
SMEM_SPEC = pl.BlockSpec(memory_space=pltpu.SMEM)


def swap(value, mask):
    pairs = [(source, source ^ mask) for source in range(lax.axis_size(AXIS))]
    return lax.ppermute(value, AXIS, pairs)


def swap_inner(value, group):
    pairs = []
    for low in range(1, LAYERS - 1, 2):
        for i in range(low * group, (low + 1) * group):
            pairs += [(i, i + group), (i + group, i)]
    return lax.ppermute(value, AXIS, pairs)


def in_vmem(*arrays):
    return [pltpu.with_memory_space_constraint(a, pltpu.VMEM) for a in arrays]


def in_hbm(*arrays):
    return [pltpu.with_memory_space_constraint(a, pltpu.HBM) for a in arrays]


def slab_of(place_ref, block, chips):
    return place_ref[0] ^ (CORES * (block % chips) + block // chips)


def load_kernel(tokens, place_ref, active_ref, enc_hbm, dec_hbm, gate_ref, enc_ref, *rest):
    dec_refs, sems = rest[:-1], rest[-1]
    width = dec_refs[0].shape[2]
    copies = [pltpu.make_async_copy(enc_hbm.at[0], enc_ref, sems.at[0])]
    for i, dec_ref in enumerate(dec_refs):
        source = dec_hbm.at[0, :, :, pl.ds(i * width, width)]
        copies.append(pltpu.make_async_copy(source, dec_ref, sems.at[i + 1]))
    for copy in copies:
        copy.start()
    group = gate_ref.shape[0] // tokens
    for block in range(group):
        tile = (slab_of(place_ref, block, group // CORES) * tokens) // TILE
        for part in range(active_ref.shape[1]):
            live = active_ref[tile, part].astype(jnp.float32)
            gate_ref[pl.ds(block * tokens, tokens), pl.ds(part * BLOCK, BLOCK)] = jnp.full((tokens, BLOCK), live)
    for copy in copies:
        copy.wait()


def loaded(place, active, enc, dec, tokens, group):
    _, depth, features = enc.shape
    _, reach, _, width = dec.shape
    dtype = enc.dtype
    return pl.pallas_call(
        functools.partial(load_kernel, tokens),
        out_shape=[pltpu.VMEM((group * tokens, features), jnp.float32), pltpu.VMEM((depth, features), dtype)]
        + [pltpu.VMEM((reach, features, width // PARTS), dtype)] * PARTS,
        in_specs=[SMEM_SPEC] * 2 + [ANY_SPEC] * 2,
        out_specs=[VMEM_SPEC] * (PARTS + 2),
        scratch_shapes=[pltpu.SemaphoreType.DMA((PARTS + 1,))],
        compiler_params=pltpu.CompilerParams(vmem_limit_bytes=1 << 20),
        cost_estimate=pl.CostEstimate(flops=0, bytes_accessed=4 * (enc.size + dec.size), transcendentals=0),
        name="load_weights",
    )(place, active, *in_hbm(enc, dec))


def decode_kernel(tokens, codes_ref, dec_ref, near_ref, far_ref):
    half = near_ref.shape[0]
    for step in range(near_ref.shape[1] // CHUNK):
        columns = pl.ds(step * CHUNK, CHUNK)
        own, later = [
            jnp.dot(codes_ref[...], dec_ref[reach, :, columns], preferred_element_type=jnp.float32)
            for reach in range(2)
        ]
        mixed = []
        for row in range(0, own.shape[0], tokens):
            mixed += [later[row : row + tokens], own[row : row + tokens]]
        mixed = jnp.concatenate(mixed, axis=0)
        near_ref[:, columns] = mixed[:half]
        far_ref[:, columns] = mixed[half:].astype(jnp.bfloat16)


def decoded(codes, dec, tokens):
    rows, features = codes.shape
    reach, _, width = dec.shape
    half = reach * rows // CORES
    return pl.pallas_call(
        functools.partial(decode_kernel, tokens),
        out_shape=[pltpu.VMEM((half, width), jnp.float32), pltpu.VMEM((half, width), jnp.bfloat16)],
        in_specs=[VMEM_SPEC] * 2,
        out_specs=[VMEM_SPEC] * 2,
        compiler_params=pltpu.CompilerParams(vmem_limit_bytes=LIMIT),
        cost_estimate=pl.CostEstimate(flops=4 * rows * width * features, bytes_accessed=2 * dec.size, transcendentals=0),
        name="decode",
    )(*in_vmem(codes, dec))


def grad_part(tokens, near_ref, far_ref, dec_ref, blocks):
    out = []
    for rows_ref in (near_ref, far_ref):
        here, after = [
            lax.dot_general(
                rows_ref[...], dec_ref[reach], (((1,), (1,)), ((), ())), preferred_element_type=jnp.float32
            )
            for reach in range(2)
        ]
        for row in range(0, here.shape[0], 2 * tokens):
            out.append(here[row : row + tokens] + after[row + tokens : row + 2 * tokens])
    return out if blocks is None else [a + b for a, b in zip(blocks, out)]


def grad_first_kernel(tokens, near_ref, far_ref, dec_ref, out_ref, used_ref):
    blocks = grad_part(tokens, near_ref, far_ref, dec_ref, None)
    for i, block in enumerate(blocks):
        out_ref[pl.ds(i * tokens, tokens), :] = block
    used_ref[...] = jnp.zeros(used_ref.shape, jnp.float32)


def grad_last_kernel(tokens, place_ref, near_ref, far_ref, dec_ref, so_far_ref, out_ref):
    group = so_far_ref.shape[0] // tokens
    so_far = [so_far_ref[pl.ds(i * tokens, tokens), :] for i in range(group)]
    blocks = grad_part(tokens, near_ref, far_ref, dec_ref, so_far)
    for i, block in enumerate(blocks):
        slab = slab_of(place_ref, i, group // CORES)
        out_ref[0, pl.ds(pl.multiple_of(slab * tokens, tokens), tokens), :] = block


def grad_cost(near, dec):
    return pl.CostEstimate(flops=4 * near.size * dec.shape[1], bytes_accessed=2 * dec.size, transcendentals=0)


def grad_first(near, far, dec, tokens):
    return pl.pallas_call(
        functools.partial(grad_first_kernel, tokens),
        out_shape=[pltpu.VMEM((near.shape[0], dec.shape[1]), jnp.float32), pltpu.VMEM((8, 128), jnp.float32)],
        in_specs=[VMEM_SPEC] * 3,
        out_specs=[VMEM_SPEC] * 2,
        compiler_params=pltpu.CompilerParams(vmem_limit_bytes=LIMIT),
        cost_estimate=grad_cost(near, dec),
        name="grad_first",
    )(*in_vmem(near, far, dec))[0]


def grad_last(place, near, far, dec, so_far, tokens):
    return pl.pallas_call(
        functools.partial(grad_last_kernel, tokens),
        out_shape=jax.ShapeDtypeStruct((1,) + so_far.shape, jnp.float32),
        in_specs=[SMEM_SPEC] + [VMEM_SPEC] * 4,
        out_specs=VMEM_SPEC,
        compiler_params=pltpu.CompilerParams(vmem_limit_bytes=LIMIT),
        cost_estimate=grad_cost(near, dec),
        name="grad_last",
    )(place, *in_vmem(near, far, dec, so_far))


def reduced(near, far, chips):
    rows = near.shape[0] // chips
    total = near + swap(far, 1).astype(jnp.float32)
    sent = [total[chip * rows : (chip + 1) * rows].astype(jnp.bfloat16) for chip in range(chips)]
    came = [swap(sent[chip], CORES * chip) for chip in range(1, chips)]
    out = total[:rows]
    for block in came:
        out = out + block.astype(jnp.float32)
    return out


def exchanged(later_sum, own_less, layer, group):
    even = layer % 2 == 0
    up, down = later_sum.astype(jnp.bfloat16), own_less.astype(jnp.bfloat16)
    outer = swap(jnp.where(even, up, down), group)
    inner = swap_inner(jnp.where(even, down, up), group)
    below = jnp.where(even, inner, outer).astype(jnp.float32)
    above = jnp.where(even, outer, inner).astype(jnp.float32)
    here = (own_less + below).astype(jnp.bfloat16)
    after = jnp.where(layer == LAYERS - 1, 0.0, later_sum + above).astype(jnp.bfloat16)
    return here, after


def on_device(resid, enc_weight, enc_bias, active, dec_weight, target):
    group = lax.axis_size(AXIS) // LAYERS
    chips = group // CORES
    index = lax.axis_index(AXIS)
    layer = index // group
    place = (index % group).astype(jnp.int32).reshape(1)
    tokens = resid.shape[1]
    gate, enc, *decs = loaded(place, active[0], enc_weight, dec_weight, tokens, group)
    near = [resid[0]] + [swap(resid[0], CORES * chip) for chip in range(1, chips)]
    others = jnp.concatenate(near[1:], axis=0)
    x = jnp.concatenate(near + [swap(near[0], 1), swap(others, 1)], axis=0)
    pre = jnp.dot(x, enc, preferred_element_type=jnp.float32) + enc_bias.astype(jnp.float32)
    codes = (jax.nn.relu(pre) * gate).astype(jnp.bfloat16)

    width = decs[0].shape[2]
    parts = [decoded(codes, dec, tokens) for dec in decs]
    sums = [reduced(*part, chips) for part in parts]
    errors, grad = [], None
    for i, total in enumerate(sums):
        wanted = target[0, :, i * width : (i + 1) * width].astype(jnp.float32)
        here, after = exchanged(total[:tokens], total[tokens:] - wanted, layer, group)
        errors.append(here)
        both = jnp.concatenate([here, after], axis=0)
        near = jnp.concatenate([both] + [swap(both, CORES * chip) for chip in range(1, chips)], axis=0)
        far = swap(near, 1)
        if i < PARTS - 1:
            grad = grad_first(near, far, decs[i], tokens)
        else:
            grad = grad_last(place, near, far, decs[i], grad, tokens)
    return (jnp.concatenate(errors, axis=1)[None], grad)


def solution(mesh):
    return jax.shard_map(
        on_device,
        mesh=mesh,
        in_specs=(
            P("layer", "groups", None),
            P("layer", None, None),
            P("layer", None),
            P("layer", "groups", None),
            P("layer", None, None, None),
            P("layer", "groups", None),
        ),
        out_specs=(P("layer", "groups", None), P("layer", "groups", None)),
        check_vma=False,
    )
```

```python
import functools

import jax
import jax.numpy as jnp
from jax import lax
from jax.experimental import pallas as pl
from jax.experimental.pallas import tpu as pltpu
from jax.sharding import PartitionSpec as P

BLOCK = 128
LAYERS = 4
TILE = 32
CORES = 2
PARTS = 2
CHUNK = 1024
LIMIT = 10 << 20
AXIS = "layer"

ANY_SPEC = pl.BlockSpec(memory_space=pl.ANY)
VMEM_SPEC = pl.BlockSpec(memory_space=pltpu.VMEM)
SMEM_SPEC = pl.BlockSpec(memory_space=pltpu.SMEM)


def swap(value, mask):
    pairs = [(source, source ^ mask) for source in range(lax.axis_size(AXIS))]
    return lax.ppermute(value, AXIS, pairs)


def raised(value, layer, group):
    size = lax.axis_size(AXIS)
    came = lax.ppermute(value, AXIS, [(i, (i + group) % size) for i in range(size)])
    return jnp.where(layer == 0, jnp.zeros_like(came), came)


def lowered(value, layer, group):
    inner = []
    for low in range(LAYERS):
        away = 0 if low in (0, LAYERS - 1) else group if low % 2 == 1 else -group
        inner += [(i, i + away) for i in range(low * group, (low + 1) * group)]
    first = swap(value, group)
    second = lax.ppermute(value, AXIS, inner)
    came = jnp.where(layer % 2 == 0, first, second)
    return jnp.where(layer == LAYERS - 1, jnp.zeros_like(came), came)


def after(values, done):
    return lax.optimization_barrier((values, done))[0]


def bit_of(part, step, bits):
    return step if part % 2 == 0 else bits - 1 - step


def bits_left(part, step, bits):
    return sorted(set(range(bits)) - {bit_of(part, s, bits) for s in range(step)})[::-1]


def halve(parts, step, bits):
    out = []
    for i, part in enumerate(parts):
        bit = bit_of(i, step, bits)
        at = bits_left(i, step, bits).index(bit)
        sent = lax.index_in_dim(part, 1, at, keepdims=False).astype(jnp.bfloat16)
        kept = lax.index_in_dim(part, 0, at, keepdims=False)
        out.append(kept + swap(sent, CORES << bit).astype(jnp.float32))
    return out


def double(parts, step, bits):
    out = []
    for i, part in enumerate(parts):
        bit = bit_of(i, step, bits)
        had = {bit_of(i, s, bits) for s in range(step + 1)}
        at = sorted(had)[::-1].index(bit)
        out.append(jnp.stack([part, swap(part, CORES << bit)], axis=at))
    return out


def by_rows(parts):
    return [part.reshape(-1, part.shape[-1]) for part in parts]


def by_bits(total, bits):
    rows, width = total.shape[0] >> bits, total.shape[1] // PARTS
    return [total[:, i * width : (i + 1) * width].reshape((2,) * bits + (rows, width)) for i in range(PARTS)]


def split(slab):
    width = slab.shape[1] // PARTS
    return [slab[:, i * width : (i + 1) * width] for i in range(PARTS)]


def in_vmem(*arrays):
    return [pltpu.with_memory_space_constraint(a, pltpu.VMEM) for a in arrays]


def slab_of(place_ref, block, chips):
    return place_ref[0] ^ (CORES * (block % chips) + block // chips)


def kernel_params():
    return pltpu.CompilerParams(vmem_limit_bytes=LIMIT)


def load_kernel(pieces, weight_ref, *rest):
    held, sems = rest[:-1], rest[-1]
    copies = [
        pltpu.make_async_copy(weight_ref.at[piece], target, sems.at[i])
        for i, (piece, target) in enumerate(zip(pieces, held))
    ]
    for copy in copies:
        copy.start()
    for copy in copies:
        copy.wait()


def loaded(weight, pieces, shape):
    return pl.pallas_call(
        functools.partial(load_kernel, pieces),
        out_shape=[pltpu.VMEM(shape, weight.dtype)] * len(pieces),
        in_specs=[ANY_SPEC],
        out_specs=[VMEM_SPEC] * len(pieces),
        scratch_shapes=[pltpu.SemaphoreType.DMA((len(pieces),))],
        compiler_params=pltpu.CompilerParams(vmem_limit_bytes=1 << 20),
        cost_estimate=pl.CostEstimate(flops=0, bytes_accessed=4 * weight.size, transcendentals=0),
        name="load_weights",
    )(pltpu.with_memory_space_constraint(weight, pltpu.HBM))


def decode(codes, dec_ref, near_ref, far_ref):
    half, width = near_ref.shape
    for step in range(width // CHUNK):
        columns = pl.ds(step * CHUNK, CHUNK)
        part = jnp.dot(codes, dec_ref[:, columns], preferred_element_type=jnp.float32)
        near_ref[:, columns] = part[:half]
        far_ref[:, columns] = part[half:].astype(jnp.bfloat16)


def joined(refs):
    return [
        jnp.concatenate([near[...], far[...]], axis=0) for near, far in zip(refs[:PARTS], refs[PARTS:])
    ]


def encode_kernel(tokens, place_ref, active_ref, *refs):
    row_refs, enc_refs = refs[: 2 * PARTS], refs[2 * PARTS : 3 * PARTS]
    bias_ref, dec_hbm, codes_ref, near_ref, far_ref, own_ref, held, next_ref, sems = refs[3 * PARTS :]
    load_next = pltpu.make_async_copy(dec_hbm.at[0, 1], next_ref, sems.at[1])
    load_own = pltpu.make_async_copy(dec_hbm.at[0, 0], own_ref, sems.at[0])
    load_next.start()
    group = held.shape[0] // tokens
    pre = bias_ref[...].astype(jnp.float32)
    for rows, enc_ref in zip(joined(row_refs), enc_refs):
        pre = pre + jnp.dot(rows, enc_ref[...], preferred_element_type=jnp.float32)
    held[...] = jnp.maximum(pre, 0.0)
    for block in range(group):
        tile = (slab_of(place_ref, block, group // CORES) * tokens) // TILE
        for part in range(active_ref.shape[1]):
            where = (pl.ds(block * tokens, tokens), pl.ds(part * BLOCK, BLOCK))
            held[where] = held[where] * active_ref[tile, part].astype(jnp.float32)
    codes_ref[...] = held[...].astype(jnp.bfloat16)
    load_own.start()
    load_next.wait()
    decode(codes_ref[...], next_ref, near_ref, far_ref)
    load_own.wait()


def decode_kernel(codes_ref, dec_ref, near_ref, far_ref):
    decode(codes_ref[...], dec_ref, near_ref, far_ref)


def halves_of(rows, width):
    return [pltpu.VMEM((rows // CORES, width), jnp.float32), pltpu.VMEM((rows // CORES, width), jnp.bfloat16)]


def encoded(place, active, near, far, enc, bias, dec, tokens):
    rows = CORES * near[0].shape[0]
    features, depth = dec.shape[2:]
    return pl.pallas_call(
        functools.partial(encode_kernel, tokens),
        out_shape=[pltpu.VMEM((rows, features), jnp.bfloat16)] + halves_of(rows, depth) + [pltpu.VMEM((features, depth), dec.dtype)],
        in_specs=[SMEM_SPEC, SMEM_SPEC] + [VMEM_SPEC] * (3 * PARTS + 1) + [ANY_SPEC],
        out_specs=[VMEM_SPEC] * 4,
        scratch_shapes=[
            pltpu.VMEM((rows, features), jnp.float32),
            pltpu.VMEM((features, depth), dec.dtype),
            pltpu.SemaphoreType.DMA((2,)),
        ],
        compiler_params=kernel_params(),
        cost_estimate=pl.CostEstimate(flops=4 * rows * depth * features, bytes_accessed=4 * depth * features, transcendentals=0),
        name="encode",
    )(place, active, *in_vmem(*near, *far, *enc, bias), pltpu.with_memory_space_constraint(dec, pltpu.HBM))


def decoded(codes, dec):
    rows, features = codes.shape
    width = dec.shape[1]
    return pl.pallas_call(
        decode_kernel,
        out_shape=halves_of(rows, width),
        in_specs=[VMEM_SPEC] * 2,
        out_specs=[VMEM_SPEC] * 2,
        compiler_params=kernel_params(),
        cost_estimate=pl.CostEstimate(flops=2 * rows * width * features, bytes_accessed=2 * width * features, transcendentals=0),
        name="decode_own",
    )(*in_vmem(codes, dec))


def back(row_refs, dec_ref, reach):
    total = None
    for i, rows in enumerate(joined(row_refs)):
        width = rows.shape[1]
        part = lax.dot_general(
            rows,
            dec_ref[0, reach, :, pl.ds(i * width, width)],
            (((1,), (1,)), ((), ())),
            preferred_element_type=jnp.float32,
        )
        total = part if total is None else total + part
    return total


def grad_own_kernel(*refs):
    row_refs, (dec_ref, out_ref, _) = refs[: 2 * PARTS], refs[2 * PARTS :]
    out_ref[...] = back(row_refs, dec_ref, 0)


def grad_all_kernel(tokens, place_ref, *refs):
    row_refs, (dec_ref, own_ref, out_ref) = refs[: 2 * PARTS], refs[2 * PARTS :]
    total = own_ref[...] + back(row_refs, dec_ref, 1)
    group = total.shape[0] // tokens
    for block in range(group):
        slab = slab_of(place_ref, block, group // CORES)
        where = pl.ds(pl.multiple_of(slab * tokens, tokens), tokens)
        out_ref[0, where, :] = total[block * tokens : (block + 1) * tokens]


def grad_cost(near, dec):
    size = 2 * sum(part.size for part in near)
    return pl.CostEstimate(flops=2 * size * dec.shape[2], bytes_accessed=dec.size, transcendentals=0)


def grad_own(near, far, dec):
    shape = (CORES * near[0].shape[0], dec.shape[2])
    return pl.pallas_call(
        grad_own_kernel,
        out_shape=[pltpu.VMEM(shape, jnp.float32), pltpu.VMEM((8, 128), jnp.float32)],
        in_specs=[VMEM_SPEC] * (2 * PARTS + 1),
        out_specs=[VMEM_SPEC] * 2,
        compiler_params=kernel_params(),
        cost_estimate=grad_cost(near, dec),
        name="grad_own",
    )(*in_vmem(*near, *far, dec))[0]


def grad_all(place, near, far, dec, own, tokens):
    return pl.pallas_call(
        functools.partial(grad_all_kernel, tokens),
        out_shape=jax.ShapeDtypeStruct((1,) + own.shape, jnp.float32),
        in_specs=[SMEM_SPEC] + [VMEM_SPEC] * (2 * PARTS + 2),
        out_specs=VMEM_SPEC,
        compiler_params=kernel_params(),
        cost_estimate=grad_cost(near, dec),
        name="grad_all",
    )(place, *in_vmem(*near, *far, dec, own))


def on_device(resid, enc_weight, enc_bias, active, dec_weight, target):
    group = lax.axis_size(AXIS) // LAYERS
    chips = group // CORES
    bits = chips.bit_length() - 1
    index = lax.axis_index(AXIS)
    layer = index // group
    place = (index % group).astype(jnp.int32).reshape(1)
    tokens = resid.shape[1]
    _, depth, features = enc_weight.shape
    depth = depth // PARTS
    enc = loaded(enc_weight, [(0, pl.ds(i * depth, depth)) for i in range(PARTS)], (depth, features))
    near = split(resid[0])
    for step in range(bits):
        near = double(near if step == 0 else after(near, enc), step, bits)
    near = by_rows(near)
    far = [swap(part, 1) for part in near]
    codes, next_near, next_far, own_dec = encoded(place, active[0], near, far, enc, enc_bias, dec_weight, tokens)

    next_far = swap(next_far, 1)
    own_near, own_far = decoded(after(codes, next_far), own_dec)
    nexts = [by_bits(next_near + next_far.astype(jnp.float32), bits)]
    owns = by_bits(own_near + swap(own_far, 1).astype(jnp.float32), bits)
    for step in range(bits):
        nexts.append(halve(nexts[-1] if step == 0 else after(nexts[-1], owns), step, bits))
    for step in range(bits):
        owns = halve(after(owns, nexts[step + 1]), step, bits)
    next_sum = jnp.concatenate([part.astype(jnp.bfloat16) for part in nexts[-1]], axis=1)
    from_before = raised(next_sum, layer, group).astype(jnp.float32)
    own_sum = jnp.concatenate(owns, axis=1)
    error = (own_sum + from_before - target[0].astype(jnp.float32)).astype(jnp.bfloat16)

    later = lowered(error, layer, group)
    heres = [split(error)]
    for step in range(bits):
        heres.append(double(heres[-1], step, bits))
    here_near = by_rows(heres[-1])
    here_far = [swap(part, 1) for part in here_near]
    afters = split(later)
    for step in range(bits):
        afters = double(after(afters, heres[step + 1]), step, bits)
    after_near = after(by_rows(afters), here_far)
    after_far = [swap(part, 1) for part in after_near]
    own_grad = grad_own(here_near, here_far, dec_weight)
    grad = grad_all(place, after_near, after_far, dec_weight, own_grad, tokens)
    return (error[None], grad)


def solution(mesh):
    return jax.shard_map(
        on_device,
        mesh=mesh,
        in_specs=(
            P("layer", "groups", None),
            P("layer", None, None),
            P("layer", None),
            P("layer", "groups", None),
            P("layer", None, None, None),
            P("layer", "groups", None),
        ),
        out_specs=(P("layer", "groups", None), P("layer", "groups", None)),
        check_vma=False,
    )
```

```python
import functools

import jax
import jax.numpy as jnp
from jax import lax
from jax.experimental import pallas as pl
from jax.experimental.pallas import tpu as pltpu
from jax.sharding import PartitionSpec as P

BLOCK = 128
LAYERS = 4
TILE = 32
CORES = 2
AXIS = "layer"
CHUNK = 1024
LIMIT = 4 << 20


def swap(value, mask):
    pairs = [(source, source ^ mask) for source in range(lax.axis_size(AXIS))]
    return lax.ppermute(value, AXIS, pairs)


def raised(value, layer, group):
    size = lax.axis_size(AXIS)
    came = lax.ppermute(value, AXIS, [(i, (i + group) % size) for i in range(size)])
    return jnp.where(layer == 0, jnp.zeros_like(came), came)


def lowered(value, layer, group):
    size = lax.axis_size(AXIS)
    came = lax.ppermute(value, AXIS, [((i + group) % size, i) for i in range(size)])
    return jnp.where(layer == LAYERS - 1, jnp.zeros_like(came), came)


def in_vmem(*arrays):
    return [pltpu.with_memory_space_constraint(a, pltpu.VMEM) for a in arrays]


VMEM_SPEC = pl.BlockSpec(memory_space=pltpu.VMEM)
SMEM_SPEC = pl.BlockSpec(memory_space=pltpu.SMEM)


def gathered(slab, chips):
    near = [slab] + [swap(slab, CORES * chip) for chip in range(1, chips)]
    far = [swap(piece, 1) for piece in near]
    return jnp.concatenate(near + far, axis=0)


def blocks_of(near, far, chips):
    rows = near.shape[0] // chips
    total = near + swap(far, 1).astype(jnp.float32)
    return [total[chip * rows : (chip + 1) * rows] for chip in range(chips)]


def summed(blocks, sent):
    total = blocks[0]
    for came in [swap(blocks[chip].astype(jnp.bfloat16), CORES * chip) for chip in sent]:
        total = total + came.astype(jnp.float32)
    return total


def load_kernel(*refs):
    count = len(refs) // 2
    sources, held, sems = refs[:count], refs[count : 2 * count], refs[-1]
    copies = [
        pltpu.make_async_copy(source, target, sems.at[i])
        for i, (source, target) in enumerate(zip(sources, held))
    ]
    for copy in copies:
        copy.start()
    for copy in copies:
        copy.wait()


def loaded(*weights):
    size = sum(w.size * w.dtype.itemsize for w in weights)
    return pl.pallas_call(
        load_kernel,
        out_shape=[pltpu.VMEM(w.shape, w.dtype) for w in weights],
        in_specs=[pl.BlockSpec(memory_space=pl.ANY)] * len(weights),
        out_specs=[pl.BlockSpec(memory_space=pltpu.VMEM)] * len(weights),
        scratch_shapes=[pltpu.SemaphoreType.DMA((len(weights),))],
        compiler_params=pltpu.CompilerParams(vmem_limit_bytes=1 << 20),
        cost_estimate=pl.CostEstimate(flops=0, bytes_accessed=2 * size, transcendentals=0),
        name="load_weights",
    )(*[pltpu.with_memory_space_constraint(w, pltpu.HBM) for w in weights])


def decode(codes, dec_ref, reach, near_ref, far_ref):
    half, width = near_ref.shape

    for step in range(width // CHUNK):
        columns = pl.ds(step * CHUNK, CHUNK)
        part = jnp.dot(codes, dec_ref[0, reach, :, columns], preferred_element_type=jnp.float32)
        near_ref[:, columns] = part[:half]
        far_ref[:, columns] = part[half:].astype(jnp.bfloat16)


def encode_kernel(tokens, place_ref, active_ref, x_ref, enc_ref, bias_ref, dec_ref, codes_ref, near_ref, far_ref, held):
    rows, depth = x_ref.shape
    group = rows // tokens
    chips = group // CORES

    half = depth // 2
    pre = sum(
        jnp.dot(x_ref[:, part], enc_ref[0, part, :], preferred_element_type=jnp.float32)
        for part in (pl.ds(0, half), pl.ds(half, half))
    )
    held[...] = jnp.maximum(pre + bias_ref[...].astype(jnp.float32), 0.0)
    for block in range(group):
        core, chip = block // chips, block % chips
        tile = ((place_ref[0] ^ (CORES * chip + core)) * tokens) // TILE
        for part in range(active_ref.shape[1]):
            where = (pl.ds(block * tokens, tokens), pl.ds(part * BLOCK, BLOCK))
            held[where] = held[where] * active_ref[tile, part].astype(jnp.float32)
    codes_ref[...] = held[...].astype(jnp.bfloat16)
    decode(codes_ref[...], dec_ref, 1, near_ref, far_ref)


def decode_kernel(codes_ref, dec_ref, near_ref, far_ref):
    decode(codes_ref[...], dec_ref, 0, near_ref, far_ref)


def halves_of(rows, width):
    return [pltpu.VMEM((rows // CORES, width), jnp.float32), pltpu.VMEM((rows // CORES, width), jnp.bfloat16)]


def encoded(place, active, x, enc, bias, dec, tokens):
    rows, depth = x.shape
    features = enc.shape[2]
    return pl.pallas_call(
        functools.partial(encode_kernel, tokens),
        out_shape=[pltpu.VMEM((rows, features), jnp.bfloat16)] + halves_of(rows, depth),
        in_specs=[SMEM_SPEC, SMEM_SPEC] + [VMEM_SPEC] * 4,
        out_specs=[VMEM_SPEC] * 3,
        scratch_shapes=[pltpu.VMEM((rows, features), jnp.float32)],
        compiler_params=pltpu.CompilerParams(vmem_limit_bytes=LIMIT),
        cost_estimate=pl.CostEstimate(flops=4 * rows * depth * features, bytes_accessed=4 * depth * features, transcendentals=0),
        name="encode",
    )(place, active, *in_vmem(x, enc, bias, dec))


def decoded(codes, dec):
    rows, features = codes.shape
    width = dec.shape[3]
    return pl.pallas_call(
        decode_kernel,
        out_shape=halves_of(rows, width),
        in_specs=[VMEM_SPEC] * 2,
        out_specs=[VMEM_SPEC] * 2,
        compiler_params=pltpu.CompilerParams(vmem_limit_bytes=LIMIT),
        cost_estimate=pl.CostEstimate(flops=2 * rows * width * features, bytes_accessed=2 * width * features, transcendentals=0),
        name="decode_own",
    )(*in_vmem(codes, dec))


def back(rows_ref, dec_ref, reach, total):
    half = rows_ref.shape[1] // 2
    for part in (pl.ds(0, half), pl.ds(half, half)):
        total = total + lax.dot_general(
            rows_ref[:, part], dec_ref[0, reach, :, part], (((1,), (1,)), ((), ())), preferred_element_type=jnp.float32
        )
    return total


def grad_own_kernel(rows_ref, dec_ref, out_ref):
    out_ref[...] = back(rows_ref, dec_ref, 0, jnp.zeros(out_ref.shape, jnp.float32))


def grad_kernel(tokens, place_ref, rows_ref, dec_ref, own_ref, out_ref):
    total = back(rows_ref, dec_ref, 1, own_ref[...])
    group = rows_ref.shape[0] // tokens
    chips = group // CORES
    for block in range(group):
        slab = place_ref[0] ^ (CORES * (block % chips) + block // chips)
        out_ref[0, pl.ds(pl.multiple_of(slab * tokens, tokens), tokens), :] = total[block * tokens : (block + 1) * tokens]


def grad_own(rows, dec):
    shape = (rows.shape[0], dec.shape[2])
    return pl.pallas_call(
        grad_own_kernel,
        out_shape=pltpu.VMEM(shape, jnp.float32),
        in_specs=[VMEM_SPEC] * 2,
        out_specs=VMEM_SPEC,
        compiler_params=pltpu.CompilerParams(vmem_limit_bytes=LIMIT),
        cost_estimate=pl.CostEstimate(flops=2 * rows.size * shape[1], bytes_accessed=dec.size, transcendentals=0),
        name="grad_own",
    )(*in_vmem(rows, dec))


def grad_all(place, rows, dec, own, tokens):
    return pl.pallas_call(
        functools.partial(grad_kernel, tokens),
        out_shape=jax.ShapeDtypeStruct((1,) + own.shape, jnp.float32),
        in_specs=[SMEM_SPEC] + [VMEM_SPEC] * 3,
        out_specs=VMEM_SPEC,
        compiler_params=pltpu.CompilerParams(vmem_limit_bytes=LIMIT),
        cost_estimate=pl.CostEstimate(flops=2 * rows.size * own.shape[1], bytes_accessed=dec.size, transcendentals=0),
        name="grad_all",
    )(place, *in_vmem(rows, dec, own))


def on_device(resid, enc_weight, enc_bias, active, dec_weight, target):
    group = lax.axis_size(AXIS) // LAYERS
    chips = group // CORES
    index = lax.axis_index(AXIS)
    layer = index // group
    place = (index % group).astype(jnp.int32).reshape(1)
    tokens = resid.shape[1]
    enc, dec = loaded(enc_weight, dec_weight)
    x = gathered(resid[0], chips)
    codes, next_near, next_far = encoded(place, active[0], x, enc, enc_bias, dec, tokens)
    own_near, own_far = decoded(codes, dec)
    nexts = blocks_of(next_near, next_far, chips)
    owns = blocks_of(own_near, own_far, chips)
    risen = raised(nexts[-1].astype(jnp.bfloat16), layer, group)
    next_sum = summed(nexts, range(1, chips - 1)).astype(jnp.bfloat16)
    owns[-1] = owns[-1] + risen.astype(jnp.float32)
    from_before = raised(next_sum, layer, group).astype(jnp.float32)
    own_sum = summed(owns, range(1, chips))
    error = (own_sum + from_before - target[0].astype(jnp.float32)).astype(jnp.bfloat16)

    later = lowered(error, layer, group)
    here = [error] + [swap(error, CORES * chip) for chip in range(1, chips)]
    after = [later] + [swap(later, CORES * chip) for chip in range(1, chips - 1)]
    here[-1], _ = lax.optimization_barrier((here[-1], later))
    last = lowered(here[-1], layer, group)
    here_near = jnp.concatenate(here, axis=0)
    here_far = swap(here_near, 1)
    here_rows = jnp.concatenate([here_near, here_far], axis=0)
    after_most, _ = lax.optimization_barrier((jnp.concatenate(after, axis=0), here_far))
    after_rows = jnp.concatenate([after_most, last, swap(after_most, 1), swap(last, 1)], axis=0)
    grad = grad_all(place, after_rows, dec, grad_own(here_rows, dec), tokens)
    return (error[None], grad)


def solution(mesh):
    return jax.shard_map(
        on_device,
        mesh=mesh,
        in_specs=(
            P("layer", "groups", None),
            P("layer", None, None),
            P("layer", None),
            P("layer", "groups", None),
            P("layer", None, None, None),
            P("layer", "groups", None),
        ),
        out_specs=(P("layer", "groups", None), P("layer", "groups", None)),
        check_vma=False,
    )
```

```python
import functools

import jax
import jax.numpy as jnp
from jax import lax
from jax.experimental import pallas as pl
from jax.experimental.pallas import tpu as pltpu
from jax.sharding import PartitionSpec as P

BLOCK = 128
LAYERS = 4
TILE = 32
CORES = 2
CHUNK = 1024
LIMIT = 4 << 20
AXIS = "layer"

ANY_SPEC = pl.BlockSpec(memory_space=pl.ANY)
VMEM_SPEC = pl.BlockSpec(memory_space=pltpu.VMEM)
SMEM_SPEC = pl.BlockSpec(memory_space=pltpu.SMEM)


def turned(chip, chips):
    bits = chips.bit_length() - 1
    return sum(((chip >> bit) & 1) << (bits - 1 - bit) for bit in range(bits))


def across(value, chip, chips):
    masks = (CORES * chip, CORES * turned(chip, chips))
    pairs = [(i, i ^ masks[i % CORES]) for i in range(lax.axis_size(AXIS))]
    return lax.ppermute(value, AXIS, pairs)


def other_core(value):
    return lax.ppermute(value, AXIS, [(i, i ^ 1) for i in range(lax.axis_size(AXIS))])


def raised(value, layer, group):
    size = lax.axis_size(AXIS)
    came = lax.ppermute(value, AXIS, [(i, (i + group) % size) for i in range(size)])
    return jnp.where(layer == 0, jnp.zeros_like(came), came)


def lowered(value, layer, group):
    size = lax.axis_size(AXIS)
    came = lax.ppermute(value, AXIS, [((i + group) % size, i) for i in range(size)])
    return jnp.where(layer == LAYERS - 1, jnp.zeros_like(came), came)


def after(values, done):
    return lax.optimization_barrier((values, done))[0]


def slab_of(place, block, chips):
    far, chip = block // chips, block % chips
    odd = (place & 1) ^ far
    return place ^ (far + CORES * (chip * (1 - odd) + turned(chip, chips) * odd))


def in_vmem(*arrays):
    return [pltpu.with_memory_space_constraint(a, pltpu.VMEM) for a in arrays]


def in_hbm(*arrays):
    return [pltpu.with_memory_space_constraint(a, pltpu.HBM) for a in arrays]


def kernel_params(limit=LIMIT):
    return pltpu.CompilerParams(vmem_limit_bytes=limit)


def load_kernel(enc_hbm, dec_hbm, enc_ref, dec_ref, sems):
    copies = [
        pltpu.make_async_copy(enc_hbm, enc_ref, sems.at[0]),
        pltpu.make_async_copy(dec_hbm.at[0, 1], dec_ref, sems.at[1]),
    ]
    for copy in copies:
        copy.start()
    for copy in copies:
        copy.wait()


def loaded(enc, dec):
    return pl.pallas_call(
        load_kernel,
        out_shape=[pltpu.VMEM(enc.shape, enc.dtype), pltpu.VMEM(dec.shape[2:], dec.dtype)],
        in_specs=[ANY_SPEC] * 2,
        out_specs=[VMEM_SPEC] * 2,
        scratch_shapes=[pltpu.SemaphoreType.DMA((2,))],
        compiler_params=kernel_params(1 << 20),
        cost_estimate=pl.CostEstimate(flops=0, bytes_accessed=4 * (enc.size + dec.size), transcendentals=0),
        name="load_weights",
    )(*in_hbm(enc, dec))


def fetches(dec_hbm, reach, held, sems):
    return [
        pltpu.make_async_copy(
            dec_hbm.at[0, reach, :, pl.ds(step * CHUNK, CHUNK)], held.at[:, pl.ds(step * CHUNK, CHUNK)], sems.at[step]
        )
        for step in range(held.shape[1] // CHUNK)
    ]


def decode(codes, dec_ref, near_ref, far_ref, copies=None):
    half, width = near_ref.shape
    for step in range(width // CHUNK):
        if copies is not None:
            copies[step].wait()
        columns = pl.ds(step * CHUNK, CHUNK)
        part = jnp.dot(codes, dec_ref[:, columns], preferred_element_type=jnp.float32)
        near_ref[:, columns] = part[:half]
        far_ref[:, columns] = part[half:].astype(jnp.bfloat16)


def encode_kernel(tokens, place_ref, active_ref, x_ref, enc_ref, bias_ref, dec_ref, codes_ref, near_ref, far_ref, held):
    rows, depth = x_ref.shape
    group = rows // tokens
    half = depth // 2
    pre = bias_ref[...].astype(jnp.float32) + sum(
        jnp.dot(x_ref[:, part], enc_ref[0, part, :], preferred_element_type=jnp.float32)
        for part in (pl.ds(0, half), pl.ds(half, half))
    )
    held[...] = jnp.maximum(pre, 0.0)
    for block in range(group):
        tile = (slab_of(place_ref[0], block, group // CORES) * tokens) // TILE
        for part in range(active_ref.shape[1]):
            where = (pl.ds(block * tokens, tokens), pl.ds(part * BLOCK, BLOCK))
            held[where] = held[where] * active_ref[tile, part].astype(jnp.float32)
    codes_ref[...] = held[...].astype(jnp.bfloat16)
    decode(codes_ref[...], dec_ref, near_ref, far_ref)


def decode_kernel(codes_ref, dec_hbm, near_ref, far_ref, held, sems):
    copies = fetches(dec_hbm, 0, held, sems)
    for copy in copies:
        copy.start()
    decode(codes_ref[...], held, near_ref, far_ref, copies)


def halves_of(rows, width):
    return [pltpu.VMEM((rows // CORES, width), jnp.float32), pltpu.VMEM((rows // CORES, width), jnp.bfloat16)]


def encoded(place, active, x, enc, bias, dec, tokens):
    rows, depth = x.shape
    features = enc.shape[2]
    return pl.pallas_call(
        functools.partial(encode_kernel, tokens),
        out_shape=[pltpu.VMEM((rows, features), jnp.bfloat16)] + halves_of(rows, depth),
        in_specs=[SMEM_SPEC, SMEM_SPEC] + [VMEM_SPEC] * 4,
        out_specs=[VMEM_SPEC] * 3,
        scratch_shapes=[pltpu.VMEM((rows, features), jnp.float32)],
        compiler_params=kernel_params(),
        cost_estimate=pl.CostEstimate(flops=4 * rows * depth * features, bytes_accessed=4 * depth * features, transcendentals=0),
        name="encode",
    )(place, active, *in_vmem(x, enc, bias, dec))


def decoded(codes, dec):
    rows, features = codes.shape
    width = dec.shape[3]
    return pl.pallas_call(
        decode_kernel,
        out_shape=halves_of(rows, width),
        in_specs=[VMEM_SPEC, ANY_SPEC],
        out_specs=[VMEM_SPEC] * 2,
        scratch_shapes=[pltpu.VMEM((features, width), dec.dtype), pltpu.SemaphoreType.DMA((width // CHUNK,))],
        compiler_params=kernel_params(2 * LIMIT),
        cost_estimate=pl.CostEstimate(flops=2 * rows * width * features, bytes_accessed=2 * width * features, transcendentals=0),
        name="decode_own",
    )(*in_vmem(codes), *in_hbm(dec))


def back(rows_ref, dec_ref, copies=None):
    sums = [None, None]
    steps = rows_ref.shape[1] // CHUNK
    for step in range(steps):
        if copies is not None:
            copies[step].wait()
        columns = pl.ds(step * CHUNK, CHUNK)
        part = lax.dot_general(
            rows_ref[:, columns], dec_ref[:, columns], (((1,), (1,)), ((), ())), preferred_element_type=jnp.float32
        )
        which = step * len(sums) // steps
        sums[which] = part if sums[which] is None else sums[which] + part
    return sums[0] + sums[1]


def grad_own_kernel(rows_ref, dec_hbm, out_ref, next_ref, held, sems, next_sem):
    copies = fetches(dec_hbm, 0, held, sems)
    load_next = pltpu.make_async_copy(dec_hbm.at[0, 1], next_ref, next_sem)
    for copy in copies:
        copy.start()
    load_next.start()
    out_ref[...] = back(rows_ref, held, copies)
    load_next.wait()


def grad_all_kernel(tokens, place_ref, rows_ref, dec_ref, own_ref, out_ref):
    total = own_ref[...] + back(rows_ref, dec_ref)
    group = total.shape[0] // tokens
    for block in range(group):
        slab = slab_of(place_ref[0], block, group // CORES)
        where = pl.ds(pl.multiple_of(slab * tokens, tokens), tokens)
        out_ref[0, where, :] = total[block * tokens : (block + 1) * tokens]


def grad_own(rows, dec):
    _, _, features, width = dec.shape
    return pl.pallas_call(
        grad_own_kernel,
        out_shape=[pltpu.VMEM((rows.shape[0], features), jnp.float32), pltpu.VMEM((features, width), dec.dtype)],
        in_specs=[VMEM_SPEC, ANY_SPEC],
        out_specs=[VMEM_SPEC] * 2,
        scratch_shapes=[
            pltpu.VMEM((features, width), dec.dtype),
            pltpu.SemaphoreType.DMA((width // CHUNK,)),
            pltpu.SemaphoreType.DMA(()),
        ],
        compiler_params=kernel_params(2 * LIMIT),
        cost_estimate=pl.CostEstimate(flops=2 * rows.size * features, bytes_accessed=2 * dec.size, transcendentals=0),
        name="grad_own",
    )(*in_vmem(rows), *in_hbm(dec))


def grad_all(place, rows, dec, own, tokens):
    return pl.pallas_call(
        functools.partial(grad_all_kernel, tokens),
        out_shape=jax.ShapeDtypeStruct((1,) + own.shape, jnp.float32),
        in_specs=[SMEM_SPEC] + [VMEM_SPEC] * 3,
        out_specs=VMEM_SPEC,
        compiler_params=kernel_params(),
        cost_estimate=pl.CostEstimate(flops=2 * rows.size * own.shape[1], bytes_accessed=2 * dec.size, transcendentals=0),
        name="grad_all",
    )(place, *in_vmem(rows, dec, own))


def blocks_of(near, far, chips):
    rows = near.shape[0] // chips
    total = near + other_core(far).astype(jnp.float32)
    return [total[chip * rows : (chip + 1) * rows] for chip in range(chips)]


def summed(blocks, sent):
    total = blocks[0]
    for came in [across(blocks[chip].astype(jnp.bfloat16), chip, len(blocks)) for chip in sent]:
        total = total + came.astype(jnp.float32)
    return total


def on_device(resid, enc_weight, enc_bias, active, dec_weight, target):
    group = lax.axis_size(AXIS) // LAYERS
    chips = group // CORES
    index = lax.axis_index(AXIS)
    layer = index // group
    place = (index % group).astype(jnp.int32).reshape(1)
    tokens = resid.shape[1]
    enc, next_dec = loaded(enc_weight, dec_weight)
    near = [resid[0]] + [across(resid[0], chip, chips) for chip in range(1, chips)]
    x = jnp.concatenate(near + [other_core(piece) for piece in near], axis=0)
    codes, next_near, next_far = encoded(place, active[0], x, enc, enc_bias, next_dec, tokens)
    own_near, own_far = decoded(codes, dec_weight)

    nexts = blocks_of(next_near, next_far, chips)
    owns = blocks_of(own_near, own_far, chips)
    risen = raised(nexts[-1].astype(jnp.bfloat16), layer, group)
    next_sum = summed(nexts, range(1, chips - 1)).astype(jnp.bfloat16)
    owns[-1] = owns[-1] + risen.astype(jnp.float32)
    from_before = raised(next_sum, layer, group).astype(jnp.float32)
    own_sum = summed(owns, range(1, chips))
    error = (own_sum + from_before - target[0].astype(jnp.float32)).astype(jnp.bfloat16)

    later = lowered(error, layer, group)
    heres = [error] + [across(error, chip, chips) for chip in range(1, chips)]
    afters = [later] + [across(later, chip, chips) for chip in range(1, chips - 1)]
    last = lowered(after(heres[-1], later), layer, group)
    here_near = jnp.concatenate(heres, axis=0)
    here_far = other_core(here_near)
    here_rows = jnp.concatenate([here_near, here_far], axis=0)
    most = after(jnp.concatenate(afters, axis=0), here_far)
    after_rows = jnp.concatenate([most, last, other_core(most), other_core(last)], axis=0)
    own_grad, next_dec = grad_own(here_rows, dec_weight)
    grad = grad_all(place, after_rows, next_dec, own_grad, tokens)
    return (error[None], grad)


def solution(mesh):
    return jax.shard_map(
        on_device,
        mesh=mesh,
        in_specs=(
            P("layer", "groups", None),
            P("layer", None, None),
            P("layer", None),
            P("layer", "groups", None),
            P("layer", None, None, None),
            P("layer", "groups", None),
        ),
        out_specs=(P("layer", "groups", None), P("layer", "groups", None)),
        check_vma=False,
    )
```

```python
import functools

import jax
import jax.numpy as jnp
from jax import lax
from jax.experimental import pallas as pl
from jax.experimental.pallas import tpu as pltpu
from jax.sharding import PartitionSpec as P

BLOCK = 128
LAYERS = 4
TILE = 32
CORES = 2
CHUNK = 1024
LIMIT = 4 << 20
AXIS = "layer"

ANY_SPEC = pl.BlockSpec(memory_space=pl.ANY)
VMEM_SPEC = pl.BlockSpec(memory_space=pltpu.VMEM)
SMEM_SPEC = pl.BlockSpec(memory_space=pltpu.SMEM)


def turned(chip, chips):
    bits = chips.bit_length() - 1
    return sum(((chip >> bit) & 1) << (bits - 1 - bit) for bit in range(bits))


def across(value, chip, chips):
    masks = (CORES * chip, CORES * turned(chip, chips))
    pairs = [(i, i ^ masks[i % CORES]) for i in range(lax.axis_size(AXIS))]
    return lax.ppermute(value, AXIS, pairs)


def other_core(value):
    return lax.ppermute(value, AXIS, [(i, i ^ 1) for i in range(lax.axis_size(AXIS))])


def raised(value, layer, group):
    size = lax.axis_size(AXIS)
    came = lax.ppermute(value, AXIS, [(i, (i + group) % size) for i in range(size)])
    return jnp.where(layer == 0, jnp.zeros_like(came), came)


def lowered(value, layer, group):
    size = lax.axis_size(AXIS)
    came = lax.ppermute(value, AXIS, [((i + group) % size, i) for i in range(size)])
    return jnp.where(layer == LAYERS - 1, jnp.zeros_like(came), came)


def after(values, done):
    return lax.optimization_barrier((values, done))[0]


def slab_of(place, block, chips):
    far, chip = block // chips, block % chips
    odd = (place & 1) ^ far
    return place ^ (far + CORES * (chip * (1 - odd) + turned(chip, chips) * odd))


def in_vmem(*arrays):
    return [pltpu.with_memory_space_constraint(a, pltpu.VMEM) for a in arrays]


def in_hbm(*arrays):
    return [pltpu.with_memory_space_constraint(a, pltpu.HBM) for a in arrays]


def kernel_params(limit=LIMIT):
    return pltpu.CompilerParams(vmem_limit_bytes=limit)


def load_kernel(tokens, place_ref, active_ref, enc_hbm, dec_hbm, gate_ref, enc_ref, next_ref, own_ref, sems):
    pieces = [(enc_hbm.at[0], enc_ref), (dec_hbm.at[0, 1], next_ref), (dec_hbm.at[0, 0], own_ref)]
    copies = [pltpu.make_async_copy(source, target, sems.at[i]) for i, (source, target) in enumerate(pieces)]
    for copy in copies:
        copy.start()
    group = gate_ref.shape[0] // tokens
    for block in range(group):
        tile = (slab_of(place_ref[0], block, group // CORES) * tokens) // TILE
        for part in range(active_ref.shape[1]):
            live = active_ref[tile, part].astype(jnp.float32)
            gate_ref[pl.ds(block * tokens, tokens), pl.ds(part * BLOCK, BLOCK)] = jnp.full((tokens, BLOCK), live)
    for copy in copies:
        copy.wait()


def loaded(place, active, enc, dec, rows, tokens):
    _, depth, features = enc.shape
    block = pltpu.VMEM(dec.shape[2:], dec.dtype)
    return pl.pallas_call(
        functools.partial(load_kernel, tokens),
        out_shape=[pltpu.VMEM((rows, features), jnp.float32), pltpu.VMEM((depth, features), enc.dtype), block, block],
        in_specs=[SMEM_SPEC] * 2 + [ANY_SPEC] * 2,
        out_specs=[VMEM_SPEC] * 4,
        scratch_shapes=[pltpu.SemaphoreType.DMA((3,))],
        compiler_params=kernel_params(1 << 20),
        cost_estimate=pl.CostEstimate(flops=0, bytes_accessed=4 * (enc.size + dec.size), transcendentals=0),
        name="load_weights",
    )(place, active, *in_hbm(enc, dec))


def reload_kernel(dec_hbm, done_hbm, own_ref, next_ref, sems):
    del done_hbm
    pieces = [(dec_hbm.at[0, 0], own_ref), (dec_hbm.at[0, 1], next_ref)]
    copies = [pltpu.make_async_copy(source, target, sems.at[i]) for i, (source, target) in enumerate(pieces)]
    for copy in copies:
        copy.start()
    for copy in copies:
        copy.wait()


def reloaded(dec, done):
    return pl.pallas_call(
        reload_kernel,
        out_shape=[pltpu.VMEM(dec.shape[2:], dec.dtype)] * 2,
        in_specs=[ANY_SPEC] * 2,
        out_specs=[VMEM_SPEC] * 2,
        scratch_shapes=[pltpu.SemaphoreType.DMA((2,))],
        compiler_params=kernel_params(1 << 20),
        cost_estimate=pl.CostEstimate(flops=0, bytes_accessed=4 * dec.size, transcendentals=0),
        name="reload_decoder",
    )(*in_hbm(dec), done)


def decode_kernel(codes_ref, dec_ref, near_ref, far_ref):
    half, width = near_ref.shape
    for step in range(width // CHUNK):
        columns = pl.ds(step * CHUNK, CHUNK)
        part = jnp.dot(codes_ref[...], dec_ref[:, columns], preferred_element_type=jnp.float32)
        near_ref[:, columns] = part[:half]
        far_ref[:, columns] = part[half:].astype(jnp.bfloat16)


def decoded(codes, dec):
    rows, features = codes.shape
    width = dec.shape[1]
    half = (rows // CORES, width)
    return pl.pallas_call(
        decode_kernel,
        out_shape=[pltpu.VMEM(half, jnp.float32), pltpu.VMEM(half, jnp.bfloat16)],
        in_specs=[VMEM_SPEC] * 2,
        out_specs=[VMEM_SPEC] * 2,
        compiler_params=kernel_params(),
        cost_estimate=pl.CostEstimate(flops=2 * rows * width * features, bytes_accessed=2 * width * features, transcendentals=0),
        name="decode",
    )(*in_vmem(codes, dec))


def back(rows_ref, dec_ref):
    half = rows_ref.shape[1] // 2
    return sum(
        lax.dot_general(
            rows_ref[:, part], dec_ref[:, part], (((1,), (1,)), ((), ())), preferred_element_type=jnp.float32
        )
        for part in (pl.ds(0, half), pl.ds(half, half))
    )


def grad_own_kernel(rows_ref, dec_ref, out_ref, _):
    out_ref[...] = back(rows_ref, dec_ref)


def grad_all_kernel(tokens, place_ref, rows_ref, dec_ref, own_ref, out_ref):
    total = own_ref[...] + back(rows_ref, dec_ref)
    group = total.shape[0] // tokens
    for block in range(group):
        slab = slab_of(place_ref[0], block, group // CORES)
        where = pl.ds(pl.multiple_of(slab * tokens, tokens), tokens)
        out_ref[0, where, :] = total[block * tokens : (block + 1) * tokens]


def grad_own(rows, dec):
    features = dec.shape[0]
    return pl.pallas_call(
        grad_own_kernel,
        out_shape=[pltpu.VMEM((rows.shape[0], features), jnp.float32), pltpu.VMEM((8, 128), jnp.float32)],
        in_specs=[VMEM_SPEC] * 2,
        out_specs=[VMEM_SPEC] * 2,
        compiler_params=kernel_params(),
        cost_estimate=pl.CostEstimate(flops=2 * rows.size * features, bytes_accessed=2 * dec.size, transcendentals=0),
        name="grad_own",
    )(*in_vmem(rows, dec))[0]


def grad_all(place, rows, dec, own, tokens):
    return pl.pallas_call(
        functools.partial(grad_all_kernel, tokens),
        out_shape=jax.ShapeDtypeStruct((1,) + own.shape, jnp.float32),
        in_specs=[SMEM_SPEC] + [VMEM_SPEC] * 3,
        out_specs=VMEM_SPEC,
        compiler_params=kernel_params(),
        cost_estimate=pl.CostEstimate(flops=2 * rows.size * own.shape[1], bytes_accessed=2 * dec.size, transcendentals=0),
        name="grad_all",
    )(place, *in_vmem(rows, dec, own))


def blocks_of(near, far, chips):
    rows = near.shape[0] // chips
    total = near + other_core(far).astype(jnp.float32)
    return [total[chip * rows : (chip + 1) * rows] for chip in range(chips)]


def summed(blocks, sent):
    total = blocks[0]
    for came in [across(blocks[chip].astype(jnp.bfloat16), chip, len(blocks)) for chip in sent]:
        total = total + came.astype(jnp.float32)
    return total


def on_device(resid, enc_weight, enc_bias, active, dec_weight, target):
    group = lax.axis_size(AXIS) // LAYERS
    chips = group // CORES
    index = lax.axis_index(AXIS)
    layer = index // group
    place = (index % group).astype(jnp.int32).reshape(1)
    tokens = resid.shape[1]
    gate, enc, next_dec, own_dec = loaded(place, active[0], enc_weight, dec_weight, group * tokens, tokens)
    slab = resid[0]
    most, last = [across(slab, chip, chips) for chip in range(1, chips - 1)], across(slab, chips - 1, chips)
    early, late = jnp.concatenate([slab, last], axis=0), jnp.concatenate(most, axis=0)
    early_far, late_far = other_core(early), other_core(late)
    x = jnp.concatenate(
        [slab, late, last, early_far[:tokens], late_far, early_far[tokens:]], axis=0
    )
    pre = jnp.dot(x, enc, preferred_element_type=jnp.float32) + enc_bias.astype(jnp.float32)
    codes = (jax.nn.relu(pre) * gate).astype(jnp.bfloat16)
    next_near, next_far = decoded(codes, next_dec)
    own_near, own_far = decoded(codes, own_dec)

    nexts = blocks_of(next_near, next_far, chips)
    owns = blocks_of(own_near, own_far, chips)
    risen = raised(nexts[-1].astype(jnp.bfloat16), layer, group)
    owns[-1] = owns[-1] + risen.astype(jnp.float32)
    next_sum = after(summed(nexts, range(1, chips - 1)).astype(jnp.bfloat16), owns[-1])
    from_before = raised(next_sum, layer, group).astype(jnp.float32)
    crossed = across(owns[-1].astype(jnp.bfloat16), chips - 1, chips)
    own_sum = summed(owns, range(1, chips - 1))
    own_dec, next_dec = reloaded(dec_weight, own_sum)
    own_sum = after(own_sum, own_dec) + crossed.astype(jnp.float32)
    error = (own_sum + from_before - target[0].astype(jnp.float32)).astype(jnp.bfloat16)

    later = lowered(error, layer, group)
    heres = [error] + [across(error, chip, chips) for chip in range(1, chips)]
    afters = [later] + [across(later, chip, chips) for chip in range(1, chips - 1)]
    last = lowered(after(heres[-1], later), layer, group)
    here_near = jnp.concatenate(heres, axis=0)
    here_far = other_core(here_near)
    here_rows = jnp.concatenate([here_near, here_far], axis=0)
    most = after(jnp.concatenate(afters, axis=0), here_far)
    after_rows = jnp.concatenate([most, last, other_core(most), other_core(last)], axis=0)
    grad = grad_all(place, after_rows, next_dec, grad_own(here_rows, own_dec), tokens)
    return (error[None], grad)


def solution(mesh):
    return jax.shard_map(
        on_device,
        mesh=mesh,
        in_specs=(
            P("layer", "groups", None),
            P("layer", None, None),
            P("layer", None),
            P("layer", "groups", None),
            P("layer", None, None, None),
            P("layer", "groups", None),
        ),
        out_specs=(P("layer", "groups", None), P("layer", "groups", None)),
        check_vma=False,
    )
```

```python
import functools

import jax
import jax.numpy as jnp
from jax import lax
from jax.experimental import pallas as pl
from jax.experimental.pallas import tpu as pltpu
from jax.sharding import PartitionSpec as P

BLOCK = 128
LAYERS = 4
TILE = 32
CORES = 2
CHUNK = 1024
LIMIT = 4 << 20
HIGH = 28 << 20
AXIS = "layer"

ANY_SPEC = pl.BlockSpec(memory_space=pl.ANY)
VMEM_SPEC = pl.BlockSpec(memory_space=pltpu.VMEM)
SMEM_SPEC = pl.BlockSpec(memory_space=pltpu.SMEM)


def turned(chip, chips):
    bits = chips.bit_length() - 1
    return sum(((chip >> bit) & 1) << (bits - 1 - bit) for bit in range(bits))


def across(value, chip, chips):
    masks = (CORES * chip, CORES * turned(chip, chips))
    pairs = [(i, i ^ masks[i % CORES]) for i in range(lax.axis_size(AXIS))]
    return lax.ppermute(value, AXIS, pairs)


def other_core(value):
    return lax.ppermute(value, AXIS, [(i, i ^ 1) for i in range(lax.axis_size(AXIS))])


def raised(value, layer, group):
    size = lax.axis_size(AXIS)
    came = lax.ppermute(value, AXIS, [(i, (i + group) % size) for i in range(size)])
    return jnp.where(layer == 0, jnp.zeros_like(came), came)


def lowered(value, layer, group):
    size = lax.axis_size(AXIS)
    came = lax.ppermute(value, AXIS, [((i + group) % size, i) for i in range(size)])
    return jnp.where(layer == LAYERS - 1, jnp.zeros_like(came), came)


def after(values, done):
    return lax.optimization_barrier((values, done))[0]


def slab_of(place, block, chips):
    far, chip = block // chips, block % chips
    odd = (place & 1) ^ far
    return place ^ (far + CORES * (chip * (1 - odd) + turned(chip, chips) * odd))


def in_vmem(*arrays):
    return [pltpu.with_memory_space_constraint(a, pltpu.VMEM) for a in arrays]


def in_hbm(*arrays):
    return [pltpu.with_memory_space_constraint(a, pltpu.HBM) for a in arrays]


def kernel_params(limit=LIMIT):
    return pltpu.CompilerParams(vmem_limit_bytes=limit)


def load_kernel(enc_hbm, dec_hbm, enc_ref, own_ref, next_ref, sems):
    pieces = [(enc_hbm.at[0], enc_ref), (dec_hbm.at[0, 1], next_ref), (dec_hbm.at[0, 0], own_ref)]
    copies = [pltpu.make_async_copy(source, target, sems.at[i]) for i, (source, target) in enumerate(pieces)]
    for copy in copies:
        copy.start()
    for copy in copies:
        copy.wait()


def loaded(enc, dec):
    block = pltpu.VMEM(dec.shape[2:], dec.dtype)
    return pl.pallas_call(
        load_kernel,
        out_shape=[pltpu.VMEM(enc.shape[1:], enc.dtype), block, block],
        in_specs=[ANY_SPEC] * 2,
        out_specs=[VMEM_SPEC] * 3,
        scratch_shapes=[pltpu.SemaphoreType.DMA((3,))],
        compiler_params=kernel_params(HIGH),
        cost_estimate=pl.CostEstimate(flops=0, bytes_accessed=4 * (enc.size + dec.size), transcendentals=0),
        name="load_weights",
    )(*in_hbm(enc, dec))


def decode(codes, dec_ref, near_ref, far_ref):
    half, width = near_ref.shape
    for step in range(width // CHUNK):
        columns = pl.ds(step * CHUNK, CHUNK)
        part = jnp.dot(codes, dec_ref[:, columns], preferred_element_type=jnp.float32)
        near_ref[:, columns] = part[:half]
        far_ref[:, columns] = part[half:].astype(jnp.bfloat16)


def gate_of(place, active_ref, rows, tokens):
    group = rows // tokens
    block = lax.broadcasted_iota(jnp.int32, (rows, BLOCK), 0) // tokens
    tile = (slab_of(place, block, group // CORES) * tokens) // TILE
    parts = []
    for part in range(active_ref.shape[1]):
        live = jnp.zeros((rows, BLOCK), jnp.int32)
        for i in range(active_ref.shape[0]):
            live = jnp.where(tile == i, active_ref[i, part], live)
        parts.append(live.astype(jnp.float32))
    return jnp.concatenate(parts, axis=1)


def encode_kernel(tokens, place_ref, active_ref, x_ref, enc_ref, bias_ref, dec_ref, codes_ref, near_ref, far_ref):
    rows, depth = x_ref.shape
    half = depth // 2
    pre = bias_ref[...].astype(jnp.float32) + sum(
        jnp.dot(x_ref[:, part], enc_ref[part, :], preferred_element_type=jnp.float32)
        for part in (pl.ds(0, half), pl.ds(half, half))
    )
    codes = jnp.maximum(pre, 0.0) * gate_of(place_ref[0], active_ref, rows, tokens)
    codes_ref[...] = codes.astype(jnp.bfloat16)
    decode(codes_ref[...], dec_ref, near_ref, far_ref)


def decode_kernel(codes_ref, dec_ref, near_ref, far_ref):
    decode(codes_ref[...], dec_ref, near_ref, far_ref)


def halves_of(rows, width):
    return [pltpu.VMEM((rows // CORES, width), jnp.float32), pltpu.VMEM((rows // CORES, width), jnp.bfloat16)]


def encoded(place, active, x, enc, bias, dec, tokens):
    rows, depth = x.shape
    features = enc.shape[1]
    return pl.pallas_call(
        functools.partial(encode_kernel, tokens),
        out_shape=[pltpu.VMEM((rows, features), jnp.bfloat16)] + halves_of(rows, depth),
        in_specs=[SMEM_SPEC, SMEM_SPEC] + [VMEM_SPEC] * 4,
        out_specs=[VMEM_SPEC] * 3,
        compiler_params=kernel_params(),
        cost_estimate=pl.CostEstimate(flops=4 * rows * depth * features, bytes_accessed=4 * depth * features, transcendentals=0),
        name="encode",
    )(place, active, *in_vmem(x, enc, bias, dec))


def decoded(codes, dec):
    rows, features = codes.shape
    width = dec.shape[1]
    return pl.pallas_call(
        decode_kernel,
        out_shape=halves_of(rows, width),
        in_specs=[VMEM_SPEC] * 2,
        out_specs=[VMEM_SPEC] * 2,
        compiler_params=kernel_params(),
        cost_estimate=pl.CostEstimate(flops=2 * rows * width * features, bytes_accessed=2 * width * features, transcendentals=0),
        name="decode_own",
    )(*in_vmem(codes, dec))


def back(rows_ref, dec_ref):
    half = rows_ref.shape[1] // 2
    return sum(
        lax.dot_general(
            rows_ref[:, part], dec_ref[:, part], (((1,), (1,)), ((), ())), preferred_element_type=jnp.float32
        )
        for part in (pl.ds(0, half), pl.ds(half, half))
    )


def grad_own_kernel(rows_ref, dec_ref, out_ref, _):
    out_ref[...] = back(rows_ref, dec_ref)


def grad_all_kernel(tokens, place_ref, rows_ref, dec_ref, own_ref, out_ref):
    total = own_ref[...] + back(rows_ref, dec_ref)
    group = total.shape[0] // tokens
    for block in range(group):
        slab = slab_of(place_ref[0], block, group // CORES)
        where = pl.ds(pl.multiple_of(slab * tokens, tokens), tokens)
        out_ref[0, where, :] = total[block * tokens : (block + 1) * tokens]


def grad_own(rows, dec):
    features = dec.shape[0]
    return pl.pallas_call(
        grad_own_kernel,
        out_shape=[pltpu.VMEM((rows.shape[0], features), jnp.float32), pltpu.VMEM((8, 128), jnp.float32)],
        in_specs=[VMEM_SPEC] * 2,
        out_specs=[VMEM_SPEC] * 2,
        compiler_params=kernel_params(),
        cost_estimate=pl.CostEstimate(flops=2 * rows.size * features, bytes_accessed=2 * dec.size, transcendentals=0),
        name="grad_own",
    )(*in_vmem(rows, dec))[0]


def grad_all(place, rows, dec, own, tokens):
    return pl.pallas_call(
        functools.partial(grad_all_kernel, tokens),
        out_shape=jax.ShapeDtypeStruct((1,) + own.shape, jnp.float32),
        in_specs=[SMEM_SPEC] + [VMEM_SPEC] * 3,
        out_specs=VMEM_SPEC,
        compiler_params=kernel_params(),
        cost_estimate=pl.CostEstimate(flops=2 * rows.size * own.shape[1], bytes_accessed=2 * dec.size, transcendentals=0),
        name="grad_all",
    )(place, *in_vmem(rows, dec, own))


def blocks_of(near, far, chips):
    rows = near.shape[0] // chips
    total = near + other_core(far).astype(jnp.float32)
    return [total[chip * rows : (chip + 1) * rows] for chip in range(chips)]


def summed(blocks, sent):
    total = blocks[0]
    for came in [across(blocks[chip].astype(jnp.bfloat16), chip, len(blocks)) for chip in sent]:
        total = total + came.astype(jnp.float32)
    return total


def on_device(resid, enc_weight, enc_bias, active, dec_weight, target):
    group = lax.axis_size(AXIS) // LAYERS
    chips = group // CORES
    index = lax.axis_index(AXIS)
    layer = index // group
    place = (index % group).astype(jnp.int32).reshape(1)
    tokens = resid.shape[1]
    enc, own_dec, next_dec = loaded(enc_weight, dec_weight)
    slab = resid[0]
    most, last = [across(slab, chip, chips) for chip in range(1, chips - 1)], across(slab, chips - 1, chips)
    early, late = jnp.concatenate([slab, last], axis=0), jnp.concatenate(most, axis=0)
    early_far, late_far = other_core(early), other_core(late)
    x = jnp.concatenate(
        [slab, late, last, early_far[:tokens], late_far, early_far[tokens:]], axis=0
    )
    codes, next_near, next_far = encoded(place, active[0], x, enc, enc_bias, next_dec, tokens)
    own_near, own_far = decoded(codes, own_dec)

    nexts = blocks_of(next_near, next_far, chips)
    owns = blocks_of(own_near, own_far, chips)
    risen = raised(nexts[-1].astype(jnp.bfloat16), layer, group)
    owns[-1] = owns[-1] + risen.astype(jnp.float32)
    next_sum = after(summed(nexts, range(1, chips - 1)).astype(jnp.bfloat16), owns[-1])
    from_before = raised(next_sum, layer, group).astype(jnp.float32)
    own_sum = summed(owns, range(1, chips))
    error = (own_sum + from_before - target[0].astype(jnp.float32)).astype(jnp.bfloat16)

    later = lowered(error, layer, group)
    heres = [error] + [across(error, chip, chips) for chip in range(1, chips)]
    afters = [later] + [across(later, chip, chips) for chip in range(1, chips - 1)]
    last = lowered(after(heres[-1], later), layer, group)
    here_near = jnp.concatenate(heres, axis=0)
    here_far = other_core(here_near)
    here_rows = jnp.concatenate([here_near, here_far], axis=0)
    most = after(jnp.concatenate(afters, axis=0), here_far)
    after_rows = jnp.concatenate([most, last, other_core(most), other_core(last)], axis=0)
    grad = grad_all(place, after_rows, next_dec, grad_own(here_rows, own_dec), tokens)
    return (error[None], grad)


def solution(mesh):
    return jax.shard_map(
        on_device,
        mesh=mesh,
        in_specs=(
            P("layer", "groups", None),
            P("layer", None, None),
            P("layer", None),
            P("layer", "groups", None),
            P("layer", None, None, None),
            P("layer", "groups", None),
        ),
        out_specs=(P("layer", "groups", None), P("layer", "groups", None)),
        check_vma=False,
    )
```

```python
import functools

import jax
import jax.numpy as jnp
from jax import lax
from jax.experimental import pallas as pl
from jax.experimental.pallas import tpu as pltpu
from jax.sharding import PartitionSpec as P

BLOCK = 128
LAYERS = 4
TILE = 32
CORES = 2
CHUNK = 1024
LIMIT = 4 << 20
AXIS = "layer"

ANY_SPEC = pl.BlockSpec(memory_space=pl.ANY)
VMEM_SPEC = pl.BlockSpec(memory_space=pltpu.VMEM)


def turned(chip, chips):
    bits = chips.bit_length() - 1
    return sum(((chip >> bit) & 1) << (bits - 1 - bit) for bit in range(bits))


def across(value, chip, chips):
    masks = (CORES * chip, CORES * turned(chip, chips))
    pairs = [(i, i ^ masks[i % CORES]) for i in range(lax.axis_size(AXIS))]
    return lax.ppermute(value, AXIS, pairs)


def other_core(value):
    return lax.ppermute(value, AXIS, [(i, i ^ 1) for i in range(lax.axis_size(AXIS))])


def raised(value, first, group):
    size = lax.axis_size(AXIS)
    came = lax.ppermute(value, AXIS, [(i, (i + group) % size) for i in range(size)])
    return jnp.where(first, jnp.zeros_like(came), came)


def lowered(value, final, group):
    size = lax.axis_size(AXIS)
    came = lax.ppermute(value, AXIS, [((i + group) % size, i) for i in range(size)])
    return jnp.where(final, jnp.zeros_like(came), came)


def after(values, done):
    return lax.optimization_barrier((values, done))[0]


def slab_of(place, block, chips):
    far, chip = block // chips, block % chips
    odd = (place & 1) ^ far
    return place ^ (far + CORES * (chip * (1 - odd) + turned(chip, chips) * odd))


def in_vmem(*arrays):
    return [pltpu.with_memory_space_constraint(a, pltpu.VMEM) for a in arrays]


def in_hbm(*arrays):
    return [pltpu.with_memory_space_constraint(a, pltpu.HBM) for a in arrays]


def kernel_params(limit=LIMIT):
    return pltpu.CompilerParams(vmem_limit_bytes=limit)


def load_kernel(enc_hbm, dec_hbm, enc_ref, own_ref, next_ref, sems):
    pieces = [(enc_hbm.at[0], enc_ref), (dec_hbm.at[0, 1], next_ref), (dec_hbm.at[0, 0], own_ref)]
    copies = [pltpu.make_async_copy(source, target, sems.at[i]) for i, (source, target) in enumerate(pieces)]
    for copy in copies:
        copy.start()
    for copy in copies:
        copy.wait()


def loaded(enc, dec):
    block = pltpu.VMEM(dec.shape[2:], dec.dtype)
    return pl.pallas_call(
        load_kernel,
        out_shape=[pltpu.VMEM(enc.shape[1:], enc.dtype), block, block],
        in_specs=[ANY_SPEC] * 2,
        out_specs=[VMEM_SPEC] * 3,
        scratch_shapes=[pltpu.SemaphoreType.DMA((3,))],
        compiler_params=kernel_params(1 << 20),
        cost_estimate=pl.CostEstimate(flops=0, bytes_accessed=4 * (enc.size + dec.size), transcendentals=0),
        name="load_weights",
    )(*in_hbm(enc, dec))


def decode(codes, dec_ref, near_ref, far_ref):
    half, width = near_ref.shape
    for step in range(width // CHUNK):
        columns = pl.ds(step * CHUNK, CHUNK)
        part = jnp.dot(codes, dec_ref[:, columns], preferred_element_type=jnp.float32)
        near_ref[:, columns] = part[:half]
        far_ref[:, columns] = part[half:].astype(jnp.bfloat16)


def place_in(group):
    return lax.axis_index(AXIS) & (group - 1)


def summed_over(depth, product):
    sums = [None, None]
    for step in range(depth // CHUNK):
        part = product(pl.ds(step * CHUNK, CHUNK))
        so_far = sums[step % 2]
        sums[step % 2] = part if so_far is None else so_far + part
    return sums[0] + sums[1]


def gate_of(active_ref, rows, tokens):
    group = rows // tokens
    block = lax.broadcasted_iota(jnp.int32, (rows, BLOCK), 0) // tokens
    tile = (slab_of(place_in(group), block, group // CORES) * tokens) // TILE
    parts = []
    for part in range(active_ref.shape[1]):
        live = jnp.zeros((rows, BLOCK), jnp.int32)
        for i in range(active_ref.shape[0]):
            live = jnp.where(tile == i, active_ref[pl.ds(i, 1), pl.ds(part, 1)], live)
        parts.append(live.astype(jnp.float32))
    return jnp.concatenate(parts, axis=1)


def encode_kernel(tokens, active_ref, x_ref, enc_ref, bias_ref, dec_ref, codes_ref, near_ref, far_ref):
    rows, depth = x_ref.shape
    pre = bias_ref[...].astype(jnp.float32) + summed_over(
        depth, lambda part: jnp.dot(x_ref[:, part], enc_ref[part, :], preferred_element_type=jnp.float32)
    )
    codes = jnp.maximum(pre, 0.0) * gate_of(active_ref, rows, tokens)
    codes_ref[...] = codes.astype(jnp.bfloat16)
    decode(codes_ref[...], dec_ref, near_ref, far_ref)


def decode_kernel(codes_ref, dec_ref, near_ref, far_ref):
    decode(codes_ref[...], dec_ref, near_ref, far_ref)


def halves_of(rows, width):
    return [pltpu.VMEM((rows // CORES, width), jnp.float32), pltpu.VMEM((rows // CORES, width), jnp.bfloat16)]


def encoded(active, x, enc, bias, dec, tokens):
    rows, depth = x.shape
    features = enc.shape[1]
    return pl.pallas_call(
        functools.partial(encode_kernel, tokens),
        out_shape=[pltpu.VMEM((rows, features), jnp.bfloat16)] + halves_of(rows, depth),
        in_specs=[VMEM_SPEC] * 5,
        out_specs=[VMEM_SPEC] * 3,
        compiler_params=kernel_params(),
        cost_estimate=pl.CostEstimate(flops=4 * rows * depth * features, bytes_accessed=4 * depth * features, transcendentals=0),
        name="encode",
    )(*in_vmem(active, x, enc, bias, dec))


def decoded(codes, dec):
    rows, features = codes.shape
    width = dec.shape[1]
    return pl.pallas_call(
        decode_kernel,
        out_shape=halves_of(rows, width),
        in_specs=[VMEM_SPEC] * 2,
        out_specs=[VMEM_SPEC] * 2,
        compiler_params=kernel_params(),
        cost_estimate=pl.CostEstimate(flops=2 * rows * width * features, bytes_accessed=2 * width * features, transcendentals=0),
        name="decode_own",
    )(*in_vmem(codes, dec))


def back(rows_ref, dec_ref):
    return summed_over(
        rows_ref.shape[1],
        lambda part: lax.dot_general(
            rows_ref[:, part], dec_ref[:, part], (((1,), (1,)), ((), ())), preferred_element_type=jnp.float32
        ),
    )


def grad_own_kernel(rows_ref, dec_ref, out_ref, _):
    out_ref[...] = back(rows_ref, dec_ref)


def grad_all_kernel(tokens, rows_ref, dec_ref, own_ref, out_ref):
    total = own_ref[...] + back(rows_ref, dec_ref)
    group = total.shape[0] // tokens
    for block in range(group):
        slab = slab_of(place_in(group), block, group // CORES)
        where = pl.ds(pl.multiple_of(slab * tokens, tokens), tokens)
        out_ref[0, where, :] = total[block * tokens : (block + 1) * tokens]


def grad_own(rows, dec):
    features = dec.shape[0]
    return pl.pallas_call(
        grad_own_kernel,
        out_shape=[pltpu.VMEM((rows.shape[0], features), jnp.float32), pltpu.VMEM((8, 128), jnp.float32)],
        in_specs=[VMEM_SPEC] * 2,
        out_specs=[VMEM_SPEC] * 2,
        compiler_params=kernel_params(),
        cost_estimate=pl.CostEstimate(flops=2 * rows.size * features, bytes_accessed=2 * dec.size, transcendentals=0),
        name="grad_own",
    )(*in_vmem(rows, dec))[0]


def grad_all(rows, dec, own, tokens):
    return pl.pallas_call(
        functools.partial(grad_all_kernel, tokens),
        out_shape=jax.ShapeDtypeStruct((1,) + own.shape, jnp.float32),
        in_specs=[VMEM_SPEC] * 3,
        out_specs=VMEM_SPEC,
        compiler_params=kernel_params(),
        cost_estimate=pl.CostEstimate(flops=2 * rows.size * own.shape[1], bytes_accessed=2 * dec.size, transcendentals=0),
        name="grad_all",
    )(*in_vmem(rows, dec, own))


def blocks_of(near, far, chips):
    rows = near.shape[0] // chips
    total = near + other_core(far).astype(jnp.float32)
    return [total[chip * rows : (chip + 1) * rows] for chip in range(chips)]


def summed(blocks, sent):
    total = blocks[0]
    for came in [across(blocks[chip].astype(jnp.bfloat16), chip, len(blocks)) for chip in sent]:
        total = total + came.astype(jnp.float32)
    return total


def on_device(resid, enc_weight, enc_bias, active, dec_weight, target):
    group = lax.axis_size(AXIS) // LAYERS
    chips = group // CORES
    index = lax.axis_index(AXIS)
    slab, first, final = lax.optimization_barrier((resid[0], index < group, index >= (LAYERS - 1) * group))
    tokens = resid.shape[1]
    enc, own_dec, next_dec = loaded(enc_weight, dec_weight)
    most, last = [across(slab, chip, chips) for chip in range(1, chips - 1)], across(slab, chips - 1, chips)
    early, late = jnp.concatenate([slab, last], axis=0), jnp.concatenate(most, axis=0)
    early_far, late_far = other_core(early), other_core(late)
    x = jnp.concatenate(
        [slab, late, last, early_far[:tokens], late_far, early_far[tokens:]], axis=0
    )
    codes, next_near, next_far = encoded(active[0], x, enc, enc_bias, next_dec, tokens)
    own_near, own_far = decoded(codes, own_dec)

    nexts = blocks_of(next_near, next_far, chips)
    owns = blocks_of(own_near, own_far, chips)
    risen = raised(nexts[-1].astype(jnp.bfloat16), first, group)
    owns[-1] = owns[-1] + risen.astype(jnp.float32)
    next_sum = after(summed(nexts, range(1, chips - 1)).astype(jnp.bfloat16), owns[-1])
    from_before = raised(next_sum, first, group).astype(jnp.float32)
    own_sum = summed(owns, range(1, chips))
    error = (own_sum + from_before - target[0].astype(jnp.float32)).astype(jnp.bfloat16)

    later = lowered(error, final, group)
    heres = [error] + [across(error, chip, chips) for chip in range(1, chips)]
    afters = [later] + [across(later, chip, chips) for chip in range(1, chips - 1)]
    last = lowered(after(heres[-1], later), final, group)
    here_near = jnp.concatenate(heres, axis=0)
    here_far = other_core(here_near)
    here_rows = jnp.concatenate([here_near, here_far], axis=0)
    most = after(jnp.concatenate(afters, axis=0), here_far)
    after_rows = jnp.concatenate([most, last, other_core(most), other_core(last)], axis=0)
    grad = grad_all(after_rows, next_dec, grad_own(here_rows, own_dec), tokens)
    return (error[None], grad)


def solution(mesh):
    return jax.shard_map(
        on_device,
        mesh=mesh,
        in_specs=(
            P("layer", "groups", None),
            P("layer", None, None),
            P("layer", None),
            P("layer", "groups", None),
            P("layer", None, None, None),
            P("layer", "groups", None),
        ),
        out_specs=(P("layer", "groups", None), P("layer", "groups", None)),
        check_vma=False,
    )
```

```python
import functools

import jax
import jax.numpy as jnp
from jax import lax
from jax.experimental import pallas as pl
from jax.experimental.pallas import tpu as pltpu
from jax.sharding import PartitionSpec as P

BLOCK = 128
LAYERS = 4
TILE = 32
CORES = 2
CHUNK = 1024
LIMIT = 4 << 20
AXIS = "layer"

ANY_SPEC = pl.BlockSpec(memory_space=pl.ANY)
VMEM_SPEC = pl.BlockSpec(memory_space=pltpu.VMEM)


def turned(chip, chips):
    bits = chips.bit_length() - 1
    return sum(((chip >> bit) & 1) << (bits - 1 - bit) for bit in range(bits))


def across(value, chip, chips):
    masks = (CORES * chip, CORES * turned(chip, chips))
    pairs = [(i, i ^ masks[i % CORES]) for i in range(lax.axis_size(AXIS))]
    return lax.ppermute(value, AXIS, pairs)


def other_core(value):
    return lax.ppermute(value, AXIS, [(i, i ^ 1) for i in range(lax.axis_size(AXIS))])


def raised(value, first, group):
    size = lax.axis_size(AXIS)
    came = lax.ppermute(value, AXIS, [(i, (i + group) % size) for i in range(size)])
    return jnp.where(first, jnp.zeros_like(came), came)


def lowered(value, final, group):
    size = lax.axis_size(AXIS)
    came = lax.ppermute(value, AXIS, [((i + group) % size, i) for i in range(size)])
    return jnp.where(final, jnp.zeros_like(came), came)


def after(values, done):
    return lax.optimization_barrier((values, done))[0]


def slab_of(place, block, chips):
    far, chip = block // chips, block % chips
    odd = (place & 1) ^ far
    return place ^ (far + CORES * (chip * (1 - odd) + turned(chip, chips) * odd))


def in_vmem(*arrays):
    return [pltpu.with_memory_space_constraint(a, pltpu.VMEM) for a in arrays]


def in_hbm(*arrays):
    return [pltpu.with_memory_space_constraint(a, pltpu.HBM) for a in arrays]


def kernel_params(limit=LIMIT):
    return pltpu.CompilerParams(vmem_limit_bytes=limit)


def load_kernel(enc_hbm, dec_hbm, enc_ref, own_ref, next_ref, sems):
    pieces = [(enc_hbm.at[0], enc_ref), (dec_hbm.at[0, 1], next_ref), (dec_hbm.at[0, 0], own_ref)]
    copies = [pltpu.make_async_copy(source, target, sems.at[i]) for i, (source, target) in enumerate(pieces)]
    for copy in copies:
        copy.start()
    for copy in copies:
        copy.wait()


def loaded(enc, dec):
    block = pltpu.VMEM(dec.shape[2:], dec.dtype)
    return pl.pallas_call(
        load_kernel,
        out_shape=[pltpu.VMEM(enc.shape[1:], enc.dtype), block, block],
        in_specs=[ANY_SPEC] * 2,
        out_specs=[VMEM_SPEC] * 3,
        scratch_shapes=[pltpu.SemaphoreType.DMA((3,))],
        compiler_params=kernel_params(1 << 20),
        cost_estimate=pl.CostEstimate(flops=0, bytes_accessed=4 * (enc.size + dec.size), transcendentals=0),
        name="load_weights",
    )(*in_hbm(enc, dec))


def decode(codes, dec_ref, near_ref, far_ref):
    half, width = near_ref.shape
    for step in range(width // CHUNK):
        columns = pl.ds(step * CHUNK, CHUNK)
        part = jnp.dot(codes, dec_ref[:, columns], preferred_element_type=jnp.float32)
        near_ref[:, columns] = part[:half]
        far_ref[:, columns] = part[half:].astype(jnp.bfloat16)


def place_in(group):
    return lax.axis_index(AXIS) & (group - 1)


def summed_over(depth, product):
    sums = [None, None]
    for step in range(depth // CHUNK):
        part = product(pl.ds(step * CHUNK, CHUNK))
        so_far = sums[step % 2]
        sums[step % 2] = part if so_far is None else so_far + part
    return sums[0] + sums[1]


def gate_of(active_ref, rows, tokens):
    group = rows // tokens
    block = lax.broadcasted_iota(jnp.int32, (rows, BLOCK), 0) // tokens
    tile = (slab_of(place_in(group), block, group // CORES) * tokens) // TILE
    parts = []
    for part in range(active_ref.shape[1]):
        live = jnp.zeros((rows, BLOCK), jnp.int32)
        for i in range(active_ref.shape[0]):
            live = jnp.where(tile == i, active_ref[pl.ds(i, 1), pl.ds(part, 1)], live)
        parts.append(live.astype(jnp.float32))
    return jnp.concatenate(parts, axis=1)


def gate_kernel(tokens, active_ref, bias_ref, gate_ref, shift_ref):
    rows = gate_ref.shape[0]
    gate_ref[...] = gate_of(active_ref, rows, tokens)
    shift_ref[...] = jnp.broadcast_to(bias_ref[...].astype(jnp.float32), shift_ref.shape)


def gated(active, bias, rows, tokens):
    shape = (rows, bias.shape[1])
    return pl.pallas_call(
        functools.partial(gate_kernel, tokens),
        out_shape=[pltpu.VMEM(shape, jnp.float32)] * 2,
        in_specs=[VMEM_SPEC] * 2,
        out_specs=[VMEM_SPEC] * 2,
        compiler_params=kernel_params(),
        cost_estimate=pl.CostEstimate(flops=8 * rows * shape[1], bytes_accessed=8 * rows * shape[1], transcendentals=0),
        name="gate",
    )(*in_vmem(active, bias))


def decode_kernel(codes_ref, dec_ref, near_ref, far_ref):
    decode(codes_ref[...], dec_ref, near_ref, far_ref)


def halves_of(rows, width):
    return [pltpu.VMEM((rows // CORES, width), jnp.float32), pltpu.VMEM((rows // CORES, width), jnp.bfloat16)]


def decoded(codes, dec):
    rows, features = codes.shape
    width = dec.shape[1]
    return pl.pallas_call(
        decode_kernel,
        out_shape=halves_of(rows, width),
        in_specs=[VMEM_SPEC] * 2,
        out_specs=[VMEM_SPEC] * 2,
        compiler_params=kernel_params(),
        cost_estimate=pl.CostEstimate(flops=2 * rows * width * features, bytes_accessed=2 * width * features, transcendentals=0),
        name="decode",
    )(*in_vmem(codes, dec))


def back(rows_ref, dec_ref):
    return summed_over(
        rows_ref.shape[1],
        lambda part: lax.dot_general(
            rows_ref[:, part], dec_ref[:, part], (((1,), (1,)), ((), ())), preferred_element_type=jnp.float32
        ),
    )


def grad_own_kernel(rows_ref, dec_ref, out_ref, _):
    out_ref[...] = back(rows_ref, dec_ref)


def grad_all_kernel(tokens, rows_ref, dec_ref, own_ref, out_ref):
    total = own_ref[...] + back(rows_ref, dec_ref)
    group = total.shape[0] // tokens
    for block in range(group):
        slab = slab_of(place_in(group), block, group // CORES)
        where = pl.ds(pl.multiple_of(slab * tokens, tokens), tokens)
        out_ref[0, where, :] = total[block * tokens : (block + 1) * tokens]


def grad_own(rows, dec):
    features = dec.shape[0]
    return pl.pallas_call(
        grad_own_kernel,
        out_shape=[pltpu.VMEM((rows.shape[0], features), jnp.float32), pltpu.VMEM((8, 128), jnp.float32)],
        in_specs=[VMEM_SPEC] * 2,
        out_specs=[VMEM_SPEC] * 2,
        compiler_params=kernel_params(),
        cost_estimate=pl.CostEstimate(flops=2 * rows.size * features, bytes_accessed=2 * dec.size, transcendentals=0),
        name="grad_own",
    )(*in_vmem(rows, dec))[0]


def grad_all(rows, dec, own, tokens):
    return pl.pallas_call(
        functools.partial(grad_all_kernel, tokens),
        out_shape=jax.ShapeDtypeStruct((1,) + own.shape, jnp.float32),
        in_specs=[VMEM_SPEC] * 3,
        out_specs=VMEM_SPEC,
        compiler_params=kernel_params(),
        cost_estimate=pl.CostEstimate(flops=2 * rows.size * own.shape[1], bytes_accessed=2 * dec.size, transcendentals=0),
        name="grad_all",
    )(*in_vmem(rows, dec, own))


def blocks_of(near, far, chips):
    rows = near.shape[0] // chips
    total = near + other_core(far).astype(jnp.float32)
    return [total[chip * rows : (chip + 1) * rows] for chip in range(chips)]


def summed(blocks, sent):
    total = blocks[0]
    for came in [across(blocks[chip].astype(jnp.bfloat16), chip, len(blocks)) for chip in sent]:
        total = total + came.astype(jnp.float32)
    return total


def on_device(resid, enc_weight, enc_bias, active, dec_weight, target):
    group = lax.axis_size(AXIS) // LAYERS
    chips = group // CORES
    index = lax.axis_index(AXIS)
    slab, first, final = lax.optimization_barrier((resid[0], index < group, index >= (LAYERS - 1) * group))
    tokens = resid.shape[1]
    enc, own_dec, next_dec = loaded(enc_weight, dec_weight)
    most, last = [across(slab, chip, chips) for chip in range(1, chips - 1)], across(slab, chips - 1, chips)
    early, late = jnp.concatenate([slab, last], axis=0), jnp.concatenate(most, axis=0)
    early_far, late_far = other_core(early), other_core(late)
    x = jnp.concatenate(
        [slab, late, last, early_far[:tokens], late_far, early_far[tokens:]], axis=0
    )
    gate, bias = gated(*after((active[0], enc_bias), enc), group * tokens, tokens)
    pre = jnp.dot(x, enc, preferred_element_type=jnp.float32) + bias
    codes = (jax.nn.relu(pre) * gate).astype(jnp.bfloat16)
    next_near, next_far = decoded(codes, next_dec)
    own_near, own_far = decoded(codes, own_dec)

    nexts = blocks_of(next_near, next_far, chips)
    owns = blocks_of(own_near, own_far, chips)
    risen = raised(nexts[-1].astype(jnp.bfloat16), first, group)
    owns[-1] = owns[-1] + risen.astype(jnp.float32)
    crossed = across(owns[-1].astype(jnp.bfloat16), chips - 1, chips).astype(jnp.float32)
    next_sum = after(summed(nexts, range(1, chips - 1)), owns[-1])
    own_less = summed(owns, range(1, chips - 1)) - target[0].astype(jnp.float32) + crossed

    below = raised(next_sum.astype(jnp.bfloat16), first, group).astype(jnp.float32)
    above = lowered(own_less.astype(jnp.bfloat16), final, group).astype(jnp.float32)
    error = (own_less + below).astype(jnp.bfloat16)
    later = jnp.where(final, 0.0, next_sum + after(above, error)).astype(jnp.bfloat16)

    heres = [error] + [across(error, chip, chips) for chip in range(1, chips)]
    afters = [later] + [across(later, chip, chips) for chip in range(1, chips - 1)]
    last = lowered(after(heres[-1], later), final, group)
    here_near = jnp.concatenate(heres, axis=0)
    here_far = other_core(here_near)
    here_rows = jnp.concatenate([here_near, here_far], axis=0)
    most = after(jnp.concatenate(afters, axis=0), here_far)
    after_rows = jnp.concatenate([most, last, other_core(most), other_core(last)], axis=0)
    grad = grad_all(after_rows, next_dec, grad_own(here_rows, own_dec), tokens)
    return (error[None], grad)


def solution(mesh):
    return jax.shard_map(
        on_device,
        mesh=mesh,
        in_specs=(
            P("layer", "groups", None),
            P("layer", None, None),
            P("layer", None),
            P("layer", "groups", None),
            P("layer", None, None, None),
            P("layer", "groups", None),
        ),
        out_specs=(P("layer", "groups", None), P("layer", "groups", None)),
        check_vma=False,
    )
```

```python
import functools

import jax
import jax.numpy as jnp
from jax import lax
from jax.experimental import pallas as pl
from jax.experimental.pallas import tpu as pltpu
from jax.sharding import PartitionSpec as P

BLOCK = 128
LAYERS = 4
TILE = 32
CORES = 2
CHUNK = 1024
LIMIT = 4 << 20
AXIS = "layer"

ANY_SPEC = pl.BlockSpec(memory_space=pl.ANY)
VMEM_SPEC = pl.BlockSpec(memory_space=pltpu.VMEM)


def turned(chip, chips):
    bits = chips.bit_length() - 1
    return sum(((chip >> bit) & 1) << (bits - 1 - bit) for bit in range(bits))


def across(value, chip, chips):
    masks = (CORES * chip, CORES * turned(chip, chips))
    pairs = [(i, i ^ masks[i % CORES]) for i in range(lax.axis_size(AXIS))]
    return lax.ppermute(value, AXIS, pairs)


def other_core(value):
    return lax.ppermute(value, AXIS, [(i, i ^ 1) for i in range(lax.axis_size(AXIS))])


def raised(value, first, group):
    size = lax.axis_size(AXIS)
    came = lax.ppermute(value, AXIS, [(i, (i + group) % size) for i in range(size)])
    return jnp.where(first, jnp.zeros_like(came), came)


def shifted(value, group):
    size = lax.axis_size(AXIS)
    return lax.ppermute(value, AXIS, [(i, i + group) for i in range(size - group)])


def lowered(value, final, group):
    size = lax.axis_size(AXIS)
    came = lax.ppermute(value, AXIS, [((i + group) % size, i) for i in range(size)])
    return jnp.where(final, jnp.zeros_like(came), came)


def after(values, done):
    return lax.optimization_barrier((values, done))[0]


def slab_of(place, block, chips):
    far, chip = block // chips, block % chips
    odd = (place & 1) ^ far
    return place ^ (far + CORES * (chip * (1 - odd) + turned(chip, chips) * odd))


def in_vmem(*arrays):
    return [pltpu.with_memory_space_constraint(a, pltpu.VMEM) for a in arrays]


def in_hbm(*arrays):
    return [pltpu.with_memory_space_constraint(a, pltpu.HBM) for a in arrays]


def kernel_params(limit=LIMIT):
    return pltpu.CompilerParams(vmem_limit_bytes=limit)


def load_kernel(enc_hbm, dec_hbm, enc_ref, own_ref, next_ref, sems):
    pieces = [(enc_hbm.at[0], enc_ref), (dec_hbm.at[0, 1], next_ref), (dec_hbm.at[0, 0], own_ref)]
    copies = [pltpu.make_async_copy(source, target, sems.at[i]) for i, (source, target) in enumerate(pieces)]
    for copy in copies:
        copy.start()
    for copy in copies:
        copy.wait()


def loaded(enc, dec):
    block = pltpu.VMEM(dec.shape[2:], dec.dtype)
    return pl.pallas_call(
        load_kernel,
        out_shape=[pltpu.VMEM(enc.shape[1:], enc.dtype), block, block],
        in_specs=[ANY_SPEC] * 2,
        out_specs=[VMEM_SPEC] * 3,
        scratch_shapes=[pltpu.SemaphoreType.DMA((3,))],
        compiler_params=kernel_params(1 << 20),
        cost_estimate=pl.CostEstimate(flops=0, bytes_accessed=4 * (enc.size + dec.size), transcendentals=0),
        name="load_weights",
    )(*in_hbm(enc, dec))


def decode(codes, dec_ref, near_ref, far_ref):
    half, width = near_ref.shape
    for step in range(width // CHUNK):
        columns = pl.ds(step * CHUNK, CHUNK)
        part = jnp.dot(codes, dec_ref[:, columns], preferred_element_type=jnp.float32)
        near_ref[:, columns] = part[:half]
        far_ref[:, columns] = part[half:].astype(jnp.bfloat16)


def place_in(group):
    return lax.axis_index(AXIS) & (group - 1)


def summed_over(depth, product):
    sums = [None, None]
    for step in range(depth // CHUNK):
        part = product(pl.ds(step * CHUNK, CHUNK))
        so_far = sums[step % 2]
        sums[step % 2] = part if so_far is None else so_far + part
    return sums[0] + sums[1]


def gate_of(active_ref, rows, tokens):
    group = rows // tokens
    block = lax.broadcasted_iota(jnp.int32, (rows, BLOCK), 0) // tokens
    tile = (slab_of(place_in(group), block, group // CORES) * tokens) // TILE
    parts = []
    for part in range(active_ref.shape[1]):
        live = jnp.zeros((rows, BLOCK), jnp.int32)
        for i in range(active_ref.shape[0]):
            live = jnp.where(tile == i, active_ref[pl.ds(i, 1), pl.ds(part, 1)], live)
        parts.append(live.astype(jnp.float32))
    return jnp.concatenate(parts, axis=1)


def gate_kernel(tokens, active_ref, bias_ref, gate_ref, shift_ref):
    rows = gate_ref.shape[0]
    gate_ref[...] = gate_of(active_ref, rows, tokens)
    shift_ref[...] = jnp.broadcast_to(bias_ref[...].astype(jnp.float32), shift_ref.shape)


def gated(active, bias, rows, tokens):
    shape = (rows, bias.shape[1])
    return pl.pallas_call(
        functools.partial(gate_kernel, tokens),
        out_shape=[pltpu.VMEM(shape, jnp.float32)] * 2,
        in_specs=[VMEM_SPEC] * 2,
        out_specs=[VMEM_SPEC] * 2,
        compiler_params=kernel_params(),
        cost_estimate=pl.CostEstimate(flops=8 * rows * shape[1], bytes_accessed=8 * rows * shape[1], transcendentals=0),
        name="gate",
    )(*in_vmem(active, bias))


def decode_kernel(codes_ref, dec_ref, near_ref, far_ref):
    decode(codes_ref[...], dec_ref, near_ref, far_ref)


def halves_of(rows, width):
    return [pltpu.VMEM((rows // CORES, width), jnp.float32), pltpu.VMEM((rows // CORES, width), jnp.bfloat16)]


def decoded(codes, dec):
    rows, features = codes.shape
    width = dec.shape[1]
    return pl.pallas_call(
        decode_kernel,
        out_shape=halves_of(rows, width),
        in_specs=[VMEM_SPEC] * 2,
        out_specs=[VMEM_SPEC] * 2,
        compiler_params=kernel_params(),
        cost_estimate=pl.CostEstimate(flops=2 * rows * width * features, bytes_accessed=2 * width * features, transcendentals=0),
        name="decode",
    )(*in_vmem(codes, dec))


def back(rows_ref, dec_ref):
    return summed_over(
        rows_ref.shape[1],
        lambda part: lax.dot_general(
            rows_ref[:, part], dec_ref[:, part], (((1,), (1,)), ((), ())), preferred_element_type=jnp.float32
        ),
    )


def grad_own_kernel(rows_ref, dec_ref, out_ref, _):
    out_ref[...] = back(rows_ref, dec_ref)


def grad_all_kernel(tokens, rows_ref, dec_ref, own_ref, out_ref):
    total = own_ref[...] + back(rows_ref, dec_ref)
    group = total.shape[0] // tokens
    for block in range(group):
        slab = slab_of(place_in(group), block, group // CORES)
        where = pl.ds(pl.multiple_of(slab * tokens, tokens), tokens)
        out_ref[0, where, :] = total[block * tokens : (block + 1) * tokens]


def grad_own(rows, dec):
    features = dec.shape[0]
    return pl.pallas_call(
        grad_own_kernel,
        out_shape=[pltpu.VMEM((rows.shape[0], features), jnp.float32), pltpu.VMEM((8, 128), jnp.float32)],
        in_specs=[VMEM_SPEC] * 2,
        out_specs=[VMEM_SPEC] * 2,
        compiler_params=kernel_params(),
        cost_estimate=pl.CostEstimate(flops=2 * rows.size * features, bytes_accessed=2 * dec.size, transcendentals=0),
        name="grad_own",
    )(*in_vmem(rows, dec))[0]


def grad_all(rows, dec, own, tokens):
    return pl.pallas_call(
        functools.partial(grad_all_kernel, tokens),
        out_shape=jax.ShapeDtypeStruct((1,) + own.shape, jnp.float32),
        in_specs=[VMEM_SPEC] * 3,
        out_specs=VMEM_SPEC,
        compiler_params=kernel_params(),
        cost_estimate=pl.CostEstimate(flops=2 * rows.size * own.shape[1], bytes_accessed=2 * dec.size, transcendentals=0),
        name="grad_all",
    )(*in_vmem(rows, dec, own))


def blocks_of(near, far, chips):
    rows = near.shape[0] // chips
    total = near + other_core(far).astype(jnp.float32)
    return [total[chip * rows : (chip + 1) * rows] for chip in range(chips)]


def summed(blocks, sent):
    total = blocks[0]
    for came in [across(blocks[chip].astype(jnp.bfloat16), chip, len(blocks)) for chip in sent]:
        total = total + came.astype(jnp.float32)
    return total


def on_device(resid, enc_weight, enc_bias, active, dec_weight, target):
    group = lax.axis_size(AXIS) // LAYERS
    chips = group // CORES
    index = lax.axis_index(AXIS)
    slab, first, final = lax.optimization_barrier((resid[0], index < group, index >= (LAYERS - 1) * group))
    tokens = resid.shape[1]
    enc, own_dec, next_dec = loaded(enc_weight, dec_weight)
    most, last = [across(slab, chip, chips) for chip in range(1, chips - 1)], across(slab, chips - 1, chips)
    early, late = jnp.concatenate([slab, last], axis=0), jnp.concatenate(most, axis=0)
    early_far, late_far = other_core(early), other_core(late)
    x = jnp.concatenate(
        [after(slab, late), late, last, early_far[:tokens], late_far, early_far[tokens:]], axis=0
    )
    gate, bias = gated(*after((active[0], enc_bias), enc), group * tokens, tokens)
    pre = jnp.dot(x, enc, preferred_element_type=jnp.float32) + bias
    codes = (jax.nn.relu(pre) * gate).astype(jnp.bfloat16)
    next_near, next_far = decoded(codes, next_dec)
    own_near, own_far = decoded(codes, own_dec)

    nexts = blocks_of(next_near, next_far, chips)
    owns = blocks_of(own_near, own_far, chips)
    risen = raised(nexts[-1].astype(jnp.bfloat16), first, group)
    owns[-1] = owns[-1] + risen.astype(jnp.float32)
    crossed = across(owns[-1].astype(jnp.bfloat16), chips - 1, chips).astype(jnp.float32)
    next_sum = after(summed(nexts, range(1, chips - 1)), owns[-1])
    own_less = summed(owns, range(1, chips - 1)) - target[0].astype(jnp.float32) + crossed

    below = shifted(next_sum.astype(jnp.bfloat16), group).astype(jnp.float32)
    above = lowered(own_less.astype(jnp.bfloat16), final, group).astype(jnp.float32)
    error = (own_less + below).astype(jnp.bfloat16)
    later = jnp.where(final, 0.0, next_sum + after(above, error)).astype(jnp.bfloat16)

    heres = [error] + [across(error, chip, chips) for chip in range(1, chips)]
    afters = [later] + [across(later, chip, chips) for chip in range(1, chips - 1)]
    last = lowered(after(heres[-1], later), final, group)
    here_near = jnp.concatenate(heres, axis=0)
    here_far = other_core(here_near)
    here_rows = jnp.concatenate([here_near, here_far], axis=0)
    most = after(jnp.concatenate(afters, axis=0), here_far)
    after_rows = jnp.concatenate([most, last, other_core(most), other_core(last)], axis=0)
    grad = grad_all(after_rows, next_dec, grad_own(here_rows, own_dec), tokens)
    return (error[None], grad)


def solution(mesh):
    return jax.shard_map(
        on_device,
        mesh=mesh,
        in_specs=(
            P("layer", "groups", None),
            P("layer", None, None),
            P("layer", None),
            P("layer", "groups", None),
            P("layer", None, None, None),
            P("layer", "groups", None),
        ),
        out_specs=(P("layer", "groups", None), P("layer", "groups", None)),
        check_vma=False,
    )
```

```python
import functools

import jax
import jax.numpy as jnp
from jax import lax
from jax.experimental import pallas as pl
from jax.experimental.pallas import tpu as pltpu
from jax.sharding import PartitionSpec as P

BLOCK = 128
LAYERS = 4
TILE = 32
CORES = 2
CHUNK = 1024
LIMIT = 4 << 20
AXIS = "layer"

ANY_SPEC = pl.BlockSpec(memory_space=pl.ANY)
VMEM_SPEC = pl.BlockSpec(memory_space=pltpu.VMEM)


def turned(chip, chips):
    bits = chips.bit_length() - 1
    return sum(((chip >> bit) & 1) << (bits - 1 - bit) for bit in range(bits))


def across(value, chip, chips):
    masks = (CORES * chip, CORES * turned(chip, chips))
    pairs = [(i, i ^ masks[i % CORES]) for i in range(lax.axis_size(AXIS))]
    return lax.ppermute(value, AXIS, pairs)


def other_core(value):
    return lax.ppermute(value, AXIS, [(i, i ^ 1) for i in range(lax.axis_size(AXIS))])


def raised(value, first, group):
    size = lax.axis_size(AXIS)
    came = lax.ppermute(value, AXIS, [(i, (i + group) % size) for i in range(size)])
    return jnp.where(first, jnp.zeros_like(came), came)


def lowered(value, group):
    size = lax.axis_size(AXIS)
    return lax.ppermute(value, AXIS, [((i + group) % size, i) for i in range(size)])


def after(values, done):
    return lax.optimization_barrier((values, done))[0]


def slab_of(place, block, chips):
    far, chip = block // chips, block % chips
    odd = (place & 1) ^ far
    return place ^ (far + CORES * (chip * (1 - odd) + turned(chip, chips) * odd))


def in_vmem(*arrays):
    return [pltpu.with_memory_space_constraint(a, pltpu.VMEM) for a in arrays]


def in_hbm(*arrays):
    return [pltpu.with_memory_space_constraint(a, pltpu.HBM) for a in arrays]


def kernel_params(limit=LIMIT):
    return pltpu.CompilerParams(vmem_limit_bytes=limit)


def load_kernel(pieces, weight_hbm, *rest):
    held, sems = rest[-1 - len(pieces) : -1], rest[-1]
    copies = [
        pltpu.make_async_copy(weight_hbm.at[piece], target, sems.at[i])
        for i, (piece, target) in enumerate(zip(pieces, held))
    ]
    for copy in copies:
        copy.start()
    for copy in copies:
        copy.wait()


def loaded(weight, pieces, *done):
    shape = weight.shape[len(pieces[0]) :]
    return pl.pallas_call(
        functools.partial(load_kernel, pieces),
        out_shape=[pltpu.VMEM(shape, weight.dtype)] * len(pieces),
        in_specs=[ANY_SPEC] * (1 + len(done)),
        out_specs=[VMEM_SPEC] * len(pieces),
        scratch_shapes=[pltpu.SemaphoreType.DMA((len(pieces),))],
        compiler_params=kernel_params(1 << 20),
        cost_estimate=pl.CostEstimate(flops=0, bytes_accessed=4 * weight.size, transcendentals=0),
        name="load_weights",
    )(*in_hbm(weight), *done)


def decode(codes, dec_ref, near_ref, far_ref):
    half, width = near_ref.shape
    for step in range(width // CHUNK):
        columns = pl.ds(step * CHUNK, CHUNK)
        part = jnp.dot(codes, dec_ref[:, columns], preferred_element_type=jnp.float32)
        near_ref[:, columns] = part[:half]
        far_ref[:, columns] = part[half:].astype(jnp.bfloat16)


def place_in(group):
    return lax.axis_index(AXIS) & (group - 1)


def summed_over(depth, product):
    sums = [None, None]
    for step in range(depth // CHUNK):
        part = product(pl.ds(step * CHUNK, CHUNK))
        so_far = sums[step % 2]
        sums[step % 2] = part if so_far is None else so_far + part
    return sums[0] + sums[1]


def gate_of(active_ref, rows, tokens):
    group = rows // tokens
    block = lax.broadcasted_iota(jnp.int32, (rows, BLOCK), 0) // tokens
    tile = (slab_of(place_in(group), block, group // CORES) * tokens) // TILE
    parts = []
    for part in range(active_ref.shape[1]):
        live = jnp.zeros((rows, BLOCK), jnp.int32)
        for i in range(active_ref.shape[0]):
            live = jnp.where(tile == i, active_ref[pl.ds(i, 1), pl.ds(part, 1)], live)
        parts.append(live.astype(jnp.float32))
    return jnp.concatenate(parts, axis=1)


def gate_kernel(tokens, active_ref, bias_ref, gate_ref, shift_ref):
    rows = gate_ref.shape[0]
    gate_ref[...] = gate_of(active_ref, rows, tokens)
    shift_ref[...] = jnp.broadcast_to(bias_ref[...].astype(jnp.float32), shift_ref.shape)


def gated(active, bias, rows, tokens):
    shape = (rows, bias.shape[1])
    return pl.pallas_call(
        functools.partial(gate_kernel, tokens),
        out_shape=[pltpu.VMEM(shape, jnp.float32)] * 2,
        in_specs=[VMEM_SPEC] * 2,
        out_specs=[VMEM_SPEC] * 2,
        compiler_params=kernel_params(),
        cost_estimate=pl.CostEstimate(flops=8 * rows * shape[1], bytes_accessed=8 * rows * shape[1], transcendentals=0),
        name="gate",
    )(*in_vmem(active, bias))


def decode_kernel(codes_ref, dec_ref, near_ref, far_ref):
    decode(codes_ref[...], dec_ref, near_ref, far_ref)


def halves_of(rows, width):
    return [pltpu.VMEM((rows // CORES, width), jnp.float32), pltpu.VMEM((rows // CORES, width), jnp.bfloat16)]


def decoded(codes, dec):
    rows, features = codes.shape
    width = dec.shape[1]
    return pl.pallas_call(
        decode_kernel,
        out_shape=halves_of(rows, width),
        in_specs=[VMEM_SPEC] * 2,
        out_specs=[VMEM_SPEC] * 2,
        compiler_params=kernel_params(),
        cost_estimate=pl.CostEstimate(flops=2 * rows * width * features, bytes_accessed=2 * width * features, transcendentals=0),
        name="decode",
    )(*in_vmem(codes, dec))


def back(rows_ref, dec_ref):
    return summed_over(
        rows_ref.shape[1],
        lambda part: lax.dot_general(
            rows_ref[:, part], dec_ref[:, part], (((1,), (1,)), ((), ())), preferred_element_type=jnp.float32
        ),
    )


def grad_first_kernel(rows_ref, dec_ref, out_ref, _):
    out_ref[...] = back(rows_ref, dec_ref)


def grad_all_kernel(tokens, rows_ref, dec_ref, first_ref, out_ref):
    total = first_ref[...] + back(rows_ref, dec_ref)
    group = total.shape[0] // tokens
    for block in range(group):
        slab = slab_of(place_in(group), block, group // CORES)
        where = pl.ds(pl.multiple_of(slab * tokens, tokens), tokens)
        out_ref[0, where, :] = total[block * tokens : (block + 1) * tokens]


def grad_first(rows, dec):
    features = dec.shape[0]
    return pl.pallas_call(
        grad_first_kernel,
        out_shape=[pltpu.VMEM((rows.shape[0], features), jnp.float32), pltpu.VMEM((8, 128), jnp.float32)],
        in_specs=[VMEM_SPEC] * 2,
        out_specs=[VMEM_SPEC] * 2,
        compiler_params=kernel_params(),
        cost_estimate=pl.CostEstimate(flops=2 * rows.size * features, bytes_accessed=2 * dec.size, transcendentals=0),
        name="grad_first",
    )(*in_vmem(rows, dec))[0]


def grad_all(rows, dec, own, tokens):
    return pl.pallas_call(
        functools.partial(grad_all_kernel, tokens),
        out_shape=jax.ShapeDtypeStruct((1,) + own.shape, jnp.float32),
        in_specs=[VMEM_SPEC] * 3,
        out_specs=VMEM_SPEC,
        compiler_params=kernel_params(),
        cost_estimate=pl.CostEstimate(flops=2 * rows.size * own.shape[1], bytes_accessed=2 * dec.size, transcendentals=0),
        name="grad_all",
    )(*in_vmem(rows, dec, own))


def both_cores(near, far):
    return near + other_core(far).astype(jnp.float32)


def halved(total, bit, chips):
    rows, width = total.shape[0] // (chips >> bit), total.shape[1]
    pairs = total.reshape(-1, 2, rows, width)
    came = across(pairs[:, 1].astype(jnp.bfloat16), 1 << bit, chips)
    return (pairs[:, 0] + came.astype(jnp.float32)).reshape(-1, width)


def gathered(slab, chips, done=None):
    pieces = [slab]
    for chip in range(1, chips):
        top = 1 << (chip.bit_length() - 1)
        piece = pieces[chip - top]
        if chip > top and done is not None:
            piece = after(piece, done)
        pieces.append(across(piece, top, chips))
    return pieces


def on_device(resid, enc_weight, enc_bias, active, dec_weight, target):
    group = lax.axis_size(AXIS) // LAYERS
    chips = group // CORES
    index = lax.axis_index(AXIS)
    slab, first, final = lax.optimization_barrier((resid[0], index < group, index >= (LAYERS - 1) * group))
    tokens = resid.shape[1]
    (enc,) = loaded(enc_weight, [(0,)])
    pieces = gathered(slab, chips, enc)
    own_dec, next_dec = loaded(dec_weight, [(0, 0), (0, 1)], pieces[1])
    most, last = after((jnp.concatenate(pieces[:-1], axis=0), pieces[-1]), own_dec)
    x = jnp.concatenate([most, last, other_core(most), other_core(last)], axis=0)
    gate, bias = gated(*after((active[0], enc_bias), enc), group * tokens, tokens)
    pre = jnp.dot(x, enc, preferred_element_type=jnp.float32) + bias
    codes = (jax.nn.relu(pre) * gate).astype(jnp.bfloat16)
    next_near, next_far = decoded(codes, next_dec)
    own_near, own_far = decoded(codes, own_dec)

    next_sum, own_sum = both_cores(next_near, next_far), both_cores(own_near, own_far)
    for bit in range(chips.bit_length() - 1):
        next_sum = halved(next_sum, bit, chips)
        own_sum = after(halved(own_sum, bit, chips), next_sum)
    own_less = own_sum - target[0].astype(jnp.float32)
    below = raised(next_sum.astype(jnp.bfloat16), first, group).astype(jnp.float32)
    above = lowered(own_less.astype(jnp.bfloat16), group)
    error = (own_less + below).astype(jnp.bfloat16)
    later = jnp.where(final, 0.0, next_sum + after(above, error).astype(jnp.float32)).astype(jnp.bfloat16)

    here_near = jnp.concatenate(gathered(error, chips), axis=0)
    here_far = other_core(here_near)
    here_rows = jnp.concatenate([here_near, here_far], axis=0)
    afters = gathered(later, chips)
    most, last = after(jnp.concatenate(afters[:-1], axis=0), here_far), afters[-1]
    after_rows = jnp.concatenate([most, last, other_core(most), other_core(last)], axis=0)
    grad = grad_all(after_rows, next_dec, grad_first(here_rows, own_dec), tokens)
    return (error[None], grad)


def solution(mesh):
    return jax.shard_map(
        on_device,
        mesh=mesh,
        in_specs=(
            P("layer", "groups", None),
            P("layer", None, None),
            P("layer", None),
            P("layer", "groups", None),
            P("layer", None, None, None),
            P("layer", "groups", None),
        ),
        out_specs=(P("layer", "groups", None), P("layer", "groups", None)),
        check_vma=False,
    )
```

```python
import functools

import jax
import jax.numpy as jnp
from jax import lax
from jax.experimental import pallas as pl
from jax.experimental.pallas import tpu as pltpu
from jax.sharding import PartitionSpec as P

BLOCK = 128
LAYERS = 4
TILE = 32
CORES = 2
CHUNK = 1024
LIMIT = 4 << 20
AXIS = "layer"

ANY_SPEC = pl.BlockSpec(memory_space=pl.ANY)
VMEM_SPEC = pl.BlockSpec(memory_space=pltpu.VMEM)


def turned(chip, chips):
    bits = chips.bit_length() - 1
    return sum(((chip >> bit) & 1) << (bits - 1 - bit) for bit in range(bits))


def across(value, chip, chips):
    masks = (CORES * chip, CORES * turned(chip, chips))
    pairs = [(i, i ^ masks[i % CORES]) for i in range(lax.axis_size(AXIS))]
    return lax.ppermute(value, AXIS, pairs)


def other_core(value):
    return lax.ppermute(value, AXIS, [(i, i ^ 1) for i in range(lax.axis_size(AXIS))])


def raised(value, first, group):
    size = lax.axis_size(AXIS)
    came = lax.ppermute(value, AXIS, [(i, (i + group) % size) for i in range(size)])
    return jnp.where(first, jnp.zeros_like(came), came)


def lowered(value, final, group):
    size = lax.axis_size(AXIS)
    came = lax.ppermute(value, AXIS, [((i + group) % size, i) for i in range(size)])
    return jnp.where(final, jnp.zeros_like(came), came)


def after(values, done):
    return lax.optimization_barrier((values, done))[0]


def slab_of(place, block, chips):
    far, chip = block // chips, block % chips
    odd = (place & 1) ^ far
    return place ^ (far + CORES * (chip * (1 - odd) + turned(chip, chips) * odd))


def in_vmem(*arrays):
    return [pltpu.with_memory_space_constraint(a, pltpu.VMEM) for a in arrays]


def in_hbm(*arrays):
    return [pltpu.with_memory_space_constraint(a, pltpu.HBM) for a in arrays]


def kernel_params(limit=LIMIT):
    return pltpu.CompilerParams(vmem_limit_bytes=limit)


def load_kernel(enc_hbm, dec_hbm, enc_ref, own_ref, next_ref, sems):
    pieces = [(enc_hbm.at[0], enc_ref), (dec_hbm.at[0, 1], next_ref), (dec_hbm.at[0, 0], own_ref)]
    copies = [pltpu.make_async_copy(source, target, sems.at[i]) for i, (source, target) in enumerate(pieces)]
    for copy in copies:
        copy.start()
    for copy in copies:
        copy.wait()


def loaded(enc, dec):
    block = pltpu.VMEM(dec.shape[2:], dec.dtype)
    return pl.pallas_call(
        load_kernel,
        out_shape=[pltpu.VMEM(enc.shape[1:], enc.dtype), block, block],
        in_specs=[ANY_SPEC] * 2,
        out_specs=[VMEM_SPEC] * 3,
        scratch_shapes=[pltpu.SemaphoreType.DMA((3,))],
        compiler_params=kernel_params(1 << 20),
        cost_estimate=pl.CostEstimate(flops=0, bytes_accessed=4 * (enc.size + dec.size), transcendentals=0),
        name="load_weights",
    )(*in_hbm(enc, dec))


def decode(codes, dec_ref, near_ref, far_ref):
    half, width = near_ref.shape
    for step in range(width // CHUNK):
        columns = pl.ds(step * CHUNK, CHUNK)
        part = jnp.dot(codes, dec_ref[:, columns], preferred_element_type=jnp.float32)
        near_ref[:, columns] = part[:half]
        far_ref[:, columns] = part[half:].astype(jnp.bfloat16)


def place_in(group):
    return lax.axis_index(AXIS) & (group - 1)


def summed_over(depth, product):
    sums = [None, None]
    for step in range(depth // CHUNK):
        part = product(pl.ds(step * CHUNK, CHUNK))
        so_far = sums[step % 2]
        sums[step % 2] = part if so_far is None else so_far + part
    return sums[0] + sums[1]


def gate_of(active_ref, rows, tokens):
    group = rows // tokens
    block = lax.broadcasted_iota(jnp.int32, (rows, BLOCK), 0) // tokens
    tile = (slab_of(place_in(group), block, group // CORES) * tokens) // TILE
    parts = []
    for part in range(active_ref.shape[1]):
        live = jnp.zeros((rows, BLOCK), jnp.int32)
        for i in range(active_ref.shape[0]):
            live = jnp.where(tile == i, active_ref[pl.ds(i, 1), pl.ds(part, 1)], live)
        parts.append(live.astype(jnp.float32))
    return jnp.concatenate(parts, axis=1)


def gate_kernel(tokens, active_ref, bias_ref, gate_ref, shift_ref):
    rows = gate_ref.shape[0]
    gate_ref[...] = gate_of(active_ref, rows, tokens)
    shift_ref[...] = jnp.broadcast_to(bias_ref[...].astype(jnp.float32), shift_ref.shape)


def gated(active, bias, rows, tokens):
    shape = (rows, bias.shape[1])
    return pl.pallas_call(
        functools.partial(gate_kernel, tokens),
        out_shape=[pltpu.VMEM(shape, jnp.float32)] * 2,
        in_specs=[VMEM_SPEC] * 2,
        out_specs=[VMEM_SPEC] * 2,
        compiler_params=kernel_params(),
        cost_estimate=pl.CostEstimate(flops=8 * rows * shape[1], bytes_accessed=8 * rows * shape[1], transcendentals=0),
        name="gate",
    )(*in_vmem(active, bias))


def decode_kernel(codes_ref, dec_ref, near_ref, far_ref):
    decode(codes_ref[...], dec_ref, near_ref, far_ref)


def halves_of(rows, width):
    return [pltpu.VMEM((rows // CORES, width), jnp.float32), pltpu.VMEM((rows // CORES, width), jnp.bfloat16)]


def decoded(codes, dec):
    rows, features = codes.shape
    width = dec.shape[1]
    return pl.pallas_call(
        decode_kernel,
        out_shape=halves_of(rows, width),
        in_specs=[VMEM_SPEC] * 2,
        out_specs=[VMEM_SPEC] * 2,
        compiler_params=kernel_params(),
        cost_estimate=pl.CostEstimate(flops=2 * rows * width * features, bytes_accessed=2 * width * features, transcendentals=0),
        name="decode",
    )(*in_vmem(codes, dec))


def back(rows_ref, dec_ref):
    return summed_over(
        rows_ref.shape[1],
        lambda part: lax.dot_general(
            rows_ref[:, part], dec_ref[:, part], (((1,), (1,)), ((), ())), preferred_element_type=jnp.float32
        ),
    )


def grad_own_kernel(rows_ref, dec_ref, out_ref, _):
    out_ref[...] = back(rows_ref, dec_ref)


def grad_all_kernel(tokens, rows_ref, dec_ref, own_ref, out_ref):
    total = own_ref[...] + back(rows_ref, dec_ref)
    group = total.shape[0] // tokens
    for block in range(group):
        slab = slab_of(place_in(group), block, group // CORES)
        where = pl.ds(pl.multiple_of(slab * tokens, tokens), tokens)
        out_ref[0, where, :] = total[block * tokens : (block + 1) * tokens]


def grad_own(rows, dec):
    features = dec.shape[0]
    return pl.pallas_call(
        grad_own_kernel,
        out_shape=[pltpu.VMEM((rows.shape[0], features), jnp.float32), pltpu.VMEM((8, 128), jnp.float32)],
        in_specs=[VMEM_SPEC] * 2,
        out_specs=[VMEM_SPEC] * 2,
        compiler_params=kernel_params(),
        cost_estimate=pl.CostEstimate(flops=2 * rows.size * features, bytes_accessed=2 * dec.size, transcendentals=0),
        name="grad_own",
    )(*in_vmem(rows, dec))[0]


def grad_all(rows, dec, own, tokens):
    return pl.pallas_call(
        functools.partial(grad_all_kernel, tokens),
        out_shape=jax.ShapeDtypeStruct((1,) + own.shape, jnp.float32),
        in_specs=[VMEM_SPEC] * 3,
        out_specs=VMEM_SPEC,
        compiler_params=kernel_params(),
        cost_estimate=pl.CostEstimate(flops=2 * rows.size * own.shape[1], bytes_accessed=2 * dec.size, transcendentals=0),
        name="grad_all",
    )(*in_vmem(rows, dec, own))


def blocks_of(near, far, chips):
    rows = near.shape[0] // chips
    total = near + other_core(far).astype(jnp.float32)
    return [total[chip * rows : (chip + 1) * rows] for chip in range(chips)]


def summed(blocks, sent):
    total = blocks[0]
    for came in [across(blocks[chip].astype(jnp.bfloat16), chip, len(blocks)) for chip in sent]:
        total = total + came.astype(jnp.float32)
    return total


def on_device(resid, enc_weight, enc_bias, active, dec_weight, target):
    group = lax.axis_size(AXIS) // LAYERS
    chips = group // CORES
    index = lax.axis_index(AXIS)
    slab, first, final = lax.optimization_barrier((resid[0], index < group, index >= (LAYERS - 1) * group))
    tokens = resid.shape[1]
    enc, own_dec, next_dec = loaded(enc_weight, dec_weight)
    most, last = [across(slab, chip, chips) for chip in range(1, chips - 1)], across(slab, chips - 1, chips)
    early, late = jnp.concatenate([slab, last], axis=0), jnp.concatenate(most, axis=0)
    early_far, late_far = other_core(early), other_core(late)
    x = jnp.concatenate(
        [slab, late, last, early_far[:tokens], late_far, early_far[tokens:]], axis=0
    )
    gate, bias = gated(*after((active[0], enc_bias), enc), group * tokens, tokens)
    pre = jnp.dot(x, enc, preferred_element_type=jnp.float32) + bias
    codes = (jax.nn.relu(pre) * gate).astype(jnp.bfloat16)
    next_near, next_far = decoded(codes, next_dec)
    own_near, own_far = decoded(codes, own_dec)

    nexts = blocks_of(next_near, next_far, chips)
    owns = blocks_of(own_near, own_far, chips)
    risen = raised(nexts[-1].astype(jnp.bfloat16), first, group)
    owns[-1] = owns[-1] + risen.astype(jnp.float32)
    crossed = across(owns[-1].astype(jnp.bfloat16), chips - 1, chips).astype(jnp.float32)
    next_sum = after(summed(nexts, range(1, chips - 1)), owns[-1])
    own_less = summed(owns, range(1, chips - 1)) - target[0].astype(jnp.float32) + crossed

    below = raised(next_sum.astype(jnp.bfloat16), first, group).astype(jnp.float32)
    above = lowered(own_less.astype(jnp.bfloat16), final, group).astype(jnp.float32)
    error = (own_less + below).astype(jnp.bfloat16)
    later = jnp.where(final, 0.0, next_sum + after(above, error)).astype(jnp.bfloat16)

    heres = [error] + [across(error, chip, chips) for chip in range(1, chips)]
    afters = [later] + [across(later, chip, chips) for chip in range(1, chips)]
    here_near = jnp.concatenate(heres, axis=0)
    here_far = other_core(here_near)
    here_rows = jnp.concatenate([here_near, here_far], axis=0)
    after_near = after(jnp.concatenate(afters, axis=0), here_far)
    after_rows = jnp.concatenate([after_near, other_core(after_near)], axis=0)
    grad = grad_all(after_rows, next_dec, grad_own(here_rows, own_dec), tokens)
    return (error[None], grad)


def solution(mesh):
    return jax.shard_map(
        on_device,
        mesh=mesh,
        in_specs=(
            P("layer", "groups", None),
            P("layer", None, None),
            P("layer", None),
            P("layer", "groups", None),
            P("layer", None, None, None),
            P("layer", "groups", None),
        ),
        out_specs=(P("layer", "groups", None), P("layer", "groups", None)),
        check_vma=False,
    )
```

```python
import functools

import jax
import jax.numpy as jnp
from jax import lax
from jax.experimental import pallas as pl
from jax.experimental.pallas import tpu as pltpu
from jax.sharding import PartitionSpec as P

BLOCK = 128
LAYERS = 4
TILE = 32
CORES = 2
CHUNK = 1024
LIMIT = 4 << 20
AXIS = "layer"

ANY_SPEC = pl.BlockSpec(memory_space=pl.ANY)
VMEM_SPEC = pl.BlockSpec(memory_space=pltpu.VMEM)


def turned(chip, chips):
    bits = chips.bit_length() - 1
    return sum(((chip >> bit) & 1) << (bits - 1 - bit) for bit in range(bits))


def across(value, chip, chips):
    masks = (CORES * chip, CORES * turned(chip, chips))
    pairs = [(i, i ^ masks[i % CORES]) for i in range(lax.axis_size(AXIS))]
    return lax.ppermute(value, AXIS, pairs)


def other_core(value):
    return lax.ppermute(value, AXIS, [(i, i ^ 1) for i in range(lax.axis_size(AXIS))])


def raised(value, first, group):
    size = lax.axis_size(AXIS)
    came = lax.ppermute(value, AXIS, [(i, (i + group) % size) for i in range(size)])
    return jnp.where(first, jnp.zeros_like(came), came)


def shifted(value, group):
    size = lax.axis_size(AXIS)
    return lax.ppermute(value, AXIS, [(i, i + group) for i in range(size - group)])


def lowered(value, group):
    size = lax.axis_size(AXIS)
    return lax.ppermute(value, AXIS, [(i + group, i) for i in range(size - group)])


def after(values, done):
    return lax.optimization_barrier((values, done))[0]


def slab_of(place, block, chips):
    far, chip = block // chips, block % chips
    odd = (place & 1) ^ far
    return place ^ (far + CORES * (chip * (1 - odd) + turned(chip, chips) * odd))


def in_vmem(*arrays):
    return [pltpu.with_memory_space_constraint(a, pltpu.VMEM) for a in arrays]


def in_hbm(*arrays):
    return [pltpu.with_memory_space_constraint(a, pltpu.HBM) for a in arrays]


def kernel_params(limit=LIMIT):
    return pltpu.CompilerParams(vmem_limit_bytes=limit)


def load_kernel(enc_hbm, dec_hbm, enc_ref, own_ref, next_ref, sems):
    pieces = [(enc_hbm.at[0], enc_ref), (dec_hbm.at[0, 1], next_ref), (dec_hbm.at[0, 0], own_ref)]
    copies = [pltpu.make_async_copy(source, target, sems.at[i]) for i, (source, target) in enumerate(pieces)]
    for copy in copies:
        copy.start()
    for copy in copies:
        copy.wait()


def loaded(enc, dec):
    block = pltpu.VMEM(dec.shape[2:], dec.dtype)
    return pl.pallas_call(
        load_kernel,
        out_shape=[pltpu.VMEM(enc.shape[1:], enc.dtype), block, block],
        in_specs=[ANY_SPEC] * 2,
        out_specs=[VMEM_SPEC] * 3,
        scratch_shapes=[pltpu.SemaphoreType.DMA((3,))],
        compiler_params=kernel_params(1 << 20),
        cost_estimate=pl.CostEstimate(flops=0, bytes_accessed=4 * (enc.size + dec.size), transcendentals=0),
        name="load_weights",
    )(*in_hbm(enc, dec))


def decode(codes, dec_ref, near_ref, far_ref):
    half, width = near_ref.shape
    for step in range(width // CHUNK):
        columns = pl.ds(step * CHUNK, CHUNK)
        part = jnp.dot(codes, dec_ref[:, columns], preferred_element_type=jnp.float32)
        near_ref[:, columns] = part[:half]
        far_ref[:, columns] = part[half:].astype(jnp.bfloat16)


def place_in(group):
    return lax.axis_index(AXIS) & (group - 1)


def summed_over(depth, product):
    sums = [None, None]
    for step in range(depth // CHUNK):
        part = product(pl.ds(step * CHUNK, CHUNK))
        so_far = sums[step % 2]
        sums[step % 2] = part if so_far is None else so_far + part
    return sums[0] + sums[1]


def gate_of(active_ref, rows, tokens):
    group = rows // tokens
    block = lax.broadcasted_iota(jnp.int32, (rows, BLOCK), 0) // tokens
    tile = (slab_of(place_in(group), block, group // CORES) * tokens) // TILE
    parts = []
    for part in range(active_ref.shape[1]):
        live = jnp.zeros((rows, BLOCK), jnp.int32)
        for i in range(active_ref.shape[0]):
            live = jnp.where(tile == i, active_ref[pl.ds(i, 1), pl.ds(part, 1)], live)
        parts.append(live.astype(jnp.float32))
    return jnp.concatenate(parts, axis=1)


def gate_kernel(tokens, active_ref, bias_ref, gate_ref, shift_ref):
    rows = gate_ref.shape[0]
    gate_ref[...] = gate_of(active_ref, rows, tokens)
    shift_ref[...] = jnp.broadcast_to(bias_ref[...].astype(jnp.float32), shift_ref.shape)


def gated(active, bias, rows, tokens):
    shape = (rows, bias.shape[1])
    return pl.pallas_call(
        functools.partial(gate_kernel, tokens),
        out_shape=[pltpu.VMEM(shape, jnp.float32)] * 2,
        in_specs=[VMEM_SPEC] * 2,
        out_specs=[VMEM_SPEC] * 2,
        compiler_params=kernel_params(),
        cost_estimate=pl.CostEstimate(flops=8 * rows * shape[1], bytes_accessed=8 * rows * shape[1], transcendentals=0),
        name="gate",
    )(*in_vmem(active, bias))


def decode_kernel(codes_ref, dec_ref, near_ref, far_ref):
    decode(codes_ref[...], dec_ref, near_ref, far_ref)


def halves_of(rows, width):
    return [pltpu.VMEM((rows // CORES, width), jnp.float32), pltpu.VMEM((rows // CORES, width), jnp.bfloat16)]


def decoded(codes, dec):
    rows, features = codes.shape
    width = dec.shape[1]
    return pl.pallas_call(
        decode_kernel,
        out_shape=halves_of(rows, width),
        in_specs=[VMEM_SPEC] * 2,
        out_specs=[VMEM_SPEC] * 2,
        compiler_params=kernel_params(),
        cost_estimate=pl.CostEstimate(flops=2 * rows * width * features, bytes_accessed=2 * width * features, transcendentals=0),
        name="decode",
    )(*in_vmem(codes, dec))


def back(rows_ref, dec_ref):
    return summed_over(
        rows_ref.shape[1],
        lambda part: lax.dot_general(
            rows_ref[:, part], dec_ref[:, part], (((1,), (1,)), ((), ())), preferred_element_type=jnp.float32
        ),
    )


def grad_own_kernel(rows_ref, dec_ref, out_ref, _):
    out_ref[...] = back(rows_ref, dec_ref)


def grad_all_kernel(tokens, rows_ref, dec_ref, own_ref, out_ref):
    total = own_ref[...] + back(rows_ref, dec_ref)
    group = total.shape[0] // tokens
    for block in range(group):
        slab = slab_of(place_in(group), block, group // CORES)
        where = pl.ds(pl.multiple_of(slab * tokens, tokens), tokens)
        out_ref[0, where, :] = total[block * tokens : (block + 1) * tokens]


def grad_own(rows, dec):
    features = dec.shape[0]
    return pl.pallas_call(
        grad_own_kernel,
        out_shape=[pltpu.VMEM((rows.shape[0], features), jnp.float32), pltpu.VMEM((8, 128), jnp.float32)],
        in_specs=[VMEM_SPEC] * 2,
        out_specs=[VMEM_SPEC] * 2,
        compiler_params=kernel_params(),
        cost_estimate=pl.CostEstimate(flops=2 * rows.size * features, bytes_accessed=2 * dec.size, transcendentals=0),
        name="grad_own",
    )(*in_vmem(rows, dec))[0]


def grad_all(rows, dec, own, tokens):
    return pl.pallas_call(
        functools.partial(grad_all_kernel, tokens),
        out_shape=jax.ShapeDtypeStruct((1,) + own.shape, jnp.float32),
        in_specs=[VMEM_SPEC] * 3,
        out_specs=VMEM_SPEC,
        compiler_params=kernel_params(),
        cost_estimate=pl.CostEstimate(flops=2 * rows.size * own.shape[1], bytes_accessed=2 * dec.size, transcendentals=0),
        name="grad_all",
    )(*in_vmem(rows, dec, own))


def blocks_of(near, far, chips):
    rows = near.shape[0] // chips
    total = near + other_core(far).astype(jnp.float32)
    return [total[chip * rows : (chip + 1) * rows] for chip in range(chips)]


def summed(blocks, sent):
    total = blocks[0]
    for came in [across(blocks[chip].astype(jnp.bfloat16), chip, len(blocks)) for chip in sent]:
        total = total + came.astype(jnp.float32)
    return total


def on_device(resid, enc_weight, enc_bias, active, dec_weight, target):
    group = lax.axis_size(AXIS) // LAYERS
    chips = group // CORES
    index = lax.axis_index(AXIS)
    slab, first, final = lax.optimization_barrier((resid[0], index < group, index >= (LAYERS - 1) * group))
    tokens = resid.shape[1]
    enc, own_dec, next_dec = loaded(enc_weight, dec_weight)
    most, last = [across(slab, chip, chips) for chip in range(1, chips - 1)], across(slab, chips - 1, chips)
    early, late = jnp.concatenate([slab, last], axis=0), jnp.concatenate(most, axis=0)
    early_far, late_far = other_core(early), other_core(late)
    x = jnp.concatenate(
        [slab, late, last, early_far[:tokens], late_far, early_far[tokens:]], axis=0
    )
    gate, bias = gated(*after((active[0], enc_bias), enc), group * tokens, tokens)
    pre = jnp.dot(x, enc, preferred_element_type=jnp.float32) + bias
    codes = (jax.nn.relu(pre) * gate).astype(jnp.bfloat16)
    next_near, next_far = decoded(codes, next_dec)
    own_near, own_far = decoded(codes, own_dec)

    nexts = blocks_of(next_near, next_far, chips)
    owns = blocks_of(own_near, own_far, chips)
    risen = raised(nexts[-1].astype(jnp.bfloat16), first, group)
    owns[-1] = owns[-1] + risen.astype(jnp.float32)
    crossed = across(owns[-1].astype(jnp.bfloat16), chips - 1, chips).astype(jnp.float32)
    next_sum = after(summed(nexts, range(1, chips - 1)), owns[-1])
    own_less = summed(owns, range(1, chips - 1)) - target[0].astype(jnp.float32) + crossed

    below = shifted(next_sum.astype(jnp.bfloat16), group).astype(jnp.float32)
    above = lowered(own_less.astype(jnp.bfloat16), group).astype(jnp.float32)
    error = (own_less + below).astype(jnp.bfloat16)
    later = jnp.where(final, 0.0, next_sum + after(above, error)).astype(jnp.bfloat16)

    heres = [error] + [across(error, chip, chips) for chip in range(1, chips)]
    afters = [later] + [across(later, chip, chips) for chip in range(1, chips)]
    here_near = jnp.concatenate(heres, axis=0)
    here_far = other_core(here_near)
    here_rows = jnp.concatenate([here_near, here_far], axis=0)
    after_near = after(jnp.concatenate(afters, axis=0), here_far)
    after_rows = jnp.concatenate([after_near, other_core(after_near)], axis=0)
    grad = grad_all(after_rows, next_dec, grad_own(here_rows, own_dec), tokens)
    return (error[None], grad)


def solution(mesh):
    return jax.shard_map(
        on_device,
        mesh=mesh,
        in_specs=(
            P("layer", "groups", None),
            P("layer", None, None),
            P("layer", None),
            P("layer", "groups", None),
            P("layer", None, None, None),
            P("layer", "groups", None),
        ),
        out_specs=(P("layer", "groups", None), P("layer", "groups", None)),
        check_vma=False,
    )
```

```python
import functools

import jax
import jax.numpy as jnp
from jax import lax
from jax.experimental import pallas as pl
from jax.experimental.pallas import tpu as pltpu
from jax.sharding import PartitionSpec as P

BLOCK = 128
LAYERS = 4
TILE = 32
CORES = 2
CHUNK = 1024
LIMIT = 4 << 20
AXIS = "layer"

ANY_SPEC = pl.BlockSpec(memory_space=pl.ANY)
VMEM_SPEC = pl.BlockSpec(memory_space=pltpu.VMEM)


def turned(chip, chips):
    bits = chips.bit_length() - 1
    return sum(((chip >> bit) & 1) << (bits - 1 - bit) for bit in range(bits))


def across(value, chip, chips):
    masks = (CORES * chip, CORES * turned(chip, chips))
    pairs = [(i, i ^ masks[i % CORES]) for i in range(lax.axis_size(AXIS))]
    return lax.ppermute(value, AXIS, pairs)


def other_core(value):
    return lax.ppermute(value, AXIS, [(i, i ^ 1) for i in range(lax.axis_size(AXIS))])


def raised(value, first, group):
    size = lax.axis_size(AXIS)
    came = lax.ppermute(value, AXIS, [(i, (i + group) % size) for i in range(size)])
    return jnp.where(first, jnp.zeros_like(came), came)


def shifted(value, group):
    size = lax.axis_size(AXIS)
    return lax.ppermute(value, AXIS, [(i, i + group) for i in range(size - group)])


def lowered(value, group):
    size = lax.axis_size(AXIS)
    return lax.ppermute(value, AXIS, [(i + group, i) for i in range(size - group)])


def after(values, done):
    return lax.optimization_barrier((values, done))[0]


def slab_of(place, block, chips):
    far, chip = block // chips, block % chips
    odd = (place & 1) ^ far
    return place ^ (far + CORES * (chip * (1 - odd) + turned(chip, chips) * odd))


def in_vmem(*arrays):
    return [pltpu.with_memory_space_constraint(a, pltpu.VMEM) for a in arrays]


def in_hbm(*arrays):
    return [pltpu.with_memory_space_constraint(a, pltpu.HBM) for a in arrays]


def kernel_params(limit=LIMIT):
    return pltpu.CompilerParams(vmem_limit_bytes=limit)


def load_kernel(enc_hbm, dec_hbm, enc_ref, own_ref, next_ref, sems):
    pieces = [(enc_hbm.at[0], enc_ref), (dec_hbm.at[0, 1], next_ref), (dec_hbm.at[0, 0], own_ref)]
    copies = [pltpu.make_async_copy(source, target, sems.at[i]) for i, (source, target) in enumerate(pieces)]
    for copy in copies:
        copy.start()
    for copy in copies:
        copy.wait()


def loaded(enc, dec):
    block = pltpu.VMEM(dec.shape[2:], dec.dtype)
    return pl.pallas_call(
        load_kernel,
        out_shape=[pltpu.VMEM(enc.shape[1:], enc.dtype), block, block],
        in_specs=[ANY_SPEC] * 2,
        out_specs=[VMEM_SPEC] * 3,
        scratch_shapes=[pltpu.SemaphoreType.DMA((3,))],
        compiler_params=kernel_params(1 << 20),
        cost_estimate=pl.CostEstimate(flops=0, bytes_accessed=4 * (enc.size + dec.size), transcendentals=0),
        name="load_weights",
    )(*in_hbm(enc, dec))


def decode(codes, dec_ref, near_ref, far_ref):
    half, width = near_ref.shape
    for step in range(width // CHUNK):
        columns = pl.ds(step * CHUNK, CHUNK)
        part = jnp.dot(codes, dec_ref[:, columns], preferred_element_type=jnp.float32)
        near_ref[:, columns] = part[:half]
        far_ref[:, columns] = part[half:].astype(jnp.bfloat16)


def place_in(group):
    return lax.axis_index(AXIS) & (group - 1)


def summed_over(depth, product):
    sums = [None, None]
    for step in range(depth // CHUNK):
        part = product(pl.ds(step * CHUNK, CHUNK))
        so_far = sums[step % 2]
        sums[step % 2] = part if so_far is None else so_far + part
    return sums[0] + sums[1]


def gate_of(active_ref, rows, tokens):
    group = rows // tokens
    block = lax.broadcasted_iota(jnp.int32, (rows, BLOCK), 0) // tokens
    tile = (slab_of(place_in(group), block, group // CORES) * tokens) // TILE
    parts = []
    for part in range(active_ref.shape[1]):
        live = jnp.zeros((rows, BLOCK), jnp.int32)
        for i in range(active_ref.shape[0]):
            live = jnp.where(tile == i, active_ref[pl.ds(i, 1), pl.ds(part, 1)], live)
        parts.append(live.astype(jnp.float32))
    return jnp.concatenate(parts, axis=1)


def gate_kernel(tokens, active_ref, bias_ref, gate_ref, shift_ref):
    rows = gate_ref.shape[0]
    gate_ref[...] = gate_of(active_ref, rows, tokens)
    shift_ref[...] = jnp.broadcast_to(bias_ref[...].astype(jnp.float32), shift_ref.shape)


def gated(active, bias, rows, tokens):
    shape = (rows, bias.shape[1])
    return pl.pallas_call(
        functools.partial(gate_kernel, tokens),
        out_shape=[pltpu.VMEM(shape, jnp.float32)] * 2,
        in_specs=[VMEM_SPEC] * 2,
        out_specs=[VMEM_SPEC] * 2,
        compiler_params=kernel_params(),
        cost_estimate=pl.CostEstimate(flops=8 * rows * shape[1], bytes_accessed=8 * rows * shape[1], transcendentals=0),
        name="gate",
    )(*in_vmem(active, bias))


def decode_kernel(codes_ref, dec_ref, near_ref, far_ref):
    decode(codes_ref[...], dec_ref, near_ref, far_ref)


def halves_of(rows, width):
    return [pltpu.VMEM((rows // CORES, width), jnp.float32), pltpu.VMEM((rows // CORES, width), jnp.bfloat16)]


def decoded(codes, dec):
    rows, features = codes.shape
    width = dec.shape[1]
    return pl.pallas_call(
        decode_kernel,
        out_shape=halves_of(rows, width),
        in_specs=[VMEM_SPEC] * 2,
        out_specs=[VMEM_SPEC] * 2,
        compiler_params=kernel_params(),
        cost_estimate=pl.CostEstimate(flops=2 * rows * width * features, bytes_accessed=2 * width * features, transcendentals=0),
        name="decode",
    )(*in_vmem(codes, dec))


def back(rows_ref, dec_ref):
    return summed_over(
        rows_ref.shape[1],
        lambda part: lax.dot_general(
            rows_ref[:, part], dec_ref[:, part], (((1,), (1,)), ((), ())), preferred_element_type=jnp.float32
        ),
    )


def grad_own_kernel(rows_ref, dec_ref, out_ref, _):
    out_ref[...] = back(rows_ref, dec_ref)


def grad_all_kernel(tokens, rows_ref, dec_ref, own_ref, out_ref):
    total = own_ref[...] + back(rows_ref, dec_ref)
    group = total.shape[0] // tokens
    for block in range(group):
        slab = slab_of(place_in(group), block, group // CORES)
        where = pl.ds(pl.multiple_of(slab * tokens, tokens), tokens)
        out_ref[0, where, :] = total[block * tokens : (block + 1) * tokens]


def grad_own(rows, dec):
    features = dec.shape[0]
    return pl.pallas_call(
        grad_own_kernel,
        out_shape=[pltpu.VMEM((rows.shape[0], features), jnp.float32), pltpu.VMEM((8, 128), jnp.float32)],
        in_specs=[VMEM_SPEC] * 2,
        out_specs=[VMEM_SPEC] * 2,
        compiler_params=kernel_params(),
        cost_estimate=pl.CostEstimate(flops=2 * rows.size * features, bytes_accessed=2 * dec.size, transcendentals=0),
        name="grad_own",
    )(*in_vmem(rows, dec))[0]


def grad_all(rows, dec, own, tokens):
    return pl.pallas_call(
        functools.partial(grad_all_kernel, tokens),
        out_shape=jax.ShapeDtypeStruct((1,) + own.shape, jnp.float32),
        in_specs=[VMEM_SPEC] * 3,
        out_specs=VMEM_SPEC,
        compiler_params=kernel_params(),
        cost_estimate=pl.CostEstimate(flops=2 * rows.size * own.shape[1], bytes_accessed=2 * dec.size, transcendentals=0),
        name="grad_all",
    )(*in_vmem(rows, dec, own))


def blocks_of(near, far, chips):
    rows = near.shape[0] // chips
    total = near + other_core(far).astype(jnp.float32)
    return [total[chip * rows : (chip + 1) * rows] for chip in range(chips)]


def summed(blocks, sent):
    total = blocks[0]
    for came in [across(blocks[chip].astype(jnp.bfloat16), chip, len(blocks)) for chip in sent]:
        total = total + came.astype(jnp.float32)
    return total


def on_device(resid, enc_weight, enc_bias, active, dec_weight, target):
    group = lax.axis_size(AXIS) // LAYERS
    chips = group // CORES
    index = lax.axis_index(AXIS)
    slab, first, final = lax.optimization_barrier((resid[0], index < group, index >= (LAYERS - 1) * group))
    tokens = resid.shape[1]
    enc, own_dec, next_dec = loaded(enc_weight, dec_weight)
    pieces = jnp.concatenate([across(slab, chip, chips) for chip in range(chips - 1, 0, -1)], axis=0)
    pieces_far = other_core(pieces)
    rows = [after(slab, pieces)] + [pieces[i * tokens : (i + 1) * tokens] for i in range(chips - 1)][::-1]
    rows += [other_core(slab)] + [pieces_far[i * tokens : (i + 1) * tokens] for i in range(chips - 1)][::-1]
    x = jnp.concatenate(rows, axis=0)
    gate, bias = gated(*after((active[0], enc_bias), enc), group * tokens, tokens)
    pre = jnp.dot(x, enc, preferred_element_type=jnp.float32) + bias
    codes = (jax.nn.relu(pre) * gate).astype(jnp.bfloat16)
    next_near, next_far = decoded(codes, next_dec)
    own_near, own_far = decoded(codes, own_dec)

    nexts = blocks_of(next_near, next_far, chips)
    owns = blocks_of(own_near, own_far, chips)
    risen = raised(nexts[-1].astype(jnp.bfloat16), first, group)
    owns[-1] = owns[-1] + risen.astype(jnp.float32)
    crossed = across(owns[-1].astype(jnp.bfloat16), chips - 1, chips).astype(jnp.float32)
    next_sum = after(summed(nexts, range(1, chips - 1)), owns[-1])
    own_less = summed(owns, range(1, chips - 1)) - target[0].astype(jnp.float32) + crossed

    below = shifted(next_sum.astype(jnp.bfloat16), group).astype(jnp.float32)
    above = lowered(own_less.astype(jnp.bfloat16), group).astype(jnp.float32)
    error = (own_less + below).astype(jnp.bfloat16)
    later = jnp.where(final, 0.0, next_sum + after(above, error)).astype(jnp.bfloat16)

    heres = [error] + [across(error, chip, chips) for chip in range(1, chips)]
    afters = [later] + [across(later, chip, chips) for chip in range(1, chips - 1)]
    last = lowered(after(heres[-1], later), group)
    here_near = jnp.concatenate(heres, axis=0)
    here_far = other_core(here_near)
    here_rows = jnp.concatenate([here_near, here_far], axis=0)
    most = after(jnp.concatenate(afters, axis=0), here_far)
    after_rows = jnp.concatenate([most, last, other_core(most), other_core(last)], axis=0)
    grad = grad_all(after_rows, next_dec, grad_own(here_rows, own_dec), tokens)
    return (error[None], grad)


def solution(mesh):
    return jax.shard_map(
        on_device,
        mesh=mesh,
        in_specs=(
            P("layer", "groups", None),
            P("layer", None, None),
            P("layer", None),
            P("layer", "groups", None),
            P("layer", None, None, None),
            P("layer", "groups", None),
        ),
        out_specs=(P("layer", "groups", None), P("layer", "groups", None)),
        check_vma=False,
    )
```

```python
import functools

import jax
import jax.numpy as jnp
from jax import lax
from jax.experimental import pallas as pl
from jax.experimental.pallas import tpu as pltpu
from jax.sharding import PartitionSpec as P

BLOCK = 128
LAYERS = 4
TILE = 32
CORES = 2
CHUNK = 1024
LIMIT = 4 << 20
AXIS = "layer"

ANY_SPEC = pl.BlockSpec(memory_space=pl.ANY)
VMEM_SPEC = pl.BlockSpec(memory_space=pltpu.VMEM)


def turned(chip, chips):
    bits = chips.bit_length() - 1
    return sum(((chip >> bit) & 1) << (bits - 1 - bit) for bit in range(bits))


def across(value, chip, chips):
    masks = (CORES * chip, CORES * turned(chip, chips))
    pairs = [(i, i ^ masks[i % CORES]) for i in range(lax.axis_size(AXIS))]
    return lax.ppermute(value, AXIS, pairs)


def other_core(value):
    return lax.ppermute(value, AXIS, [(i, i ^ 1) for i in range(lax.axis_size(AXIS))])


def raised(value, first, group):
    size = lax.axis_size(AXIS)
    came = lax.ppermute(value, AXIS, [(i, (i + group) % size) for i in range(size)])
    return jnp.where(first, jnp.zeros_like(came), came)


def shifted(value, group):
    size = lax.axis_size(AXIS)
    return lax.ppermute(value, AXIS, [(i, i + group) for i in range(size - group)])


def lowered(value, group):
    size = lax.axis_size(AXIS)
    return lax.ppermute(value, AXIS, [(i + group, i) for i in range(size - group)])


def rotated_down(value, final, group):
    size = lax.axis_size(AXIS)
    came = lax.ppermute(value, AXIS, [((i + group) % size, i) for i in range(size)])
    return jnp.where(final, jnp.zeros_like(came), came)


def after(values, done):
    return lax.optimization_barrier((values, done))[0]


def slab_of(place, block, chips):
    far, chip = block // chips, block % chips
    odd = (place & 1) ^ far
    return place ^ (far + CORES * (chip * (1 - odd) + turned(chip, chips) * odd))


def in_vmem(*arrays):
    return [pltpu.with_memory_space_constraint(a, pltpu.VMEM) for a in arrays]


def in_hbm(*arrays):
    return [pltpu.with_memory_space_constraint(a, pltpu.HBM) for a in arrays]


def kernel_params(limit=LIMIT):
    return pltpu.CompilerParams(vmem_limit_bytes=limit)


def load_kernel(enc_hbm, dec_hbm, enc_ref, own_ref, next_ref, sems):
    pieces = [(enc_hbm.at[0], enc_ref), (dec_hbm.at[0, 1], next_ref), (dec_hbm.at[0, 0], own_ref)]
    copies = [pltpu.make_async_copy(source, target, sems.at[i]) for i, (source, target) in enumerate(pieces)]
    for copy in copies:
        copy.start()
    for copy in copies:
        copy.wait()


def loaded(enc, dec):
    block = pltpu.VMEM(dec.shape[2:], dec.dtype)
    return pl.pallas_call(
        load_kernel,
        out_shape=[pltpu.VMEM(enc.shape[1:], enc.dtype), block, block],
        in_specs=[ANY_SPEC] * 2,
        out_specs=[VMEM_SPEC] * 3,
        scratch_shapes=[pltpu.SemaphoreType.DMA((3,))],
        compiler_params=kernel_params(1 << 20),
        cost_estimate=pl.CostEstimate(flops=0, bytes_accessed=4 * (enc.size + dec.size), transcendentals=0),
        name="load_weights",
    )(*in_hbm(enc, dec))


def decode(codes, dec_ref, near_ref, far_ref):
    half, width = near_ref.shape
    for step in range(width // CHUNK):
        columns = pl.ds(step * CHUNK, CHUNK)
        part = jnp.dot(codes, dec_ref[:, columns], preferred_element_type=jnp.float32)
        near_ref[:, columns] = part[:half]
        far_ref[:, columns] = part[half:].astype(jnp.bfloat16)


def place_in(group):
    return lax.axis_index(AXIS) & (group - 1)


def summed_over(depth, product):
    sums = [None, None]
    for step in range(depth // CHUNK):
        part = product(pl.ds(step * CHUNK, CHUNK))
        so_far = sums[step % 2]
        sums[step % 2] = part if so_far is None else so_far + part
    return sums[0] + sums[1]


def gate_of(active_ref, rows, tokens):
    group = rows // tokens
    block = lax.broadcasted_iota(jnp.int32, (rows, BLOCK), 0) // tokens
    tile = (slab_of(place_in(group), block, group // CORES) * tokens) // TILE
    parts = []
    for part in range(active_ref.shape[1]):
        live = jnp.zeros((rows, BLOCK), jnp.int32)
        for i in range(active_ref.shape[0]):
            live = jnp.where(tile == i, active_ref[pl.ds(i, 1), pl.ds(part, 1)], live)
        parts.append(live.astype(jnp.float32))
    return jnp.concatenate(parts, axis=1)


def gate_kernel(tokens, active_ref, bias_ref, gate_ref, shift_ref):
    rows = gate_ref.shape[0]
    gate_ref[...] = gate_of(active_ref, rows, tokens)
    shift_ref[...] = jnp.broadcast_to(bias_ref[...].astype(jnp.float32), shift_ref.shape)


def gated(active, bias, rows, tokens):
    shape = (rows, bias.shape[1])
    return pl.pallas_call(
        functools.partial(gate_kernel, tokens),
        out_shape=[pltpu.VMEM(shape, jnp.float32)] * 2,
        in_specs=[VMEM_SPEC] * 2,
        out_specs=[VMEM_SPEC] * 2,
        compiler_params=kernel_params(),
        cost_estimate=pl.CostEstimate(flops=8 * rows * shape[1], bytes_accessed=8 * rows * shape[1], transcendentals=0),
        name="gate",
    )(*in_vmem(active, bias))


def decode_kernel(codes_ref, dec_ref, near_ref, far_ref):
    decode(codes_ref[...], dec_ref, near_ref, far_ref)


def halves_of(rows, width):
    return [pltpu.VMEM((rows // CORES, width), jnp.float32), pltpu.VMEM((rows // CORES, width), jnp.bfloat16)]


def decoded(codes, dec):
    rows, features = codes.shape
    width = dec.shape[1]
    return pl.pallas_call(
        decode_kernel,
        out_shape=halves_of(rows, width),
        in_specs=[VMEM_SPEC] * 2,
        out_specs=[VMEM_SPEC] * 2,
        compiler_params=kernel_params(),
        cost_estimate=pl.CostEstimate(flops=2 * rows * width * features, bytes_accessed=2 * width * features, transcendentals=0),
        name="decode",
    )(*in_vmem(codes, dec))


def back(rows_ref, dec_ref):
    return summed_over(
        rows_ref.shape[1],
        lambda part: lax.dot_general(
            rows_ref[:, part], dec_ref[:, part], (((1,), (1,)), ((), ())), preferred_element_type=jnp.float32
        ),
    )


def grad_own_kernel(rows_ref, dec_ref, out_ref, _):
    out_ref[...] = back(rows_ref, dec_ref)


def grad_all_kernel(tokens, rows_ref, dec_ref, own_ref, out_ref):
    total = own_ref[...] + back(rows_ref, dec_ref)
    group = total.shape[0] // tokens
    for block in range(group):
        chips = group // CORES
        label = (chips - block % chips) % chips
        slab = slab_of(place_in(group), block // chips * chips + label, chips)
        where = pl.ds(pl.multiple_of(slab * tokens, tokens), tokens)
        out_ref[0, where, :] = total[block * tokens : (block + 1) * tokens]


def grad_own(rows, dec):
    features = dec.shape[0]
    return pl.pallas_call(
        grad_own_kernel,
        out_shape=[pltpu.VMEM((rows.shape[0], features), jnp.float32), pltpu.VMEM((8, 128), jnp.float32)],
        in_specs=[VMEM_SPEC] * 2,
        out_specs=[VMEM_SPEC] * 2,
        compiler_params=kernel_params(),
        cost_estimate=pl.CostEstimate(flops=2 * rows.size * features, bytes_accessed=2 * dec.size, transcendentals=0),
        name="grad_own",
    )(*in_vmem(rows, dec))[0]


def grad_all(rows, dec, own, tokens):
    return pl.pallas_call(
        functools.partial(grad_all_kernel, tokens),
        out_shape=jax.ShapeDtypeStruct((1,) + own.shape, jnp.float32),
        in_specs=[VMEM_SPEC] * 3,
        out_specs=VMEM_SPEC,
        compiler_params=kernel_params(),
        cost_estimate=pl.CostEstimate(flops=2 * rows.size * own.shape[1], bytes_accessed=2 * dec.size, transcendentals=0),
        name="grad_all",
    )(*in_vmem(rows, dec, own))


def blocks_of(near, far, chips):
    rows = near.shape[0] // chips
    total = near + other_core(far).astype(jnp.float32)
    return [total[chip * rows : (chip + 1) * rows] for chip in range(chips)]


def summed(blocks, sent):
    total = blocks[0]
    for came in [across(blocks[chip].astype(jnp.bfloat16), chip, len(blocks)) for chip in sent]:
        total = total + came.astype(jnp.float32)
    return total


def on_device(resid, enc_weight, enc_bias, active, dec_weight, target):
    group = lax.axis_size(AXIS) // LAYERS
    chips = group // CORES
    index = lax.axis_index(AXIS)
    slab, first, final = lax.optimization_barrier((resid[0], index < group, index >= (LAYERS - 1) * group))
    tokens = resid.shape[1]
    enc, own_dec, next_dec = loaded(enc_weight, dec_weight)
    pieces = jnp.concatenate([across(slab, chip, chips) for chip in range(chips - 1, 0, -1)], axis=0)
    pieces_far = other_core(pieces)
    rows = [after(slab, pieces)] + [pieces[i * tokens : (i + 1) * tokens] for i in range(chips - 1)][::-1]
    rows += [other_core(slab)] + [pieces_far[i * tokens : (i + 1) * tokens] for i in range(chips - 1)][::-1]
    x = jnp.concatenate(rows, axis=0)
    gate, bias = gated(*after((active[0], enc_bias), enc), group * tokens, tokens)
    pre = jnp.dot(x, enc, preferred_element_type=jnp.float32) + bias
    codes = (jax.nn.relu(pre) * gate).astype(jnp.bfloat16)
    next_near, next_far = decoded(codes, next_dec)
    own_near, own_far = decoded(codes, own_dec)

    nexts = blocks_of(next_near, next_far, chips)
    owns = blocks_of(own_near, own_far, chips)
    risen = raised(nexts[-1].astype(jnp.bfloat16), first, group)
    owns[-1] = owns[-1] + risen.astype(jnp.float32)
    crossed = across(owns[-1].astype(jnp.bfloat16), chips - 1, chips).astype(jnp.float32)
    next_sum = after(summed(nexts, range(1, chips - 1)), owns[-1])
    own_less = summed(owns, range(1, chips - 1)) - target[0].astype(jnp.float32) + crossed

    below = shifted(next_sum.astype(jnp.bfloat16), group).astype(jnp.float32)
    above = lowered(own_less.astype(jnp.bfloat16), group).astype(jnp.float32)
    error = (own_less + below).astype(jnp.bfloat16)
    later = jnp.where(final, 0.0, next_sum + after(above, error)).astype(jnp.bfloat16)

    heres = [error] + [across(error, chip, chips) for chip in range(chips - 1, 0, -1)]
    passed = rotated_down(after(heres[-1], later), final, group)
    here_near = jnp.concatenate(heres, axis=0)
    here_far = other_core(here_near)
    here_rows = jnp.concatenate([here_near, here_far], axis=0)
    straight = [across(later, chip, chips) for chip in range(chips - 1, 1, -1)]
    most = after(jnp.concatenate([later] + straight, axis=0), here_far)
    after_rows = jnp.concatenate([most, passed, other_core(most), other_core(passed)], axis=0)
    grad = grad_all(after_rows, next_dec, grad_own(here_rows, own_dec), tokens)
    return (error[None], grad)


def solution(mesh):
    return jax.shard_map(
        on_device,
        mesh=mesh,
        in_specs=(
            P("layer", "groups", None),
            P("layer", None, None),
            P("layer", None),
            P("layer", "groups", None),
            P("layer", None, None, None),
            P("layer", "groups", None),
        ),
        out_specs=(P("layer", "groups", None), P("layer", "groups", None)),
        check_vma=False,
    )
```

```python
import functools

import jax
import jax.numpy as jnp
from jax import lax
from jax.experimental import pallas as pl
from jax.experimental.pallas import tpu as pltpu
from jax.sharding import PartitionSpec as P

BLOCK = 128
LAYERS = 4
TILE = 32
CORES = 2
CHUNK = 1024
LIMIT = 4 << 20
AXIS = "layer"

ANY_SPEC = pl.BlockSpec(memory_space=pl.ANY)
VMEM_SPEC = pl.BlockSpec(memory_space=pltpu.VMEM)


def turned(chip, chips):
    bits = chips.bit_length() - 1
    return sum(((chip >> bit) & 1) << (bits - 1 - bit) for bit in range(bits))


def across(value, chip, chips):
    masks = (CORES * chip, CORES * turned(chip, chips))
    pairs = [(i, i ^ masks[i % CORES]) for i in range(lax.axis_size(AXIS))]
    return lax.ppermute(value, AXIS, pairs)


def other_core(value):
    return lax.ppermute(value, AXIS, [(i, i ^ 1) for i in range(lax.axis_size(AXIS))])


def raised(value, first, group):
    size = lax.axis_size(AXIS)
    came = lax.ppermute(value, AXIS, [(i, (i + group) % size) for i in range(size)])
    return jnp.where(first, jnp.zeros_like(came), came)


def shifted(value, group):
    size = lax.axis_size(AXIS)
    return lax.ppermute(value, AXIS, [(i, i + group) for i in range(size - group)])


def lowered(value, group):
    size = lax.axis_size(AXIS)
    return lax.ppermute(value, AXIS, [(i + group, i) for i in range(size - group)])


def rotated_down(value, final, group):
    size = lax.axis_size(AXIS)
    came = lax.ppermute(value, AXIS, [((i + group) % size, i) for i in range(size)])
    return jnp.where(final, jnp.zeros_like(came), came)


def after(values, done):
    return lax.optimization_barrier((values, done))[0]


def slab_of(place, block, chips):
    far, chip = block // chips, block % chips
    odd = (place & 1) ^ far
    return place ^ (far + CORES * (chip * (1 - odd) + turned(chip, chips) * odd))


def in_vmem(*arrays):
    return [pltpu.with_memory_space_constraint(a, pltpu.VMEM) for a in arrays]


def in_hbm(*arrays):
    return [pltpu.with_memory_space_constraint(a, pltpu.HBM) for a in arrays]


def kernel_params(limit=LIMIT):
    return pltpu.CompilerParams(vmem_limit_bytes=limit)


def load_kernel(enc_hbm, dec_hbm, enc_ref, own_ref, next_ref, sems):
    pieces = [(enc_hbm.at[0], enc_ref), (dec_hbm.at[0, 1], next_ref), (dec_hbm.at[0, 0], own_ref)]
    copies = [pltpu.make_async_copy(source, target, sems.at[i]) for i, (source, target) in enumerate(pieces)]
    for copy in copies:
        copy.start()
    for copy in copies:
        copy.wait()


def loaded(enc, dec):
    block = pltpu.VMEM(dec.shape[2:], dec.dtype)
    return pl.pallas_call(
        load_kernel,
        out_shape=[pltpu.VMEM(enc.shape[1:], enc.dtype), block, block],
        in_specs=[ANY_SPEC] * 2,
        out_specs=[VMEM_SPEC] * 3,
        scratch_shapes=[pltpu.SemaphoreType.DMA((3,))],
        compiler_params=kernel_params(1 << 20),
        cost_estimate=pl.CostEstimate(flops=0, bytes_accessed=4 * (enc.size + dec.size), transcendentals=0),
        name="load_weights",
    )(*in_hbm(enc, dec))


def decode(codes, dec_ref, near_ref, far_ref):
    half, width = near_ref.shape
    for step in range(width // CHUNK):
        columns = pl.ds(step * CHUNK, CHUNK)
        part = jnp.dot(codes, dec_ref[:, columns], preferred_element_type=jnp.float32)
        near_ref[:, columns] = part[:half]
        far_ref[:, columns] = part[half:].astype(jnp.bfloat16)


def place_in(group):
    return lax.axis_index(AXIS) & (group - 1)


def summed_over(depth, product):
    sums = [None, None]
    for step in range(depth // CHUNK):
        part = product(pl.ds(step * CHUNK, CHUNK))
        so_far = sums[step % 2]
        sums[step % 2] = part if so_far is None else so_far + part
    return sums[0] + sums[1]


def gate_of(active_ref, rows, tokens):
    group = rows // tokens
    block = lax.broadcasted_iota(jnp.int32, (rows, BLOCK), 0) // tokens
    tile = (slab_of(place_in(group), block, group // CORES) * tokens) // TILE
    parts = []
    for part in range(active_ref.shape[1]):
        live = jnp.zeros((rows, BLOCK), jnp.int32)
        for i in range(active_ref.shape[0]):
            live = jnp.where(tile == i, active_ref[pl.ds(i, 1), pl.ds(part, 1)], live)
        parts.append(live.astype(jnp.float32))
    return jnp.concatenate(parts, axis=1)


def gate_kernel(tokens, active_ref, bias_ref, gate_ref, shift_ref):
    rows = gate_ref.shape[0]
    gate_ref[...] = gate_of(active_ref, rows, tokens)
    shift_ref[...] = jnp.broadcast_to(bias_ref[...].astype(jnp.float32), shift_ref.shape)


def gated(active, bias, rows, tokens):
    shape = (rows, bias.shape[1])
    return pl.pallas_call(
        functools.partial(gate_kernel, tokens),
        out_shape=[pltpu.VMEM(shape, jnp.float32)] * 2,
        in_specs=[VMEM_SPEC] * 2,
        out_specs=[VMEM_SPEC] * 2,
        compiler_params=kernel_params(),
        cost_estimate=pl.CostEstimate(flops=8 * rows * shape[1], bytes_accessed=8 * rows * shape[1], transcendentals=0),
        name="gate",
    )(*in_vmem(active, bias))


def decode_kernel(codes_ref, dec_ref, near_ref, far_ref):
    decode(codes_ref[...], dec_ref, near_ref, far_ref)


def halves_of(rows, width):
    return [pltpu.VMEM((rows // CORES, width), jnp.float32), pltpu.VMEM((rows // CORES, width), jnp.bfloat16)]


def decoded(codes, dec):
    rows, features = codes.shape
    width = dec.shape[1]
    return pl.pallas_call(
        decode_kernel,
        out_shape=halves_of(rows, width),
        in_specs=[VMEM_SPEC] * 2,
        out_specs=[VMEM_SPEC] * 2,
        compiler_params=kernel_params(),
        cost_estimate=pl.CostEstimate(flops=2 * rows * width * features, bytes_accessed=2 * width * features, transcendentals=0),
        name="decode",
    )(*in_vmem(codes, dec))


def back(rows_ref, dec_ref):
    return summed_over(
        rows_ref.shape[1],
        lambda part: lax.dot_general(
            rows_ref[:, part], dec_ref[:, part], (((1,), (1,)), ((), ())), preferred_element_type=jnp.float32
        ),
    )


def grad_own_kernel(rows_ref, dec_ref, out_ref, _):
    out_ref[...] = back(rows_ref, dec_ref)


def grad_all_kernel(tokens, rows_ref, dec_ref, own_ref, out_ref):
    total = own_ref[...] + back(rows_ref, dec_ref)
    group = total.shape[0] // tokens
    for block in range(group):
        chips = group // CORES
        row = block % chips
        label = row % (chips - 1) + 1 if row else 0
        slab = slab_of(place_in(group), block // chips * chips + label, chips)
        where = pl.ds(pl.multiple_of(slab * tokens, tokens), tokens)
        out_ref[0, where, :] = total[block * tokens : (block + 1) * tokens]


def grad_own(rows, dec):
    features = dec.shape[0]
    return pl.pallas_call(
        grad_own_kernel,
        out_shape=[pltpu.VMEM((rows.shape[0], features), jnp.float32), pltpu.VMEM((8, 128), jnp.float32)],
        in_specs=[VMEM_SPEC] * 2,
        out_specs=[VMEM_SPEC] * 2,
        compiler_params=kernel_params(),
        cost_estimate=pl.CostEstimate(flops=2 * rows.size * features, bytes_accessed=2 * dec.size, transcendentals=0),
        name="grad_own",
    )(*in_vmem(rows, dec))[0]


def grad_all(rows, dec, own, tokens):
    return pl.pallas_call(
        functools.partial(grad_all_kernel, tokens),
        out_shape=jax.ShapeDtypeStruct((1,) + own.shape, jnp.float32),
        in_specs=[VMEM_SPEC] * 3,
        out_specs=VMEM_SPEC,
        compiler_params=kernel_params(),
        cost_estimate=pl.CostEstimate(flops=2 * rows.size * own.shape[1], bytes_accessed=2 * dec.size, transcendentals=0),
        name="grad_all",
    )(*in_vmem(rows, dec, own))


def blocks_of(near, far, chips):
    rows = near.shape[0] // chips
    total = near + other_core(far).astype(jnp.float32)
    return [total[chip * rows : (chip + 1) * rows] for chip in range(chips)]


def summed(blocks, sent):
    total = blocks[0]
    for came in [across(blocks[chip].astype(jnp.bfloat16), chip, len(blocks)) for chip in sent]:
        total = total + came.astype(jnp.float32)
    return total


def on_device(resid, enc_weight, enc_bias, active, dec_weight, target):
    group = lax.axis_size(AXIS) // LAYERS
    chips = group // CORES
    index = lax.axis_index(AXIS)
    slab, first, final = lax.optimization_barrier((resid[0], index < group, index >= (LAYERS - 1) * group))
    tokens = resid.shape[1]
    enc, own_dec, next_dec = loaded(enc_weight, dec_weight)
    pieces = jnp.concatenate([across(slab, chip, chips) for chip in range(chips - 1, 0, -1)], axis=0)
    pieces_far = other_core(pieces)
    rows = [after(slab, pieces)] + [pieces[i * tokens : (i + 1) * tokens] for i in range(chips - 1)][::-1]
    rows += [other_core(slab)] + [pieces_far[i * tokens : (i + 1) * tokens] for i in range(chips - 1)][::-1]
    x = jnp.concatenate(rows, axis=0)
    gate, bias = gated(*after((active[0], enc_bias), enc), group * tokens, tokens)
    pre = jnp.dot(x, enc, preferred_element_type=jnp.float32) + bias
    codes = (jax.nn.relu(pre) * gate).astype(jnp.bfloat16)
    next_near, next_far = decoded(codes, next_dec)
    own_near, own_far = decoded(codes, own_dec)

    nexts = blocks_of(next_near, next_far, chips)
    owns = blocks_of(own_near, own_far, chips)
    risen = raised(nexts[1].astype(jnp.bfloat16), first, group)
    owns[1] = owns[1] + risen.astype(jnp.float32)
    crossed = across(owns[1].astype(jnp.bfloat16), 1, chips).astype(jnp.float32)
    next_sum = after(summed(nexts, range(2, chips)), owns[1])
    own_less = summed(owns, range(2, chips)) - target[0].astype(jnp.float32) + crossed

    below = shifted(next_sum.astype(jnp.bfloat16), group).astype(jnp.float32)
    above = lowered(own_less.astype(jnp.bfloat16), group).astype(jnp.float32)
    error = (own_less + below).astype(jnp.bfloat16)
    later = jnp.where(final, 0.0, next_sum + after(above, error)).astype(jnp.bfloat16)

    heres = [error] + [across(error, chip, chips) for chip in [*range(2, chips), 1]]
    passed = rotated_down(after(heres[-1], later), final, group)
    here_near = jnp.concatenate(heres, axis=0)
    here_far = other_core(here_near)
    here_rows = jnp.concatenate([here_near, here_far], axis=0)
    straight = [across(later, chip, chips) for chip in range(2, chips)]
    most = after(jnp.concatenate([later] + straight, axis=0), here_far)
    after_rows = jnp.concatenate([most, passed, other_core(most), other_core(passed)], axis=0)
    grad = grad_all(after_rows, next_dec, grad_own(here_rows, own_dec), tokens)
    return (error[None], grad)


def solution(mesh):
    return jax.shard_map(
        on_device,
        mesh=mesh,
        in_specs=(
            P("layer", "groups", None),
            P("layer", None, None),
            P("layer", None),
            P("layer", "groups", None),
            P("layer", None, None, None),
            P("layer", "groups", None),
        ),
        out_specs=(P("layer", "groups", None), P("layer", "groups", None)),
        check_vma=False,
    )
```

```python
import functools

import jax
import jax.numpy as jnp
from jax import lax
from jax.experimental import pallas as pl
from jax.experimental.pallas import tpu as pltpu
from jax.sharding import PartitionSpec as P

BLOCK = 128
LAYERS = 4
TILE = 32
CORES = 2
CHUNK = 1024
LIMIT = 4 << 20
AXIS = "layer"

ANY_SPEC = pl.BlockSpec(memory_space=pl.ANY)
VMEM_SPEC = pl.BlockSpec(memory_space=pltpu.VMEM)


def turned(chip, chips):
    bits = chips.bit_length() - 1
    return sum(((chip >> bit) & 1) << (bits - 1 - bit) for bit in range(bits))


def across(value, chip, chips):
    masks = (CORES * chip, CORES * turned(chip, chips))
    pairs = [(i, i ^ masks[i % CORES]) for i in range(lax.axis_size(AXIS))]
    return lax.ppermute(value, AXIS, pairs)


def other_core(value):
    return lax.ppermute(value, AXIS, [(i, i ^ 1) for i in range(lax.axis_size(AXIS))])


def raised(value, first, group):
    size = lax.axis_size(AXIS)
    came = lax.ppermute(value, AXIS, [(i, (i + group) % size) for i in range(size)])
    return jnp.where(first, jnp.zeros_like(came), came)


def shifted(value, group):
    size = lax.axis_size(AXIS)
    return lax.ppermute(value, AXIS, [(i, i + group) for i in range(size - group)])


def lowered(value, group):
    size = lax.axis_size(AXIS)
    return lax.ppermute(value, AXIS, [(i + group, i) for i in range(size - group)])


def rotated_down(value, final, group):
    size = lax.axis_size(AXIS)
    came = lax.ppermute(value, AXIS, [((i + group) % size, i) for i in range(size)])
    return jnp.where(final, jnp.zeros_like(came), came)


def after(values, done):
    return lax.optimization_barrier((values, done))[0]


def slab_of(place, block, chips):
    far, chip = block // chips, block % chips
    odd = (place & 1) ^ far
    return place ^ (far + CORES * (chip * (1 - odd) + turned(chip, chips) * odd))


def in_vmem(*arrays):
    return [pltpu.with_memory_space_constraint(a, pltpu.VMEM) for a in arrays]


def in_hbm(*arrays):
    return [pltpu.with_memory_space_constraint(a, pltpu.HBM) for a in arrays]


def kernel_params(limit=LIMIT):
    return pltpu.CompilerParams(vmem_limit_bytes=limit)


def load_kernel(enc_hbm, dec_hbm, enc_ref, own_ref, next_ref, sems):
    pieces = [(enc_hbm.at[0], enc_ref), (dec_hbm.at[0, 1], next_ref), (dec_hbm.at[0, 0], own_ref)]
    copies = [pltpu.make_async_copy(source, target, sems.at[i]) for i, (source, target) in enumerate(pieces)]
    for copy in copies:
        copy.start()
    for copy in copies:
        copy.wait()


def loaded(enc, dec):
    block = pltpu.VMEM(dec.shape[2:], dec.dtype)
    return pl.pallas_call(
        load_kernel,
        out_shape=[pltpu.VMEM(enc.shape[1:], enc.dtype), block, block],
        in_specs=[ANY_SPEC] * 2,
        out_specs=[VMEM_SPEC] * 3,
        scratch_shapes=[pltpu.SemaphoreType.DMA((3,))],
        compiler_params=kernel_params(1 << 20),
        cost_estimate=pl.CostEstimate(flops=0, bytes_accessed=4 * (enc.size + dec.size), transcendentals=0),
        name="load_weights",
    )(*in_hbm(enc, dec))


def decode(codes, dec_ref, near_ref, far_ref):
    half, width = near_ref.shape
    for step in range(width // CHUNK):
        columns = pl.ds(step * CHUNK, CHUNK)
        part = jnp.dot(codes, dec_ref[:, columns], preferred_element_type=jnp.float32)
        near_ref[:, columns] = part[:half]
        far_ref[:, columns] = part[half:].astype(jnp.bfloat16)


def place_in(group):
    return lax.axis_index(AXIS) & (group - 1)


def summed_over(depth, product):
    sums = [None, None]
    for step in range(depth // CHUNK):
        part = product(pl.ds(step * CHUNK, CHUNK))
        so_far = sums[step % 2]
        sums[step % 2] = part if so_far is None else so_far + part
    return sums[0] + sums[1]


def gate_of(active_ref, rows, tokens):
    group = rows // tokens
    block = lax.broadcasted_iota(jnp.int32, (rows, BLOCK), 0) // tokens
    tile = (slab_of(place_in(group), block, group // CORES) * tokens) // TILE
    parts = []
    for part in range(active_ref.shape[1]):
        live = jnp.zeros((rows, BLOCK), jnp.int32)
        for i in range(active_ref.shape[0]):
            live = jnp.where(tile == i, active_ref[pl.ds(i, 1), pl.ds(part, 1)], live)
        parts.append(live.astype(jnp.float32))
    return jnp.concatenate(parts, axis=1)


def gate_kernel(tokens, active_ref, bias_ref, gate_ref, shift_ref):
    rows = gate_ref.shape[0]
    gate_ref[...] = gate_of(active_ref, rows, tokens)
    shift_ref[...] = jnp.broadcast_to(bias_ref[...].astype(jnp.float32), shift_ref.shape)


def gated(active, bias, rows, tokens):
    shape = (rows, bias.shape[1])
    return pl.pallas_call(
        functools.partial(gate_kernel, tokens),
        out_shape=[pltpu.VMEM(shape, jnp.float32)] * 2,
        in_specs=[VMEM_SPEC] * 2,
        out_specs=[VMEM_SPEC] * 2,
        compiler_params=kernel_params(),
        cost_estimate=pl.CostEstimate(flops=8 * rows * shape[1], bytes_accessed=8 * rows * shape[1], transcendentals=0),
        name="gate",
    )(*in_vmem(active, bias))


def decode_kernel(codes_ref, dec_ref, near_ref, far_ref):
    decode(codes_ref[...], dec_ref, near_ref, far_ref)


def halves_of(rows, width):
    return [pltpu.VMEM((rows // CORES, width), jnp.float32), pltpu.VMEM((rows // CORES, width), jnp.bfloat16)]


def decoded(codes, dec):
    rows, features = codes.shape
    width = dec.shape[1]
    return pl.pallas_call(
        decode_kernel,
        out_shape=halves_of(rows, width),
        in_specs=[VMEM_SPEC] * 2,
        out_specs=[VMEM_SPEC] * 2,
        compiler_params=kernel_params(),
        cost_estimate=pl.CostEstimate(flops=2 * rows * width * features, bytes_accessed=2 * width * features, transcendentals=0),
        name="decode",
    )(*in_vmem(codes, dec))


def back(rows_ref, dec_ref):
    return summed_over(
        rows_ref.shape[1],
        lambda part: lax.dot_general(
            rows_ref[:, part], dec_ref[:, part], (((1,), (1,)), ((), ())), preferred_element_type=jnp.float32
        ),
    )


def grad_own_kernel(rows_ref, dec_ref, out_ref, _):
    out_ref[...] = back(rows_ref, dec_ref)


def grad_all_kernel(tokens, rows_ref, dec_ref, own_ref, out_ref):
    total = own_ref[...] + back(rows_ref, dec_ref)
    group = total.shape[0] // tokens
    for block in range(group):
        chips = group // CORES
        row = block % chips
        label = row % (chips - 1) + 1 if row else 0
        slab = slab_of(place_in(group), block // chips * chips + label, chips)
        where = pl.ds(pl.multiple_of(slab * tokens, tokens), tokens)
        out_ref[0, where, :] = total[block * tokens : (block + 1) * tokens]


def grad_own(rows, dec):
    features = dec.shape[0]
    return pl.pallas_call(
        grad_own_kernel,
        out_shape=[pltpu.VMEM((rows.shape[0], features), jnp.float32), pltpu.VMEM((8, 128), jnp.float32)],
        in_specs=[VMEM_SPEC] * 2,
        out_specs=[VMEM_SPEC] * 2,
        compiler_params=kernel_params(),
        cost_estimate=pl.CostEstimate(flops=2 * rows.size * features, bytes_accessed=2 * dec.size, transcendentals=0),
        name="grad_own",
    )(*in_vmem(rows, dec))[0]


def grad_all(rows, dec, own, tokens):
    return pl.pallas_call(
        functools.partial(grad_all_kernel, tokens),
        out_shape=jax.ShapeDtypeStruct((1,) + own.shape, jnp.float32),
        in_specs=[VMEM_SPEC] * 3,
        out_specs=VMEM_SPEC,
        compiler_params=kernel_params(),
        cost_estimate=pl.CostEstimate(flops=2 * rows.size * own.shape[1], bytes_accessed=2 * dec.size, transcendentals=0),
        name="grad_all",
    )(*in_vmem(rows, dec, own))


def blocks_of(near, far, chips):
    rows = near.shape[0] // chips
    total = near + other_core(far).astype(jnp.float32)
    return [total[chip * rows : (chip + 1) * rows] for chip in range(chips)]


def summed(blocks, sent):
    total = blocks[0]
    for came in [across(blocks[chip].astype(jnp.bfloat16), chip, len(blocks)) for chip in sent]:
        total = total + came.astype(jnp.float32)
    return total


def on_device(resid, enc_weight, enc_bias, active, dec_weight, target):
    group = lax.axis_size(AXIS) // LAYERS
    chips = group // CORES
    index = lax.axis_index(AXIS)
    slab, first, final = lax.optimization_barrier((resid[0], index < group, index >= (LAYERS - 1) * group))
    tokens = resid.shape[1]
    enc, own_dec, next_dec = loaded(enc_weight, dec_weight)
    pieces = jnp.concatenate([across(slab, chip, chips) for chip in range(chips - 1, 0, -1)], axis=0)
    pieces_far = other_core(pieces)
    rows = [after(slab, pieces)] + [pieces[i * tokens : (i + 1) * tokens] for i in range(chips - 1)][::-1]
    rows += [other_core(slab)] + [pieces_far[i * tokens : (i + 1) * tokens] for i in range(chips - 1)][::-1]
    x = jnp.concatenate(rows, axis=0)
    gate, bias = gated(*after((active[0], enc_bias), enc), group * tokens, tokens)
    pre = jnp.dot(x, enc, preferred_element_type=jnp.float32) + bias
    codes = (jax.nn.relu(pre) * gate).astype(jnp.bfloat16)
    next_near, next_far = decoded(codes, next_dec)
    own_near, own_far = decoded(codes, own_dec)

    nexts = blocks_of(next_near, next_far, chips)
    owns = blocks_of(own_near, own_far, chips)
    risen = raised(nexts[-1].astype(jnp.bfloat16), first, group)
    owns[-1] = owns[-1] + risen.astype(jnp.float32)
    crossed = across(owns[-1].astype(jnp.bfloat16), chips - 1, chips).astype(jnp.float32)
    next_sum = after(summed(nexts, range(1, chips - 1)), owns[-1])
    own_less = summed(owns, range(1, chips - 1)) - target[0].astype(jnp.float32) + crossed

    below = shifted(next_sum.astype(jnp.bfloat16), group).astype(jnp.float32)
    above = lowered(own_less.astype(jnp.bfloat16), group).astype(jnp.float32)
    error = (own_less + below).astype(jnp.bfloat16)
    later = jnp.where(final, 0.0, next_sum + after(above, error)).astype(jnp.bfloat16)

    pieces = {}
    for chip in range(1, chips):
        top = 1 << (chip.bit_length() - 1)
        pieces[chip] = across(pieces.get(chip - top, error), top, chips)
    heres = [error] + [pieces[chip] for chip in [*range(2, chips), 1]]
    passed = rotated_down(after(heres[-1], later), final, group)
    here_near = jnp.concatenate(heres, axis=0)
    here_far = other_core(here_near)
    here_rows = jnp.concatenate([here_near, here_far], axis=0)
    straight = [across(later, chip, chips) for chip in range(2, chips)]
    most = after(jnp.concatenate([later] + straight, axis=0), here_far)
    passed = after(passed, here_near)
    after_rows = jnp.concatenate([most, passed, other_core(most), other_core(passed)], axis=0)
    grad = grad_all(after_rows, next_dec, grad_own(here_rows, own_dec), tokens)
    return (error[None], grad)


def solution(mesh):
    return jax.shard_map(
        on_device,
        mesh=mesh,
        in_specs=(
            P("layer", "groups", None),
            P("layer", None, None),
            P("layer", None),
            P("layer", "groups", None),
            P("layer", None, None, None),
            P("layer", "groups", None),
        ),
        out_specs=(P("layer", "groups", None), P("layer", "groups", None)),
        check_vma=False,
    )
```

```python
import functools

import jax
import jax.numpy as jnp
from jax import lax
from jax.experimental import pallas as pl
from jax.experimental.pallas import tpu as pltpu
from jax.sharding import PartitionSpec as P

BLOCK = 128
LAYERS = 4
TILE = 32
CORES = 2
CHUNK = 1024
LIMIT = 4 << 20
AXIS = "layer"

ANY_SPEC = pl.BlockSpec(memory_space=pl.ANY)
VMEM_SPEC = pl.BlockSpec(memory_space=pltpu.VMEM)


def turned(chip, chips):
    bits = chips.bit_length() - 1
    return sum(((chip >> bit) & 1) << (bits - 1 - bit) for bit in range(bits))


def across(value, chip, chips):
    masks = (CORES * chip, CORES * turned(chip, chips))
    pairs = [(i, i ^ masks[i % CORES]) for i in range(lax.axis_size(AXIS))]
    return lax.ppermute(value, AXIS, pairs)


def other_core(value):
    return lax.ppermute(value, AXIS, [(i, i ^ 1) for i in range(lax.axis_size(AXIS))])


def raised(value, first, group):
    size = lax.axis_size(AXIS)
    came = lax.ppermute(value, AXIS, [(i, (i + group) % size) for i in range(size)])
    return jnp.where(first, jnp.zeros_like(came), came)


def shifted(value, group):
    size = lax.axis_size(AXIS)
    return lax.ppermute(value, AXIS, [(i, i + group) for i in range(size - group)])


def lowered(value, group):
    size = lax.axis_size(AXIS)
    return lax.ppermute(value, AXIS, [(i + group, i) for i in range(size - group)])


def rotated_down(value, group):
    size = lax.axis_size(AXIS)
    return lax.ppermute(value, AXIS, [((i + group) % size, i) for i in range(size)])


def after(values, done):
    return lax.optimization_barrier((values, done))[0]


def slab_of(place, block, chips):
    far, chip = block // chips, block % chips
    odd = (place & 1) ^ far
    return place ^ (far + CORES * (chip * (1 - odd) + turned(chip, chips) * odd))


def in_vmem(*arrays):
    return [pltpu.with_memory_space_constraint(a, pltpu.VMEM) for a in arrays]


def in_hbm(*arrays):
    return [pltpu.with_memory_space_constraint(a, pltpu.HBM) for a in arrays]


def kernel_params(limit=LIMIT):
    return pltpu.CompilerParams(vmem_limit_bytes=limit)


def load_kernel(enc_hbm, dec_hbm, enc_ref, own_ref, next_ref, sems):
    pieces = [(enc_hbm.at[0], enc_ref), (dec_hbm.at[0, 1], next_ref), (dec_hbm.at[0, 0], own_ref)]
    copies = [pltpu.make_async_copy(source, target, sems.at[i]) for i, (source, target) in enumerate(pieces)]
    for copy in copies:
        copy.start()
    for copy in copies:
        copy.wait()


def loaded(enc, dec):
    block = pltpu.VMEM(dec.shape[2:], dec.dtype)
    return pl.pallas_call(
        load_kernel,
        out_shape=[pltpu.VMEM(enc.shape[1:], enc.dtype), block, block],
        in_specs=[ANY_SPEC] * 2,
        out_specs=[VMEM_SPEC] * 3,
        scratch_shapes=[pltpu.SemaphoreType.DMA((3,))],
        compiler_params=kernel_params(1 << 20),
        cost_estimate=pl.CostEstimate(flops=0, bytes_accessed=4 * (enc.size + dec.size), transcendentals=0),
        name="load_weights",
    )(*in_hbm(enc, dec))


def decode(codes, dec_ref, near_ref, far_ref):
    half, width = near_ref.shape
    for step in range(width // CHUNK):
        columns = pl.ds(step * CHUNK, CHUNK)
        part = jnp.dot(codes, dec_ref[:, columns], preferred_element_type=jnp.float32)
        near_ref[:, columns] = part[:half]
        far_ref[:, columns] = part[half:].astype(jnp.bfloat16)


def place_in(group):
    return lax.axis_index(AXIS) & (group - 1)


def summed_over(depth, product):
    sums = [None, None]
    for step in range(depth // CHUNK):
        part = product(pl.ds(step * CHUNK, CHUNK))
        so_far = sums[step % 2]
        sums[step % 2] = part if so_far is None else so_far + part
    return sums[0] + sums[1]


def gate_of(active_ref, rows, tokens):
    group = rows // tokens
    block = lax.broadcasted_iota(jnp.int32, (rows, BLOCK), 0) // tokens
    tile = (slab_of(place_in(group), block, group // CORES) * tokens) // TILE
    parts = []
    for part in range(active_ref.shape[1]):
        live = jnp.zeros((rows, BLOCK), jnp.int32)
        for i in range(active_ref.shape[0]):
            live = jnp.where(tile == i, active_ref[pl.ds(i, 1), pl.ds(part, 1)], live)
        parts.append(live.astype(jnp.float32))
    return jnp.concatenate(parts, axis=1)


def gate_kernel(tokens, active_ref, bias_ref, gate_ref, shift_ref):
    rows = gate_ref.shape[0]
    gate_ref[...] = gate_of(active_ref, rows, tokens)
    shift_ref[...] = jnp.broadcast_to(bias_ref[...].astype(jnp.float32), shift_ref.shape)


def gated(active, bias, rows, tokens):
    shape = (rows, bias.shape[1])
    return pl.pallas_call(
        functools.partial(gate_kernel, tokens),
        out_shape=[pltpu.VMEM(shape, jnp.float32)] * 2,
        in_specs=[VMEM_SPEC] * 2,
        out_specs=[VMEM_SPEC] * 2,
        compiler_params=kernel_params(),
        cost_estimate=pl.CostEstimate(flops=8 * rows * shape[1], bytes_accessed=8 * rows * shape[1], transcendentals=0),
        name="gate",
    )(*in_vmem(active, bias))


def decode_kernel(codes_ref, dec_ref, near_ref, far_ref):
    decode(codes_ref[...], dec_ref, near_ref, far_ref)


def halves_of(rows, width):
    return [pltpu.VMEM((rows // CORES, width), jnp.float32), pltpu.VMEM((rows // CORES, width), jnp.bfloat16)]


def decoded(codes, dec):
    rows, features = codes.shape
    width = dec.shape[1]
    return pl.pallas_call(
        decode_kernel,
        out_shape=halves_of(rows, width),
        in_specs=[VMEM_SPEC] * 2,
        out_specs=[VMEM_SPEC] * 2,
        compiler_params=kernel_params(),
        cost_estimate=pl.CostEstimate(flops=2 * rows * width * features, bytes_accessed=2 * width * features, transcendentals=0),
        name="decode",
    )(*in_vmem(codes, dec))


def back(rows_ref, dec_ref):
    return summed_over(
        rows_ref.shape[1],
        lambda part: lax.dot_general(
            rows_ref[:, part], dec_ref[:, part], (((1,), (1,)), ((), ())), preferred_element_type=jnp.float32
        ),
    )


def grad_own_kernel(rows_ref, dec_ref, out_ref, _):
    out_ref[...] = back(rows_ref, dec_ref)


def grad_all_kernel(tokens, rows_ref, dec_ref, own_ref, out_ref):
    total = own_ref[...] + back(rows_ref, dec_ref)
    group = total.shape[0] // tokens
    for block in range(group):
        chips = group // CORES
        row = block % chips
        label = row % (chips - 1) + 1 if row else 0
        slab = slab_of(place_in(group), block // chips * chips + label, chips)
        where = pl.ds(pl.multiple_of(slab * tokens, tokens), tokens)
        out_ref[0, where, :] = total[block * tokens : (block + 1) * tokens]


def grad_own(rows, dec):
    features = dec.shape[0]
    return pl.pallas_call(
        grad_own_kernel,
        out_shape=[pltpu.VMEM((rows.shape[0], features), jnp.float32), pltpu.VMEM((8, 128), jnp.float32)],
        in_specs=[VMEM_SPEC] * 2,
        out_specs=[VMEM_SPEC] * 2,
        compiler_params=kernel_params(),
        cost_estimate=pl.CostEstimate(flops=2 * rows.size * features, bytes_accessed=2 * dec.size, transcendentals=0),
        name="grad_own",
    )(*in_vmem(rows, dec))[0]


def grad_all(rows, dec, own, tokens):
    return pl.pallas_call(
        functools.partial(grad_all_kernel, tokens),
        out_shape=jax.ShapeDtypeStruct((1,) + own.shape, jnp.float32),
        in_specs=[VMEM_SPEC] * 3,
        out_specs=VMEM_SPEC,
        compiler_params=kernel_params(),
        cost_estimate=pl.CostEstimate(flops=2 * rows.size * own.shape[1], bytes_accessed=2 * dec.size, transcendentals=0),
        name="grad_all",
    )(*in_vmem(rows, dec, own))


def blocks_of(near, far, chips):
    rows = near.shape[0] // chips
    total = near + other_core(far).astype(jnp.float32)
    return [total[chip * rows : (chip + 1) * rows] for chip in range(chips)]


def summed(blocks, sent):
    total = blocks[0]
    for came in [across(blocks[chip].astype(jnp.bfloat16), chip, len(blocks)) for chip in sent]:
        total = total + came.astype(jnp.float32)
    return total


def on_device(resid, enc_weight, enc_bias, active, dec_weight, target):
    group = lax.axis_size(AXIS) // LAYERS
    chips = group // CORES
    index = lax.axis_index(AXIS)
    slab, first, final = lax.optimization_barrier((resid[0], index < group, index >= (LAYERS - 1) * group))
    tokens = resid.shape[1]
    enc, own_dec, next_dec = loaded(enc_weight, dec_weight)
    pieces = jnp.concatenate([across(slab, chip, chips) for chip in range(chips - 1, 0, -1)], axis=0)
    pieces_far = other_core(pieces)
    rows = [after(slab, pieces)] + [pieces[i * tokens : (i + 1) * tokens] for i in range(chips - 1)][::-1]
    rows += [other_core(slab)] + [pieces_far[i * tokens : (i + 1) * tokens] for i in range(chips - 1)][::-1]
    x = jnp.concatenate(rows, axis=0)
    gate, bias = gated(*after((active[0], enc_bias), enc), group * tokens, tokens)
    pre = jnp.dot(x, enc, preferred_element_type=jnp.float32) + bias
    codes = (jax.nn.relu(pre) * gate).astype(jnp.bfloat16)
    next_near, next_far = decoded(codes, next_dec)
    own_near, own_far = decoded(codes, own_dec)

    nexts = blocks_of(next_near, next_far, chips)
    owns = blocks_of(own_near, own_far, chips)
    risen = raised(nexts[-1].astype(jnp.bfloat16), first, group)
    owns[-1] = owns[-1] + risen.astype(jnp.float32)
    crossed = across(owns[-1].astype(jnp.bfloat16), chips - 1, chips).astype(jnp.float32)
    next_sum = after(summed(nexts, range(1, chips - 1)), owns[-1])
    own_less = summed(owns, range(1, chips - 1)) - target[0].astype(jnp.float32) + crossed

    below = shifted(next_sum.astype(jnp.bfloat16), group).astype(jnp.float32)
    above = lowered(own_less.astype(jnp.bfloat16), group).astype(jnp.float32)
    error = (own_less + below).astype(jnp.bfloat16)
    later = jnp.where(final, 0.0, next_sum + after(above, error)).astype(jnp.bfloat16)

    heres = [error] + [across(error, chip, chips) for chip in [*range(2, chips), 1]]
    passed = rotated_down(after(heres[-1], later), group)
    here_near = jnp.concatenate(heres, axis=0)
    here_far = other_core(here_near)
    here_rows = jnp.concatenate([here_near, here_far], axis=0)
    straight = [across(later, chip, chips) for chip in range(2, chips)]
    most = after(jnp.concatenate([later] + straight, axis=0), here_far)
    own_grad = grad_own(here_rows, own_dec)
    most_far = other_core(most)
    passed = jnp.where(final, jnp.zeros_like(passed), after(passed, (own_grad, most_far)))
    after_rows = jnp.concatenate([most, passed, most_far, other_core(passed)], axis=0)
    grad = grad_all(after_rows, next_dec, own_grad, tokens)
    return (error[None], grad)


def solution(mesh):
    return jax.shard_map(
        on_device,
        mesh=mesh,
        in_specs=(
            P("layer", "groups", None),
            P("layer", None, None),
            P("layer", None),
            P("layer", "groups", None),
            P("layer", None, None, None),
            P("layer", "groups", None),
        ),
        out_specs=(P("layer", "groups", None), P("layer", "groups", None)),
        check_vma=False,
    )
```

```python
import functools

import jax
import jax.numpy as jnp
from jax import lax
from jax.experimental import pallas as pl
from jax.experimental.pallas import tpu as pltpu
from jax.sharding import PartitionSpec as P

BLOCK = 128
LAYERS = 4
TILE = 32
CORES = 2
CHUNK = 1024
LIMIT = 4 << 20
AXIS = "layer"

ANY_SPEC = pl.BlockSpec(memory_space=pl.ANY)
VMEM_SPEC = pl.BlockSpec(memory_space=pltpu.VMEM)


def turned(chip, chips):
    bits = chips.bit_length() - 1
    return sum(((chip >> bit) & 1) << (bits - 1 - bit) for bit in range(bits))


def across(value, chip, chips):
    masks = (CORES * chip, CORES * turned(chip, chips))
    pairs = [(i, i ^ masks[i % CORES]) for i in range(lax.axis_size(AXIS))]
    return lax.ppermute(value, AXIS, pairs)


def other_core(value):
    return lax.ppermute(value, AXIS, [(i, i ^ 1) for i in range(lax.axis_size(AXIS))])


def raised(value, first, group):
    size = lax.axis_size(AXIS)
    came = lax.ppermute(value, AXIS, [(i, (i + group) % size) for i in range(size)])
    return jnp.where(first, jnp.zeros_like(came), came)


def shifted(value, group):
    size = lax.axis_size(AXIS)
    return lax.ppermute(value, AXIS, [(i, i + group) for i in range(size - group)])


def lowered(value, final, group):
    size = lax.axis_size(AXIS)
    came = lax.ppermute(value, AXIS, [((i + group) % size, i) for i in range(size)])
    return jnp.where(final, jnp.zeros_like(came), came)


def rotated_down(value, final, group):
    size = lax.axis_size(AXIS)
    came = lax.ppermute(value, AXIS, [((i + group) % size, i) for i in range(size)])
    return jnp.where(final, jnp.zeros_like(came), came)


def after(values, done):
    return lax.optimization_barrier((values, done))[0]


def slab_of(place, block, chips):
    far, chip = block // chips, block % chips
    odd = (place & 1) ^ far
    return place ^ (far + CORES * (chip * (1 - odd) + turned(chip, chips) * odd))


def in_vmem(*arrays):
    return [pltpu.with_memory_space_constraint(a, pltpu.VMEM) for a in arrays]


def in_hbm(*arrays):
    return [pltpu.with_memory_space_constraint(a, pltpu.HBM) for a in arrays]


def kernel_params(limit=LIMIT):
    return pltpu.CompilerParams(vmem_limit_bytes=limit)


def load_kernel(enc_hbm, dec_hbm, enc_ref, own_ref, next_ref, sems):
    pieces = [(enc_hbm.at[0], enc_ref), (dec_hbm.at[0, 1], next_ref), (dec_hbm.at[0, 0], own_ref)]
    copies = [pltpu.make_async_copy(source, target, sems.at[i]) for i, (source, target) in enumerate(pieces)]
    for copy in copies:
        copy.start()
    for copy in copies:
        copy.wait()


def loaded(enc, dec):
    block = pltpu.VMEM(dec.shape[2:], dec.dtype)
    return pl.pallas_call(
        load_kernel,
        out_shape=[pltpu.VMEM(enc.shape[1:], enc.dtype), block, block],
        in_specs=[ANY_SPEC] * 2,
        out_specs=[VMEM_SPEC] * 3,
        scratch_shapes=[pltpu.SemaphoreType.DMA((3,))],
        compiler_params=kernel_params(1 << 20),
        cost_estimate=pl.CostEstimate(flops=0, bytes_accessed=4 * (enc.size + dec.size), transcendentals=0),
        name="load_weights",
    )(*in_hbm(enc, dec))


def decode(codes, dec_ref, near_ref, far_ref):
    half, width = near_ref.shape
    for step in range(width // CHUNK):
        columns = pl.ds(step * CHUNK, CHUNK)
        part = jnp.dot(codes, dec_ref[:, columns], preferred_element_type=jnp.float32)
        near_ref[:, columns] = part[:half]
        far_ref[:, columns] = part[half:].astype(jnp.bfloat16)


def place_in(group):
    return lax.axis_index(AXIS) & (group - 1)


def summed_over(depth, product):
    sums = [None, None]
    for step in range(depth // CHUNK):
        part = product(pl.ds(step * CHUNK, CHUNK))
        so_far = sums[step % 2]
        sums[step % 2] = part if so_far is None else so_far + part
    return sums[0] + sums[1]


def gate_of(active_ref, rows, tokens):
    group = rows // tokens
    block = lax.broadcasted_iota(jnp.int32, (rows, BLOCK), 0) // tokens
    tile = (slab_of(place_in(group), block, group // CORES) * tokens) // TILE
    parts = []
    for part in range(active_ref.shape[1]):
        live = jnp.zeros((rows, BLOCK), jnp.int32)
        for i in range(active_ref.shape[0]):
            live = jnp.where(tile == i, active_ref[pl.ds(i, 1), pl.ds(part, 1)], live)
        parts.append(live.astype(jnp.float32))
    return jnp.concatenate(parts, axis=1)


def gate_kernel(tokens, active_ref, bias_ref, gate_ref, shift_ref):
    rows = gate_ref.shape[0]
    gate_ref[...] = gate_of(active_ref, rows, tokens)
    shift_ref[...] = jnp.broadcast_to(bias_ref[...].astype(jnp.float32), shift_ref.shape)


def gated(active, bias, rows, tokens):
    shape = (rows, bias.shape[1])
    return pl.pallas_call(
        functools.partial(gate_kernel, tokens),
        out_shape=[pltpu.VMEM(shape, jnp.float32)] * 2,
        in_specs=[VMEM_SPEC] * 2,
        out_specs=[VMEM_SPEC] * 2,
        compiler_params=kernel_params(),
        cost_estimate=pl.CostEstimate(flops=8 * rows * shape[1], bytes_accessed=8 * rows * shape[1], transcendentals=0),
        name="gate",
    )(*in_vmem(active, bias))


def decode_kernel(codes_ref, dec_ref, near_ref, far_ref):
    decode(codes_ref[...], dec_ref, near_ref, far_ref)


def halves_of(rows, width):
    return [pltpu.VMEM((rows // CORES, width), jnp.float32), pltpu.VMEM((rows // CORES, width), jnp.bfloat16)]


def decoded(codes, dec):
    rows, features = codes.shape
    width = dec.shape[1]
    return pl.pallas_call(
        decode_kernel,
        out_shape=halves_of(rows, width),
        in_specs=[VMEM_SPEC] * 2,
        out_specs=[VMEM_SPEC] * 2,
        compiler_params=kernel_params(),
        cost_estimate=pl.CostEstimate(flops=2 * rows * width * features, bytes_accessed=2 * width * features, transcendentals=0),
        name="decode",
    )(*in_vmem(codes, dec))


def back(rows_ref, dec_ref):
    return summed_over(
        rows_ref.shape[1],
        lambda part: lax.dot_general(
            rows_ref[:, part], dec_ref[:, part], (((1,), (1,)), ((), ())), preferred_element_type=jnp.float32
        ),
    )


def grad_own_kernel(rows_ref, dec_ref, out_ref, _):
    out_ref[...] = back(rows_ref, dec_ref)


def grad_all_kernel(tokens, rows_ref, dec_ref, own_ref, out_ref):
    total = own_ref[...] + back(rows_ref, dec_ref)
    group = total.shape[0] // tokens
    for block in range(group):
        chips = group // CORES
        label = (chips - block % chips) % chips
        slab = slab_of(place_in(group), block // chips * chips + label, chips)
        where = pl.ds(pl.multiple_of(slab * tokens, tokens), tokens)
        out_ref[0, where, :] = total[block * tokens : (block + 1) * tokens]


def grad_own(rows, dec):
    features = dec.shape[0]
    return pl.pallas_call(
        grad_own_kernel,
        out_shape=[pltpu.VMEM((rows.shape[0], features), jnp.float32), pltpu.VMEM((8, 128), jnp.float32)],
        in_specs=[VMEM_SPEC] * 2,
        out_specs=[VMEM_SPEC] * 2,
        compiler_params=kernel_params(),
        cost_estimate=pl.CostEstimate(flops=2 * rows.size * features, bytes_accessed=2 * dec.size, transcendentals=0),
        name="grad_own",
    )(*in_vmem(rows, dec))[0]


def grad_all(rows, dec, own, tokens):
    return pl.pallas_call(
        functools.partial(grad_all_kernel, tokens),
        out_shape=jax.ShapeDtypeStruct((1,) + own.shape, jnp.float32),
        in_specs=[VMEM_SPEC] * 3,
        out_specs=VMEM_SPEC,
        compiler_params=kernel_params(),
        cost_estimate=pl.CostEstimate(flops=2 * rows.size * own.shape[1], bytes_accessed=2 * dec.size, transcendentals=0),
        name="grad_all",
    )(*in_vmem(rows, dec, own))


def blocks_of(near, far, chips):
    rows = near.shape[0] // chips
    total = near + other_core(far).astype(jnp.float32)
    return [total[chip * rows : (chip + 1) * rows] for chip in range(chips)]


def summed(blocks, sent):
    total = blocks[0]
    for came in [across(blocks[chip].astype(jnp.bfloat16), chip, len(blocks)) for chip in sent]:
        total = total + came.astype(jnp.float32)
    return total


def on_device(resid, enc_weight, enc_bias, active, dec_weight, target):
    group = lax.axis_size(AXIS) // LAYERS
    chips = group // CORES
    index = lax.axis_index(AXIS)
    slab, first, final = lax.optimization_barrier((resid[0], index < group, index >= (LAYERS - 1) * group))
    tokens = resid.shape[1]
    enc, own_dec, next_dec = loaded(enc_weight, dec_weight)
    pieces = jnp.concatenate([across(slab, chip, chips) for chip in range(chips - 1, 0, -1)], axis=0)
    pieces_far = other_core(pieces)
    rows = [after(slab, pieces)] + [pieces[i * tokens : (i + 1) * tokens] for i in range(chips - 1)][::-1]
    rows += [other_core(slab)] + [pieces_far[i * tokens : (i + 1) * tokens] for i in range(chips - 1)][::-1]
    x = jnp.concatenate(rows, axis=0)
    gate, bias = gated(*after((active[0], enc_bias), enc), group * tokens, tokens)
    pre = jnp.dot(x, enc, preferred_element_type=jnp.float32) + bias
    codes = (jax.nn.relu(pre) * gate).astype(jnp.bfloat16)
    next_near, next_far = decoded(codes, next_dec)
    own_near, own_far = decoded(codes, own_dec)

    nexts = blocks_of(next_near, next_far, chips)
    owns = blocks_of(own_near, own_far, chips)
    risen = raised(nexts[-1].astype(jnp.bfloat16), first, group)
    owns[-1] = owns[-1] + risen.astype(jnp.float32)
    crossed = across(owns[-1].astype(jnp.bfloat16), chips - 1, chips).astype(jnp.float32)
    next_sum = after(summed(nexts, range(1, chips - 1)), owns[-1])
    own_less = summed(owns, range(1, chips - 1)) - target[0].astype(jnp.float32) + crossed

    below = shifted(next_sum.astype(jnp.bfloat16), group).astype(jnp.float32)
    above = lowered(own_less.astype(jnp.bfloat16), final, group).astype(jnp.float32)
    error = (own_less + below).astype(jnp.bfloat16)
    later = jnp.where(final, 0.0, next_sum + after(above, error)).astype(jnp.bfloat16)

    heres = [error] + [across(error, chip, chips) for chip in range(chips - 1, 0, -1)]
    passed = rotated_down(after(heres[-1], later), final, group)
    here_near = jnp.concatenate(heres, axis=0)
    here_far = other_core(here_near)
    here_rows = jnp.concatenate([here_near, here_far], axis=0)
    straight = [across(later, chip, chips) for chip in range(chips - 1, 1, -1)]
    most = after(jnp.concatenate([later] + straight, axis=0), here_far)
    after_rows = jnp.concatenate([most, passed, other_core(most), other_core(passed)], axis=0)
    grad = grad_all(after_rows, next_dec, grad_own(here_rows, own_dec), tokens)
    return (error[None], grad)


def solution(mesh):
    return jax.shard_map(
        on_device,
        mesh=mesh,
        in_specs=(
            P("layer", "groups", None),
            P("layer", None, None),
            P("layer", None),
            P("layer", "groups", None),
            P("layer", None, None, None),
            P("layer", "groups", None),
        ),
        out_specs=(P("layer", "groups", None), P("layer", "groups", None)),
        check_vma=False,
    )
```

```python
import functools

import jax
import jax.numpy as jnp
from jax import lax
from jax.experimental import pallas as pl
from jax.experimental.pallas import tpu as pltpu
from jax.sharding import PartitionSpec as P

BLOCK = 128
LAYERS = 4
TILE = 32
CORES = 2
CHUNK = 1024
LIMIT = 4 << 20
AXIS = "layer"

ANY_SPEC = pl.BlockSpec(memory_space=pl.ANY)
VMEM_SPEC = pl.BlockSpec(memory_space=pltpu.VMEM)


def turned(chip, chips):
    bits = chips.bit_length() - 1
    return sum(((chip >> bit) & 1) << (bits - 1 - bit) for bit in range(bits))


def across(value, chip, chips):
    masks = (CORES * chip, CORES * turned(chip, chips))
    pairs = [(i, i ^ masks[i % CORES]) for i in range(lax.axis_size(AXIS))]
    return lax.ppermute(value, AXIS, pairs)


def other_core(value):
    return lax.ppermute(value, AXIS, [(i, i ^ 1) for i in range(lax.axis_size(AXIS))])


def raised(value, first, group):
    size = lax.axis_size(AXIS)
    came = lax.ppermute(value, AXIS, [(i, (i + group) % size) for i in range(size)])
    return jnp.where(first, jnp.zeros_like(came), came)


def shifted(value, group):
    size = lax.axis_size(AXIS)
    return lax.ppermute(value, AXIS, [(i, i + group) for i in range(size - group)])


def lowered(value, final, group):
    size = lax.axis_size(AXIS)
    came = lax.ppermute(value, AXIS, [((i + group) % size, i) for i in range(size)])
    return jnp.where(final, jnp.zeros_like(came), came)


def rotated_down(value, final, group):
    size = lax.axis_size(AXIS)
    came = lax.ppermute(value, AXIS, [((i + group) % size, i) for i in range(size)])
    return jnp.where(final, jnp.zeros_like(came), came)


def after(values, done):
    return lax.optimization_barrier((values, done))[0]


def slab_of(place, block, chips):
    far, chip = block // chips, block % chips
    odd = (place & 1) ^ far
    return place ^ (far + CORES * (chip * (1 - odd) + turned(chip, chips) * odd))


def in_vmem(*arrays):
    return [pltpu.with_memory_space_constraint(a, pltpu.VMEM) for a in arrays]


def in_hbm(*arrays):
    return [pltpu.with_memory_space_constraint(a, pltpu.HBM) for a in arrays]


def kernel_params(limit=LIMIT):
    return pltpu.CompilerParams(vmem_limit_bytes=limit)


def load_kernel(enc_hbm, dec_hbm, enc_ref, own_ref, next_ref, sems):
    pieces = [(enc_hbm.at[0], enc_ref), (dec_hbm.at[0, 1], next_ref), (dec_hbm.at[0, 0], own_ref)]
    copies = [pltpu.make_async_copy(source, target, sems.at[i]) for i, (source, target) in enumerate(pieces)]
    for copy in copies:
        copy.start()
    for copy in copies:
        copy.wait()


def loaded(enc, dec):
    block = pltpu.VMEM(dec.shape[2:], dec.dtype)
    return pl.pallas_call(
        load_kernel,
        out_shape=[pltpu.VMEM(enc.shape[1:], enc.dtype), block, block],
        in_specs=[ANY_SPEC] * 2,
        out_specs=[VMEM_SPEC] * 3,
        scratch_shapes=[pltpu.SemaphoreType.DMA((3,))],
        compiler_params=kernel_params(1 << 20),
        cost_estimate=pl.CostEstimate(flops=0, bytes_accessed=4 * (enc.size + dec.size), transcendentals=0),
        name="load_weights",
    )(*in_hbm(enc, dec))


def decode(codes, dec_ref, near_ref, far_ref):
    half, width = near_ref.shape
    for step in range(width // CHUNK):
        columns = pl.ds(step * CHUNK, CHUNK)
        part = jnp.dot(codes, dec_ref[:, columns], preferred_element_type=jnp.float32)
        near_ref[:, columns] = part[:half]
        far_ref[:, columns] = part[half:].astype(jnp.bfloat16)


def place_in(group):
    return lax.axis_index(AXIS) & (group - 1)


def summed_over(depth, product):
    sums = [None, None]
    for step in range(depth // CHUNK):
        part = product(pl.ds(step * CHUNK, CHUNK))
        so_far = sums[step % 2]
        sums[step % 2] = part if so_far is None else so_far + part
    return sums[0] + sums[1]


def gate_of(active_ref, rows, tokens):
    group = rows // tokens
    block = lax.broadcasted_iota(jnp.int32, (rows, BLOCK), 0) // tokens
    tile = (slab_of(place_in(group), block, group // CORES) * tokens) // TILE
    parts = []
    for part in range(active_ref.shape[1]):
        live = jnp.zeros((rows, BLOCK), jnp.int32)
        for i in range(active_ref.shape[0]):
            live = jnp.where(tile == i, active_ref[pl.ds(i, 1), pl.ds(part, 1)], live)
        parts.append(live.astype(jnp.float32))
    return jnp.concatenate(parts, axis=1)


def gate_kernel(tokens, active_ref, bias_ref, gate_ref, shift_ref):
    rows = gate_ref.shape[0]
    gate_ref[...] = gate_of(active_ref, rows, tokens)
    shift_ref[...] = jnp.broadcast_to(bias_ref[...].astype(jnp.float32), shift_ref.shape)


def gated(active, bias, rows, tokens):
    shape = (rows, bias.shape[1])
    return pl.pallas_call(
        functools.partial(gate_kernel, tokens),
        out_shape=[pltpu.VMEM(shape, jnp.float32)] * 2,
        in_specs=[VMEM_SPEC] * 2,
        out_specs=[VMEM_SPEC] * 2,
        compiler_params=kernel_params(),
        cost_estimate=pl.CostEstimate(flops=8 * rows * shape[1], bytes_accessed=8 * rows * shape[1], transcendentals=0),
        name="gate",
    )(*in_vmem(active, bias))


def decode_kernel(codes_ref, dec_ref, near_ref, far_ref):
    decode(codes_ref[...], dec_ref, near_ref, far_ref)


def halves_of(rows, width):
    return [pltpu.VMEM((rows // CORES, width), jnp.float32), pltpu.VMEM((rows // CORES, width), jnp.bfloat16)]


def decoded(codes, dec):
    rows, features = codes.shape
    width = dec.shape[1]
    return pl.pallas_call(
        decode_kernel,
        out_shape=halves_of(rows, width),
        in_specs=[VMEM_SPEC] * 2,
        out_specs=[VMEM_SPEC] * 2,
        compiler_params=kernel_params(),
        cost_estimate=pl.CostEstimate(flops=2 * rows * width * features, bytes_accessed=2 * width * features, transcendentals=0),
        name="decode",
    )(*in_vmem(codes, dec))


def back(rows_ref, dec_ref):
    return summed_over(
        rows_ref.shape[1],
        lambda part: lax.dot_general(
            rows_ref[:, part], dec_ref[:, part], (((1,), (1,)), ((), ())), preferred_element_type=jnp.float32
        ),
    )


def grad_own_kernel(rows_ref, dec_ref, out_ref, _):
    out_ref[...] = back(rows_ref, dec_ref)


def grad_all_kernel(tokens, rows_ref, dec_ref, own_ref, out_ref):
    total = own_ref[...] + back(rows_ref, dec_ref)
    group = total.shape[0] // tokens
    for block in range(group):
        chips = group // CORES
        row = block % chips
        label = row % (chips - 1) + 1 if row else 0
        slab = slab_of(place_in(group), block // chips * chips + label, chips)
        where = pl.ds(pl.multiple_of(slab * tokens, tokens), tokens)
        out_ref[0, where, :] = total[block * tokens : (block + 1) * tokens]


def grad_own(rows, dec):
    features = dec.shape[0]
    return pl.pallas_call(
        grad_own_kernel,
        out_shape=[pltpu.VMEM((rows.shape[0], features), jnp.float32), pltpu.VMEM((8, 128), jnp.float32)],
        in_specs=[VMEM_SPEC] * 2,
        out_specs=[VMEM_SPEC] * 2,
        compiler_params=kernel_params(),
        cost_estimate=pl.CostEstimate(flops=2 * rows.size * features, bytes_accessed=2 * dec.size, transcendentals=0),
        name="grad_own",
    )(*in_vmem(rows, dec))[0]


def grad_all(rows, dec, own, tokens):
    return pl.pallas_call(
        functools.partial(grad_all_kernel, tokens),
        out_shape=jax.ShapeDtypeStruct((1,) + own.shape, jnp.float32),
        in_specs=[VMEM_SPEC] * 3,
        out_specs=VMEM_SPEC,
        compiler_params=kernel_params(),
        cost_estimate=pl.CostEstimate(flops=2 * rows.size * own.shape[1], bytes_accessed=2 * dec.size, transcendentals=0),
        name="grad_all",
    )(*in_vmem(rows, dec, own))


def blocks_of(near, far, chips):
    rows = near.shape[0] // chips
    total = near + other_core(far).astype(jnp.float32)
    return [total[chip * rows : (chip + 1) * rows] for chip in range(chips)]


def summed(blocks, sent):
    total = blocks[0]
    for came in [across(blocks[chip].astype(jnp.bfloat16), chip, len(blocks)) for chip in sent]:
        total = total + came.astype(jnp.float32)
    return total


def on_device(resid, enc_weight, enc_bias, active, dec_weight, target):
    group = lax.axis_size(AXIS) // LAYERS
    chips = group // CORES
    index = lax.axis_index(AXIS)
    slab, first, final = lax.optimization_barrier((resid[0], index < group, index >= (LAYERS - 1) * group))
    tokens = resid.shape[1]
    enc, own_dec, next_dec = loaded(enc_weight, dec_weight)
    pieces = jnp.concatenate([across(slab, chip, chips) for chip in range(chips - 1, 0, -1)], axis=0)
    pieces_far = other_core(pieces)
    rows = [after(slab, pieces)] + [pieces[i * tokens : (i + 1) * tokens] for i in range(chips - 1)][::-1]
    rows += [other_core(slab)] + [pieces_far[i * tokens : (i + 1) * tokens] for i in range(chips - 1)][::-1]
    x = jnp.concatenate(rows, axis=0)
    gate, bias = gated(*after((active[0], enc_bias), enc), group * tokens, tokens)
    pre = jnp.dot(x, enc, preferred_element_type=jnp.float32) + bias
    codes = (jax.nn.relu(pre) * gate).astype(jnp.bfloat16)
    next_near, next_far = decoded(codes, next_dec)
    own_near, own_far = decoded(codes, own_dec)

    nexts = blocks_of(next_near, next_far, chips)
    owns = blocks_of(own_near, own_far, chips)
    risen = raised(nexts[-1].astype(jnp.bfloat16), first, group)
    owns[-1] = owns[-1] + risen.astype(jnp.float32)
    crossed = across(owns[-1].astype(jnp.bfloat16), chips - 1, chips).astype(jnp.float32)
    next_sum = after(summed(nexts, range(1, chips - 1)), owns[-1])
    own_less = summed(owns, range(1, chips - 1)) - target[0].astype(jnp.float32) + crossed

    below = shifted(next_sum.astype(jnp.bfloat16), group).astype(jnp.float32)
    above = lowered(own_less.astype(jnp.bfloat16), final, group).astype(jnp.float32)
    error = (own_less + below).astype(jnp.bfloat16)
    later = jnp.where(final, 0.0, next_sum + after(above, error)).astype(jnp.bfloat16)

    heres = [error] + [across(error, chip, chips) for chip in [*range(2, chips), 1]]
    passed = rotated_down(after(heres[-1], later), final, group)
    here_near = jnp.concatenate(heres, axis=0)
    here_far = other_core(here_near)
    here_rows = jnp.concatenate([here_near, here_far], axis=0)
    straight = [across(later, chip, chips) for chip in range(2, chips)]
    most = after(jnp.concatenate([later] + straight, axis=0), here_far)
    after_rows = jnp.concatenate([most, passed, other_core(most), other_core(passed)], axis=0)
    grad = grad_all(after_rows, next_dec, grad_own(here_rows, own_dec), tokens)
    return (error[None], grad)


def solution(mesh):
    return jax.shard_map(
        on_device,
        mesh=mesh,
        in_specs=(
            P("layer", "groups", None),
            P("layer", None, None),
            P("layer", None),
            P("layer", "groups", None),
            P("layer", None, None, None),
            P("layer", "groups", None),
        ),
        out_specs=(P("layer", "groups", None), P("layer", "groups", None)),
        check_vma=False,
    )
```

```python
import functools

import jax
import jax.numpy as jnp
from jax import lax
from jax.experimental import pallas as pl
from jax.experimental.pallas import tpu as pltpu
from jax.sharding import PartitionSpec as P

BLOCK = 128
LAYERS = 4
TILE = 32
CORES = 2
CHUNK = 1024
LIMIT = 4 << 20
AXIS = "layer"

ANY_SPEC = pl.BlockSpec(memory_space=pl.ANY)
VMEM_SPEC = pl.BlockSpec(memory_space=pltpu.VMEM)


def turned(chip, chips):
    bits = chips.bit_length() - 1
    return sum(((chip >> bit) & 1) << (bits - 1 - bit) for bit in range(bits))


def across(value, chip, chips):
    masks = (CORES * chip, CORES * turned(chip, chips))
    pairs = [(i, i ^ masks[i % CORES]) for i in range(lax.axis_size(AXIS))]
    return lax.ppermute(value, AXIS, pairs)


def other_core(value):
    return lax.ppermute(value, AXIS, [(i, i ^ 1) for i in range(lax.axis_size(AXIS))])


def raised(value, first, group):
    size = lax.axis_size(AXIS)
    came = lax.ppermute(value, AXIS, [(i, (i + group) % size) for i in range(size)])
    return jnp.where(first, jnp.zeros_like(came), came)


def shifted(value, group):
    size = lax.axis_size(AXIS)
    return lax.ppermute(value, AXIS, [(i, i + group) for i in range(size - group)])


def lowered(value, group):
    size = lax.axis_size(AXIS)
    return lax.ppermute(value, AXIS, [(i + group, i) for i in range(size - group)])


def rotated_down(value, final, group):
    size = lax.axis_size(AXIS)
    came = lax.ppermute(value, AXIS, [((i + group) % size, i) for i in range(size)])
    return jnp.where(final, jnp.zeros_like(came), came)


def after(values, done):
    return lax.optimization_barrier((values, done))[0]


def slab_of(place, block, chips):
    far, chip = block // chips, block % chips
    odd = (place & 1) ^ far
    return place ^ (far + CORES * (chip * (1 - odd) + turned(chip, chips) * odd))


def in_vmem(*arrays):
    return [pltpu.with_memory_space_constraint(a, pltpu.VMEM) for a in arrays]


def in_hbm(*arrays):
    return [pltpu.with_memory_space_constraint(a, pltpu.HBM) for a in arrays]


def kernel_params(limit=LIMIT):
    return pltpu.CompilerParams(vmem_limit_bytes=limit)


def load_kernel(enc_hbm, dec_hbm, enc_ref, own_ref, next_ref, sems):
    pieces = [(enc_hbm.at[0], enc_ref), (dec_hbm.at[0, 1], next_ref), (dec_hbm.at[0, 0], own_ref)]
    copies = [pltpu.make_async_copy(source, target, sems.at[i]) for i, (source, target) in enumerate(pieces)]
    for copy in copies:
        copy.start()
    for copy in copies:
        copy.wait()


def loaded(enc, dec):
    block = pltpu.VMEM(dec.shape[2:], dec.dtype)
    return pl.pallas_call(
        load_kernel,
        out_shape=[pltpu.VMEM(enc.shape[1:], enc.dtype), block, block],
        in_specs=[ANY_SPEC] * 2,
        out_specs=[VMEM_SPEC] * 3,
        scratch_shapes=[pltpu.SemaphoreType.DMA((3,))],
        compiler_params=kernel_params(1 << 20),
        cost_estimate=pl.CostEstimate(flops=0, bytes_accessed=4 * (enc.size + dec.size), transcendentals=0),
        name="load_weights",
    )(*in_hbm(enc, dec))


def decode(codes, dec_ref, near_ref, far_ref):
    half, width = near_ref.shape
    for step in range(width // CHUNK):
        columns = pl.ds(step * CHUNK, CHUNK)
        part = jnp.dot(codes, dec_ref[:, columns], preferred_element_type=jnp.float32)
        near_ref[:, columns] = part[:half]
        far_ref[:, columns] = part[half:].astype(jnp.bfloat16)


def place_in(group):
    return lax.axis_index(AXIS) & (group - 1)


def summed_over(depth, product):
    sums = [None, None]
    for step in range(depth // CHUNK):
        part = product(pl.ds(step * CHUNK, CHUNK))
        so_far = sums[step % 2]
        sums[step % 2] = part if so_far is None else so_far + part
    return sums[0] + sums[1]


def gate_of(active_ref, rows, tokens):
    group = rows // tokens
    block = lax.broadcasted_iota(jnp.int32, (rows, BLOCK), 0) // tokens
    tile = (slab_of(place_in(group), block, group // CORES) * tokens) // TILE
    parts = []
    for part in range(active_ref.shape[1]):
        live = jnp.zeros((rows, BLOCK), jnp.int32)
        for i in range(active_ref.shape[0]):
            live = jnp.where(tile == i, active_ref[pl.ds(i, 1), pl.ds(part, 1)], live)
        parts.append(live.astype(jnp.float32))
    return jnp.concatenate(parts, axis=1)


def gate_kernel(tokens, active_ref, bias_ref, gate_ref, shift_ref):
    rows = gate_ref.shape[0]
    gate_ref[...] = gate_of(active_ref, rows, tokens)
    shift_ref[...] = jnp.broadcast_to(bias_ref[...].astype(jnp.float32), shift_ref.shape)


def gated(active, bias, rows, tokens):
    shape = (rows, bias.shape[1])
    return pl.pallas_call(
        functools.partial(gate_kernel, tokens),
        out_shape=[pltpu.VMEM(shape, jnp.float32)] * 2,
        in_specs=[VMEM_SPEC] * 2,
        out_specs=[VMEM_SPEC] * 2,
        compiler_params=kernel_params(),
        cost_estimate=pl.CostEstimate(flops=8 * rows * shape[1], bytes_accessed=8 * rows * shape[1], transcendentals=0),
        name="gate",
    )(*in_vmem(active, bias))


def decode_kernel(codes_ref, dec_ref, near_ref, far_ref):
    decode(codes_ref[...], dec_ref, near_ref, far_ref)


def halves_of(rows, width):
    return [pltpu.VMEM((rows // CORES, width), jnp.float32), pltpu.VMEM((rows // CORES, width), jnp.bfloat16)]


def decoded(codes, dec):
    rows, features = codes.shape
    width = dec.shape[1]
    return pl.pallas_call(
        decode_kernel,
        out_shape=halves_of(rows, width),
        in_specs=[VMEM_SPEC] * 2,
        out_specs=[VMEM_SPEC] * 2,
        compiler_params=kernel_params(),
        cost_estimate=pl.CostEstimate(flops=2 * rows * width * features, bytes_accessed=2 * width * features, transcendentals=0),
        name="decode",
    )(*in_vmem(codes, dec))


def back(rows_ref, dec_ref):
    return summed_over(
        rows_ref.shape[1],
        lambda part: lax.dot_general(
            rows_ref[:, part], dec_ref[:, part], (((1,), (1,)), ((), ())), preferred_element_type=jnp.float32
        ),
    )


def grad_own_kernel(rows_ref, dec_ref, out_ref, _):
    out_ref[...] = back(rows_ref, dec_ref)


def grad_all_kernel(tokens, rows_ref, dec_ref, own_ref, out_ref):
    total = own_ref[...] + back(rows_ref, dec_ref)
    group = total.shape[0] // tokens
    for block in range(group):
        chips = group // CORES
        label = (chips - block % chips) % chips
        slab = slab_of(place_in(group), block // chips * chips + label, chips)
        where = pl.ds(pl.multiple_of(slab * tokens, tokens), tokens)
        out_ref[0, where, :] = total[block * tokens : (block + 1) * tokens]


def grad_own(rows, dec):
    features = dec.shape[0]
    return pl.pallas_call(
        grad_own_kernel,
        out_shape=[pltpu.VMEM((rows.shape[0], features), jnp.float32), pltpu.VMEM((8, 128), jnp.float32)],
        in_specs=[VMEM_SPEC] * 2,
        out_specs=[VMEM_SPEC] * 2,
        compiler_params=kernel_params(),
        cost_estimate=pl.CostEstimate(flops=2 * rows.size * features, bytes_accessed=2 * dec.size, transcendentals=0),
        name="grad_own",
    )(*in_vmem(rows, dec))[0]


def grad_all(rows, dec, own, tokens):
    return pl.pallas_call(
        functools.partial(grad_all_kernel, tokens),
        out_shape=jax.ShapeDtypeStruct((1,) + own.shape, jnp.float32),
        in_specs=[VMEM_SPEC] * 3,
        out_specs=VMEM_SPEC,
        compiler_params=kernel_params(),
        cost_estimate=pl.CostEstimate(flops=2 * rows.size * own.shape[1], bytes_accessed=2 * dec.size, transcendentals=0),
        name="grad_all",
    )(*in_vmem(rows, dec, own))


def blocks_of(near, far, chips):
    rows = near.shape[0] // chips
    total = near + other_core(far).astype(jnp.float32)
    return [total[chip * rows : (chip + 1) * rows] for chip in range(chips)]


def summed(blocks, sent):
    total = blocks[0]
    for came in [across(blocks[chip].astype(jnp.bfloat16), chip, len(blocks)) for chip in sent]:
        total = total + came.astype(jnp.float32)
    return total


def on_device(resid, enc_weight, enc_bias, active, dec_weight, target):
    group = lax.axis_size(AXIS) // LAYERS
    chips = group // CORES
    index = lax.axis_index(AXIS)
    slab, first, final = lax.optimization_barrier((resid[0], index < group, index >= (LAYERS - 1) * group))
    tokens = resid.shape[1]
    enc, own_dec, next_dec = loaded(enc_weight, dec_weight)
    last = across(slab, chips - 1, chips)
    last_far = other_core(after(last, enc))
    most = jnp.concatenate(after([across(slab, chip, chips) for chip in range(1, chips - 1)], last_far), axis=0)
    x = jnp.concatenate([after(slab, most), most, last, other_core(slab), other_core(most), last_far], axis=0)
    gate, bias = gated(*after((active[0], enc_bias), enc), group * tokens, tokens)
    pre = jnp.dot(x, enc, preferred_element_type=jnp.float32) + bias
    codes = (jax.nn.relu(pre) * gate).astype(jnp.bfloat16)
    next_near, next_far = decoded(codes, next_dec)
    own_near, own_far = decoded(codes, own_dec)

    nexts = blocks_of(next_near, next_far, chips)
    owns = blocks_of(own_near, own_far, chips)
    risen = raised(nexts[-1].astype(jnp.bfloat16), first, group)
    owns[-1] = owns[-1] + risen.astype(jnp.float32)
    crossed = across(owns[-1].astype(jnp.bfloat16), chips - 1, chips).astype(jnp.float32)
    next_sum = after(summed(nexts, range(1, chips - 1)), owns[-1])
    own_less = summed(owns, range(1, chips - 1)) - target[0].astype(jnp.float32) + crossed

    below = shifted(next_sum.astype(jnp.bfloat16), group).astype(jnp.float32)
    above = lowered(own_less.astype(jnp.bfloat16), group).astype(jnp.float32)
    error = (own_less + below).astype(jnp.bfloat16)
    later = jnp.where(final, 0.0, next_sum + after(above, error)).astype(jnp.bfloat16)

    heres = [error] + [across(error, chip, chips) for chip in range(chips - 1, 0, -1)]
    passed = rotated_down(after(heres[-1], later), final, group)
    here_near = jnp.concatenate(heres, axis=0)
    here_far = other_core(here_near)
    here_rows = jnp.concatenate([here_near, here_far], axis=0)
    straight = [across(later, chip, chips) for chip in range(chips - 1, 1, -1)]
    most = after(jnp.concatenate([later] + straight, axis=0), here_far)
    after_rows = jnp.concatenate([most, passed, other_core(most), other_core(passed)], axis=0)
    grad = grad_all(after_rows, next_dec, grad_own(here_rows, own_dec), tokens)
    return (error[None], grad)


def solution(mesh):
    return jax.shard_map(
        on_device,
        mesh=mesh,
        in_specs=(
            P("layer", "groups", None),
            P("layer", None, None),
            P("layer", None),
            P("layer", "groups", None),
            P("layer", None, None, None),
            P("layer", "groups", None),
        ),
        out_specs=(P("layer", "groups", None), P("layer", "groups", None)),
        check_vma=False,
    )
```

```python
import functools

import jax
import jax.numpy as jnp
from jax import lax
from jax.experimental import pallas as pl
from jax.experimental.pallas import tpu as pltpu
from jax.sharding import PartitionSpec as P

BLOCK = 128
LAYERS = 4
TILE = 32
CORES = 2
CHUNK = 1024
LIMIT = 4 << 20
AXIS = "layer"

ANY_SPEC = pl.BlockSpec(memory_space=pl.ANY)
VMEM_SPEC = pl.BlockSpec(memory_space=pltpu.VMEM)


def turned(chip, chips):
    bits = chips.bit_length() - 1
    return sum(((chip >> bit) & 1) << (bits - 1 - bit) for bit in range(bits))


def across(value, chip, chips):
    masks = (CORES * chip, CORES * turned(chip, chips))
    pairs = [(i, i ^ masks[i % CORES]) for i in range(lax.axis_size(AXIS))]
    return lax.ppermute(value, AXIS, pairs)


def other_core(value):
    return lax.ppermute(value, AXIS, [(i, i ^ 1) for i in range(lax.axis_size(AXIS))])


def raised(value, first, group):
    size = lax.axis_size(AXIS)
    came = lax.ppermute(value, AXIS, [(i, (i + group) % size) for i in range(size)])
    return jnp.where(first, jnp.zeros_like(came), came)


def shifted(value, group):
    size = lax.axis_size(AXIS)
    return lax.ppermute(value, AXIS, [(i, i + group) for i in range(size - group)])


def lowered(value, group):
    size = lax.axis_size(AXIS)
    return lax.ppermute(value, AXIS, [(i + group, i) for i in range(size - group)])


def rotated_down(value, final, group):
    size = lax.axis_size(AXIS)
    came = lax.ppermute(value, AXIS, [((i + group) % size, i) for i in range(size)])
    return jnp.where(final, jnp.zeros_like(came), came)


def after(values, done):
    return lax.optimization_barrier((values, done))[0]


def slab_of(place, block, chips):
    far, chip = block // chips, block % chips
    odd = (place & 1) ^ far
    return place ^ (far + CORES * (chip * (1 - odd) + turned(chip, chips) * odd))


def in_vmem(*arrays):
    return [pltpu.with_memory_space_constraint(a, pltpu.VMEM) for a in arrays]


def in_hbm(*arrays):
    return [pltpu.with_memory_space_constraint(a, pltpu.HBM) for a in arrays]


def kernel_params(limit=LIMIT):
    return pltpu.CompilerParams(vmem_limit_bytes=limit)


def load_kernel(enc_hbm, dec_hbm, enc_ref, own_ref, next_ref, sems):
    pieces = [(enc_hbm.at[0], enc_ref), (dec_hbm.at[0, 1], next_ref), (dec_hbm.at[0, 0], own_ref)]
    copies = [pltpu.make_async_copy(source, target, sems.at[i]) for i, (source, target) in enumerate(pieces)]
    for copy in copies:
        copy.start()
    for copy in copies:
        copy.wait()


def loaded(enc, dec):
    block = pltpu.VMEM(dec.shape[2:], dec.dtype)
    return pl.pallas_call(
        load_kernel,
        out_shape=[pltpu.VMEM(enc.shape[1:], enc.dtype), block, block],
        in_specs=[ANY_SPEC] * 2,
        out_specs=[VMEM_SPEC] * 3,
        scratch_shapes=[pltpu.SemaphoreType.DMA((3,))],
        compiler_params=kernel_params(1 << 20),
        cost_estimate=pl.CostEstimate(flops=0, bytes_accessed=4 * (enc.size + dec.size), transcendentals=0),
        name="load_weights",
    )(*in_hbm(enc, dec))


def decode(codes, dec_ref, near_ref, far_ref):
    half, width = near_ref.shape
    for step in range(width // CHUNK):
        columns = pl.ds(step * CHUNK, CHUNK)
        part = jnp.dot(codes, dec_ref[:, columns], preferred_element_type=jnp.float32)
        near_ref[:, columns] = part[:half]
        far_ref[:, columns] = part[half:].astype(jnp.bfloat16)


def place_in(group):
    return lax.axis_index(AXIS) & (group - 1)


def summed_over(depth, product):
    sums = [None, None]
    for step in range(depth // CHUNK):
        part = product(pl.ds(step * CHUNK, CHUNK))
        so_far = sums[step % 2]
        sums[step % 2] = part if so_far is None else so_far + part
    return sums[0] + sums[1]


def gate_of(active_ref, rows, tokens):
    group = rows // tokens
    block = lax.broadcasted_iota(jnp.int32, (rows, BLOCK), 0) // tokens
    tile = (slab_of(place_in(group), block, group // CORES) * tokens) // TILE
    parts = []
    for part in range(active_ref.shape[1]):
        live = jnp.zeros((rows, BLOCK), jnp.int32)
        for i in range(active_ref.shape[0]):
            live = jnp.where(tile == i, active_ref[pl.ds(i, 1), pl.ds(part, 1)], live)
        parts.append(live.astype(jnp.float32))
    return jnp.concatenate(parts, axis=1)


def gate_kernel(tokens, active_ref, bias_ref, gate_ref, shift_ref):
    rows = gate_ref.shape[0]
    gate_ref[...] = gate_of(active_ref, rows, tokens)
    shift_ref[...] = jnp.broadcast_to(bias_ref[...].astype(jnp.float32), shift_ref.shape)


def gated(active, bias, rows, tokens):
    shape = (rows, bias.shape[1])
    return pl.pallas_call(
        functools.partial(gate_kernel, tokens),
        out_shape=[pltpu.VMEM(shape, jnp.float32)] * 2,
        in_specs=[VMEM_SPEC] * 2,
        out_specs=[VMEM_SPEC] * 2,
        compiler_params=kernel_params(),
        cost_estimate=pl.CostEstimate(flops=8 * rows * shape[1], bytes_accessed=8 * rows * shape[1], transcendentals=0),
        name="gate",
    )(*in_vmem(active, bias))


def decode_kernel(codes_ref, dec_ref, near_ref, far_ref):
    decode(codes_ref[...], dec_ref, near_ref, far_ref)


def halves_of(rows, width):
    return [pltpu.VMEM((rows // CORES, width), jnp.float32), pltpu.VMEM((rows // CORES, width), jnp.bfloat16)]


def decoded(codes, dec):
    rows, features = codes.shape
    width = dec.shape[1]
    return pl.pallas_call(
        decode_kernel,
        out_shape=halves_of(rows, width),
        in_specs=[VMEM_SPEC] * 2,
        out_specs=[VMEM_SPEC] * 2,
        compiler_params=kernel_params(),
        cost_estimate=pl.CostEstimate(flops=2 * rows * width * features, bytes_accessed=2 * width * features, transcendentals=0),
        name="decode",
    )(*in_vmem(codes, dec))


def back(rows_ref, dec_ref):
    turned_round = summed_over(
        rows_ref.shape[1],
        lambda part: lax.dot_general(
            dec_ref[:, part], rows_ref[:, part], (((1,), (1,)), ((), ())), preferred_element_type=jnp.float32
        ),
    )
    return turned_round.T


def grad_own_kernel(rows_ref, dec_ref, out_ref, _):
    out_ref[...] = back(rows_ref, dec_ref)


def grad_all_kernel(tokens, rows_ref, dec_ref, own_ref, out_ref):
    total = own_ref[...] + back(rows_ref, dec_ref)
    group = total.shape[0] // tokens
    for block in range(group):
        chips = group // CORES
        label = (chips - block % chips) % chips
        slab = slab_of(place_in(group), block // chips * chips + label, chips)
        where = pl.ds(pl.multiple_of(slab * tokens, tokens), tokens)
        out_ref[0, where, :] = total[block * tokens : (block + 1) * tokens]


def grad_own(rows, dec):
    features = dec.shape[0]
    return pl.pallas_call(
        grad_own_kernel,
        out_shape=[pltpu.VMEM((rows.shape[0], features), jnp.float32), pltpu.VMEM((8, 128), jnp.float32)],
        in_specs=[VMEM_SPEC] * 2,
        out_specs=[VMEM_SPEC] * 2,
        compiler_params=kernel_params(),
        cost_estimate=pl.CostEstimate(flops=2 * rows.size * features, bytes_accessed=2 * dec.size, transcendentals=0),
        name="grad_own",
    )(*in_vmem(rows, dec))[0]


def grad_all(rows, dec, own, tokens):
    return pl.pallas_call(
        functools.partial(grad_all_kernel, tokens),
        out_shape=jax.ShapeDtypeStruct((1,) + own.shape, jnp.float32),
        in_specs=[VMEM_SPEC] * 3,
        out_specs=VMEM_SPEC,
        compiler_params=kernel_params(),
        cost_estimate=pl.CostEstimate(flops=2 * rows.size * own.shape[1], bytes_accessed=2 * dec.size, transcendentals=0),
        name="grad_all",
    )(*in_vmem(rows, dec, own))


def blocks_of(near, far, chips):
    rows = near.shape[0] // chips
    total = near + other_core(far).astype(jnp.float32)
    return [total[chip * rows : (chip + 1) * rows] for chip in range(chips)]


def summed(blocks, sent):
    total = blocks[0]
    for came in [across(blocks[chip].astype(jnp.bfloat16), chip, len(blocks)) for chip in sent]:
        total = total + came.astype(jnp.float32)
    return total


def on_device(resid, enc_weight, enc_bias, active, dec_weight, target):
    group = lax.axis_size(AXIS) // LAYERS
    chips = group // CORES
    index = lax.axis_index(AXIS)
    slab, first, final = lax.optimization_barrier((resid[0], index < group, index >= (LAYERS - 1) * group))
    tokens = resid.shape[1]
    enc, own_dec, next_dec = loaded(enc_weight, dec_weight)
    pieces = jnp.concatenate([across(slab, chip, chips) for chip in range(chips - 1, 0, -1)], axis=0)
    pieces_far = other_core(pieces)
    rows = [after(slab, pieces)] + [pieces[i * tokens : (i + 1) * tokens] for i in range(chips - 1)][::-1]
    rows += [other_core(slab)] + [pieces_far[i * tokens : (i + 1) * tokens] for i in range(chips - 1)][::-1]
    x = jnp.concatenate(rows, axis=0)
    gate, bias = gated(*after((active[0], enc_bias), enc), group * tokens, tokens)
    pre = jnp.dot(x, enc, preferred_element_type=jnp.float32) + bias
    codes = (jax.nn.relu(pre) * gate).astype(jnp.bfloat16)
    next_near, next_far = decoded(codes, next_dec)
    own_near, own_far = decoded(codes, own_dec)

    nexts = blocks_of(next_near, next_far, chips)
    owns = blocks_of(own_near, own_far, chips)
    risen = raised(nexts[-1].astype(jnp.bfloat16), first, group)
    owns[-1] = owns[-1] + risen.astype(jnp.float32)
    crossed = across(owns[-1].astype(jnp.bfloat16), chips - 1, chips).astype(jnp.float32)
    next_sum = after(summed(nexts, range(1, chips - 1)), owns[-1])
    own_less = summed(owns, range(1, chips - 1)) - target[0].astype(jnp.float32) + crossed

    below = shifted(next_sum.astype(jnp.bfloat16), group).astype(jnp.float32)
    above = lowered(own_less.astype(jnp.bfloat16), group).astype(jnp.float32)
    error = (own_less + below).astype(jnp.bfloat16)
    later = jnp.where(final, 0.0, next_sum + after(above, error)).astype(jnp.bfloat16)

    heres = [error] + [across(error, chip, chips) for chip in range(chips - 1, 0, -1)]
    passed = rotated_down(after(heres[-1], later), final, group)
    here_near = jnp.concatenate(heres, axis=0)
    here_far = other_core(here_near)
    here_rows = jnp.concatenate([here_near, here_far], axis=0)
    straight = [across(later, chip, chips) for chip in range(chips - 1, 1, -1)]
    most = after(jnp.concatenate([later] + straight, axis=0), here_far)
    after_rows = jnp.concatenate([most, passed, other_core(most), other_core(passed)], axis=0)
    grad = grad_all(after_rows, next_dec, grad_own(here_rows, own_dec), tokens)
    return (error[None], grad)


def solution(mesh):
    return jax.shard_map(
        on_device,
        mesh=mesh,
        in_specs=(
            P("layer", "groups", None),
            P("layer", None, None),
            P("layer", None),
            P("layer", "groups", None),
            P("layer", None, None, None),
            P("layer", "groups", None),
        ),
        out_specs=(P("layer", "groups", None), P("layer", "groups", None)),
        check_vma=False,
    )
```

```python
import functools

import jax
import jax.numpy as jnp
from jax import lax
from jax.experimental import pallas as pl
from jax.experimental.pallas import tpu as pltpu
from jax.sharding import PartitionSpec as P

BLOCK = 128
LAYERS = 4
TILE = 32
CORES = 2
CHUNK = 1024
LIMIT = 4 << 20
AXIS = "layer"

ANY_SPEC = pl.BlockSpec(memory_space=pl.ANY)
VMEM_SPEC = pl.BlockSpec(memory_space=pltpu.VMEM)


def turned(chip, chips):
    bits = chips.bit_length() - 1
    return sum(((chip >> bit) & 1) << (bits - 1 - bit) for bit in range(bits))


def across(value, chip, chips):
    masks = (CORES * chip, CORES * turned(chip, chips))
    pairs = [(i, i ^ masks[i % CORES]) for i in range(lax.axis_size(AXIS))]
    return lax.ppermute(value, AXIS, pairs)


def other_core(value):
    return lax.ppermute(value, AXIS, [(i, i ^ 1) for i in range(lax.axis_size(AXIS))])


def raised(value, first, group):
    size = lax.axis_size(AXIS)
    came = lax.ppermute(value, AXIS, [(i, (i + group) % size) for i in range(size)])
    return jnp.where(first, jnp.zeros_like(came), came)


def shifted(value, group):
    size = lax.axis_size(AXIS)
    return lax.ppermute(value, AXIS, [(i, i + group) for i in range(size - group)])


def lowered(value, group):
    size = lax.axis_size(AXIS)
    return lax.ppermute(value, AXIS, [(i + group, i) for i in range(size - group)])


def rotated_down(value, final, group):
    size = lax.axis_size(AXIS)
    came = lax.ppermute(value, AXIS, [((i + group) % size, i) for i in range(size)])
    return jnp.where(final, jnp.zeros_like(came), came)


def after(values, done):
    return lax.optimization_barrier((values, done))[0]


def slab_of(place, block, chips):
    far, chip = block // chips, block % chips
    odd = (place & 1) ^ far
    return place ^ (far + CORES * (chip * (1 - odd) + turned(chip, chips) * odd))


def in_vmem(*arrays):
    return [pltpu.with_memory_space_constraint(a, pltpu.VMEM) for a in arrays]


def in_hbm(*arrays):
    return [pltpu.with_memory_space_constraint(a, pltpu.HBM) for a in arrays]


def kernel_params(limit=LIMIT):
    return pltpu.CompilerParams(vmem_limit_bytes=limit)


def load_kernel(enc_hbm, dec_hbm, enc_ref, own_ref, next_ref, sems):
    pieces = [(enc_hbm.at[0], enc_ref), (dec_hbm.at[0, 1], next_ref), (dec_hbm.at[0, 0], own_ref)]
    copies = [pltpu.make_async_copy(source, target, sems.at[i]) for i, (source, target) in enumerate(pieces)]
    for copy in copies:
        copy.start()
    for copy in copies:
        copy.wait()


def loaded(enc, dec):
    block = pltpu.VMEM(dec.shape[2:], dec.dtype)
    return pl.pallas_call(
        load_kernel,
        out_shape=[pltpu.VMEM(enc.shape[1:], enc.dtype), block, block],
        in_specs=[ANY_SPEC] * 2,
        out_specs=[VMEM_SPEC] * 3,
        scratch_shapes=[pltpu.SemaphoreType.DMA((3,))],
        compiler_params=kernel_params(1 << 20),
        cost_estimate=pl.CostEstimate(flops=0, bytes_accessed=4 * (enc.size + dec.size), transcendentals=0),
        name="load_weights",
    )(*in_hbm(enc, dec))


def decode(codes, dec_ref, near_ref, far_ref):
    half, width = near_ref.shape
    for step in range(width // CHUNK):
        columns = pl.ds(step * CHUNK, CHUNK)
        part = jnp.dot(codes, dec_ref[:, columns], preferred_element_type=jnp.float32)
        near_ref[:, columns] = part[:half]
        far_ref[:, columns] = part[half:].astype(jnp.bfloat16)


def place_in(group):
    return lax.axis_index(AXIS) & (group - 1)


def summed_over(depth, product):
    sums = [None, None]
    for step in range(depth // CHUNK):
        part = product(pl.ds(step * CHUNK, CHUNK))
        so_far = sums[step % 2]
        sums[step % 2] = part if so_far is None else so_far + part
    return sums[0] + sums[1]


def gate_of(active_ref, rows, tokens):
    group = rows // tokens
    block = lax.broadcasted_iota(jnp.int32, (rows, BLOCK), 0) // tokens
    tile = (slab_of(place_in(group), block, group // CORES) * tokens) // TILE
    parts = []
    for part in range(active_ref.shape[1]):
        live = jnp.zeros((rows, BLOCK), jnp.int32)
        for i in range(active_ref.shape[0]):
            live = jnp.where(tile == i, active_ref[pl.ds(i, 1), pl.ds(part, 1)], live)
        parts.append(live.astype(jnp.float32))
    return jnp.concatenate(parts, axis=1)


def gate_kernel(tokens, active_ref, bias_ref, gate_ref, shift_ref):
    rows = gate_ref.shape[0]
    gate_ref[...] = gate_of(active_ref, rows, tokens)
    shift_ref[...] = jnp.broadcast_to(bias_ref[...].astype(jnp.float32), shift_ref.shape)


def gated(active, bias, rows, tokens):
    shape = (rows, bias.shape[1])
    return pl.pallas_call(
        functools.partial(gate_kernel, tokens),
        out_shape=[pltpu.VMEM(shape, jnp.float32)] * 2,
        in_specs=[VMEM_SPEC] * 2,
        out_specs=[VMEM_SPEC] * 2,
        compiler_params=kernel_params(),
        cost_estimate=pl.CostEstimate(flops=8 * rows * shape[1], bytes_accessed=8 * rows * shape[1], transcendentals=0),
        name="gate",
    )(*in_vmem(active, bias))


def decode_kernel(codes_ref, dec_ref, near_ref, far_ref):
    decode(codes_ref[...], dec_ref, near_ref, far_ref)


def halves_of(rows, width):
    return [pltpu.VMEM((rows // CORES, width), jnp.float32), pltpu.VMEM((rows // CORES, width), jnp.bfloat16)]


def decoded(codes, dec):
    rows, features = codes.shape
    width = dec.shape[1]
    return pl.pallas_call(
        decode_kernel,
        out_shape=halves_of(rows, width),
        in_specs=[VMEM_SPEC] * 2,
        out_specs=[VMEM_SPEC] * 2,
        compiler_params=kernel_params(),
        cost_estimate=pl.CostEstimate(flops=2 * rows * width * features, bytes_accessed=2 * width * features, transcendentals=0),
        name="decode",
    )(*in_vmem(codes, dec))


def back(rows_ref, dec_ref):
    return summed_over(
        rows_ref.shape[1],
        lambda part: lax.dot_general(
            rows_ref[:, part], dec_ref[:, part], (((1,), (1,)), ((), ())), preferred_element_type=jnp.float32
        ),
    )


def back_turned(rows_ref, dec_ref):
    turned_round = summed_over(
        rows_ref.shape[1],
        lambda part: lax.dot_general(
            dec_ref[:, part], rows_ref[:, part], (((1,), (1,)), ((), ())), preferred_element_type=jnp.float32
        ),
    )
    return turned_round.T


def grad_own_kernel(rows_ref, dec_ref, out_ref, _):
    out_ref[...] = back(rows_ref, dec_ref)


def grad_all_kernel(tokens, rows_ref, dec_ref, own_ref, out_ref):
    total = own_ref[...] + back_turned(rows_ref, dec_ref)
    group = total.shape[0] // tokens
    for block in range(group):
        chips = group // CORES
        label = (chips - block % chips) % chips
        slab = slab_of(place_in(group), block // chips * chips + label, chips)
        where = pl.ds(pl.multiple_of(slab * tokens, tokens), tokens)
        out_ref[0, where, :] = total[block * tokens : (block + 1) * tokens]


def grad_own(rows, dec):
    features = dec.shape[0]
    return pl.pallas_call(
        grad_own_kernel,
        out_shape=[pltpu.VMEM((rows.shape[0], features), jnp.float32), pltpu.VMEM((8, 128), jnp.float32)],
        in_specs=[VMEM_SPEC] * 2,
        out_specs=[VMEM_SPEC] * 2,
        compiler_params=kernel_params(),
        cost_estimate=pl.CostEstimate(flops=2 * rows.size * features, bytes_accessed=2 * dec.size, transcendentals=0),
        name="grad_own",
    )(*in_vmem(rows, dec))[0]


def grad_all(rows, dec, own, tokens):
    return pl.pallas_call(
        functools.partial(grad_all_kernel, tokens),
        out_shape=jax.ShapeDtypeStruct((1,) + own.shape, jnp.float32),
        in_specs=[VMEM_SPEC] * 3,
        out_specs=VMEM_SPEC,
        compiler_params=kernel_params(),
        cost_estimate=pl.CostEstimate(flops=2 * rows.size * own.shape[1], bytes_accessed=2 * dec.size, transcendentals=0),
        name="grad_all",
    )(*in_vmem(rows, dec, own))


def blocks_of(near, far, chips):
    rows = near.shape[0] // chips
    total = near + other_core(far).astype(jnp.float32)
    return [total[chip * rows : (chip + 1) * rows] for chip in range(chips)]


def summed(blocks, sent):
    total = blocks[0]
    for came in [across(blocks[chip].astype(jnp.bfloat16), chip, len(blocks)) for chip in sent]:
        total = total + came.astype(jnp.float32)
    return total


def on_device(resid, enc_weight, enc_bias, active, dec_weight, target):
    group = lax.axis_size(AXIS) // LAYERS
    chips = group // CORES
    index = lax.axis_index(AXIS)
    slab, first, final = lax.optimization_barrier((resid[0], index < group, index >= (LAYERS - 1) * group))
    tokens = resid.shape[1]
    enc, own_dec, next_dec = loaded(enc_weight, dec_weight)
    pieces = jnp.concatenate([across(slab, chip, chips) for chip in range(chips - 1, 0, -1)], axis=0)
    pieces_far = other_core(pieces)
    rows = [after(slab, pieces)] + [pieces[i * tokens : (i + 1) * tokens] for i in range(chips - 1)][::-1]
    rows += [other_core(slab)] + [pieces_far[i * tokens : (i + 1) * tokens] for i in range(chips - 1)][::-1]
    x = jnp.concatenate(rows, axis=0)
    gate, bias = gated(*after((active[0], enc_bias), enc), group * tokens, tokens)
    pre = jnp.dot(x, enc, preferred_element_type=jnp.float32) + bias
    codes = (jax.nn.relu(pre) * gate).astype(jnp.bfloat16)
    next_near, next_far = decoded(codes, next_dec)
    own_near, own_far = decoded(codes, own_dec)

    nexts = blocks_of(next_near, next_far, chips)
    owns = blocks_of(own_near, own_far, chips)
    risen = raised(nexts[-1].astype(jnp.bfloat16), first, group)
    owns[-1] = owns[-1] + risen.astype(jnp.float32)
    crossed = across(owns[-1].astype(jnp.bfloat16), chips - 1, chips).astype(jnp.float32)
    next_sum = after(summed(nexts, range(1, chips - 1)), owns[-1])
    own_less = summed(owns, range(1, chips - 1)) - target[0].astype(jnp.float32) + crossed

    below = shifted(next_sum.astype(jnp.bfloat16), group).astype(jnp.float32)
    above = lowered(own_less.astype(jnp.bfloat16), group).astype(jnp.float32)
    error = (own_less + below).astype(jnp.bfloat16)
    later = jnp.where(final, 0.0, next_sum + after(above, error)).astype(jnp.bfloat16)

    heres = [error] + [across(error, chip, chips) for chip in range(chips - 1, 0, -1)]
    passed = rotated_down(after(heres[-1], later), final, group)
    here_near = jnp.concatenate(heres, axis=0)
    here_far = other_core(here_near)
    here_rows = jnp.concatenate([here_near, here_far], axis=0)
    straight = [across(later, chip, chips) for chip in range(chips - 1, 1, -1)]
    most = after(jnp.concatenate([later] + straight, axis=0), here_far)
    after_rows = jnp.concatenate([most, passed, other_core(most), other_core(passed)], axis=0)
    grad = grad_all(after_rows, next_dec, grad_own(here_rows, own_dec), tokens)
    return (error[None], grad)


def solution(mesh):
    return jax.shard_map(
        on_device,
        mesh=mesh,
        in_specs=(
            P("layer", "groups", None),
            P("layer", None, None),
            P("layer", None),
            P("layer", "groups", None),
            P("layer", None, None, None),
            P("layer", "groups", None),
        ),
        out_specs=(P("layer", "groups", None), P("layer", "groups", None)),
        check_vma=False,
    )
```
